32 devices in a mesh: dp: 16 (over z, y, core), mp: 2 (over x).
Axes of the slice: x: 2, y: 2, z: 4, core: 2. Of those that a mesh axis runs over, the one named last changes fastest.
Arguments:
- decoder_layer_input: bfloat16 [16384, 768], P('dp'), may hold values from -6 to 6
- encoder_states: bfloat16 [4096, 768], P('dp'), may hold values from -6 to 6
- retrieved_owner: int32 [16384, 8], P('dp'), may hold values from 0 to 15, all different within a row; in each aligned block of 1024 rows (0 to 1023, 1024 to 2047, ...) at most 728 rows name the same one
- retrieved_block: int32 [16384, 8], P('dp'), may hold values from 0 to 1
- self_query: bfloat16 [768, 768], P(None, 'mp'), may hold values from -0.21875 to 0.21875
- self_attention_key: bfloat16 [768, 768], P(None, 'mp'), may hold values from -0.21875 to 0.21875
- self_value: bfloat16 [768, 768], P(None, 'mp'), may hold values from -0.21875 to 0.21875
- self_out: bfloat16 [768, 768], P('mp'), may hold values from -2.5 to 2.5
- gain_first: float32 [768], replicated, may hold values from 0.5 to 1.5
- shift_first: float32 [768], replicated, may hold values from -2 to 2
- cross_query: bfloat16 [768, 768], P(None, 'mp'), may hold values from -0.21875 to 0.21875
- cross_key: bfloat16 [768, 768], P(None, 'mp'), may hold values from -0.21875 to 0.21875
- cross_value: bfloat16 [768, 768], P(None, 'mp'), may hold values from -0.21875 to 0.21875
- cross_out: bfloat16 [768, 768], P('mp'), may hold values from -3 to 3
- gain_second: float32 [768], replicated, may hold values from 0.5 to 1.5
- shift_second: float32 [768], replicated, may hold values from -2 to 2
- hidden_up: bfloat16 [768, 3072], P(None, 'mp'), may hold values from -0.21875 to 0.21875
- hidden_down: bfloat16 [3072, 768], P('mp'), may hold values from -0.109375 to 0.109375
- gain_third: float32 [768], replicated, may hold values from 0.5 to 1.5
- shift_third: float32 [768], replicated, may hold values from -2 to 2
- out_grad: bfloat16 [16384, 768], P('dp'), may hold values from -6 to 6
Outputs:
- layer_out: bfloat16 [16384, 768], P('dp')
- input_grad: float32 [16384, 768], P('dp')
- encoder_grad: float32 [4096, 768], P('dp')
- self_query_grad: float32 [768, 768], P('dp', 'mp')
- self_attention_key_grad: float32 [768, 768], P('dp', 'mp')
- self_value_grad: float32 [768, 768], P('dp', 'mp')
- self_out_grad: float32 [768, 768], P('mp', 'dp')
- gain_first_grad: float32 [768], P('dp')
- shift_first_grad: float32 [768], P('dp')
- cross_query_grad: float32 [768, 768], P('dp', 'mp')
- cross_key_grad: float32 [768, 768], P('dp', 'mp')
- cross_value_grad: float32 [768, 768], P('dp', 'mp')
- cross_out_grad: float32 [768, 768], P('mp', 'dp')
- gain_second_grad: float32 [768], P('dp')
- shift_second_grad: float32 [768], P('dp')
- hidden_up_grad: float32 [768, 3072], P('dp', 'mp')
- hidden_down_grad: float32 [3072, 768], P('mp', 'dp')
- gain_third_grad: float32 [768], P('dp')
- shift_third_grad: float32 [768], P('dp')
The draws below stay inside these ranges and needn't reach their ends.
Inputs may be any that keep to these rules, and one draw needn't show every extreme that they name: `retrieved_owner`: each row names 8 different owners. The rows of one sequence name any one owner at most 728 times, a bound that some block reaches in every draw.
All inputs are finite; a program needn't handle non-finite values.
Results may differ from the reference program's by a relative error of at most 0.025.
The reference program's roundings to bfloat16 on the way count: a program that leaves them out, or rounds other values in their place, can miss the bound.
Values may be sent and summed in bfloat16 or wider, within the bound.
No kernel may reach another device: no remote copies, remote signals or barrier semaphores. Data moves between devices by JAX's collectives and lax.ppermute only.
A program may use at most 384 MiB of HBM per device.

```python
import math
import jax
import jax.numpy as jnp
import numpy as np
from jax import lax

D = 768
H = 12
DH = 64
FF = 3072
SEQ = 1024
KB = 8
BLOCK = 128
BLOCKS_DEV = 2
ENC_DEV = 256
TOKENS = 16384
ENC = 4096
CAP = 728
N_DP = 16


def set_ends(entries, rng, low, top_value):
    spot = [jax.random.randint(jax.random.fold_in(rng, axis), (), 0, length) for axis, length in enumerate(entries.shape)]
    main_axis = entries.shape.index(max(entries.shape))
    next_to = spot[:main_axis] + [(spot[main_axis] + 1) % entries.shape[main_axis]] + spot[main_axis + 1:]
    return entries.at[tuple(spot)].set(low).at[tuple(next_to)].set(top_value)


def raised(array, stream_key, source, target, blocks, factor):
    def block_of(axis_at):
        return (jnp.arange(array.shape[axis_at]) // (array.shape[axis_at] // blocks)).reshape((-1,) + (1,) * (array.ndim - 1 - axis_at))

    first = jax.random.permutation(stream_key, blocks)[block_of(target)]
    other_side = (block_of(target) + blocks // 2) % blocks
    return jnp.where((block_of(source) == first) | (block_of(source) == other_side), factor * array, array)


def block_scale(rng, shape, cuts, least, top_value):
    level, own = 1.0, jax.random.fold_in(rng, 6)
    for position, parts in cuts:
        heights = jnp.exp(jax.random.uniform(jax.random.fold_in(own, position), (parts,), jnp.float32, least / len(cuts), top_value / len(cuts)))
        level = level * jnp.repeat(heights, shape[position] // parts).reshape([-1 if axis == position else 1 for axis in range(len(shape))])
    return level


def shared_out(key, own, number, rows, amount, top, limit, slope):
    order = jax.random.permutation(key, amount)
    heavy_load, ordinary = portions_of(amount, rows * top, limit, slope, True), portions_of(amount, rows * top, limit, slope, False)
    places = jnp.arange(amount)

    def named(tallies, turn):
        used = int((tallies > 0).sum())
        fixed = max(1, used // 4)
        passed = fixed + (places - fixed + turn * (used - fixed)) % max(1, amount - fixed)
        return jnp.zeros((amount,), jnp.int32).at[order[jnp.where(places < fixed, places, passed)]].set(jnp.asarray(tallies, jnp.int32))

    tallies = jnp.where(number % 4 == 0, named(heavy_load, number // 4), named(ordinary, number - number // 4 - 1))
    mixed = jax.random.permutation(jax.random.fold_in(own, 3), amount)
    donor, sink = mixed[0:amount // 2 * 2:2], mixed[1:amount // 2 * 2:2]
    room = jnp.minimum(tallies[donor] - 1, limit - tallies[sink]) // 2
    room = jnp.where((donor == order[0]) | (sink == order[0]) | (tallies[sink] == 0), 0, jnp.maximum(room, 0))
    passed = jax.random.randint(jax.random.fold_in(own, 4), (amount // 2,), 0, 1 << 20) % (room + 1)
    tallies = tallies.at[donor].add(-passed).at[sink].add(passed)
    labels = jnp.searchsorted(jnp.cumsum(tallies), jnp.arange(rows * top), side="right").astype(jnp.int32)
    table = labels.reshape(top, rows).T
    table = table[jax.random.permutation(jax.random.fold_in(own, 1), rows)]
    turn = jax.random.randint(jax.random.fold_in(own, 2), (rows, 1), 0, top)
    return jnp.take_along_axis(table, (jnp.arange(top)[None, :] + turn) % top, axis=1)


def portions_of(count, total, most, lean, full):
    loads = [(1 << 20) // math.isqrt(grade ** lean) + 1 for grade in range(1, count + 1)]
    largest = most if full else min(most, max(-(-total // count), total * loads[0] // sum(loads)))
    least = 1 if total - largest >= count - 1 else 0
    counts, rest = [largest] + [least] * (count - 1), total - largest - least * (count - 1)
    while rest > 0:
        candidates = [i for i in range(1, count) if counts[i] < largest] or [i for i in range(1, count) if counts[i] < most]
        pool, budget = sum([loads[i] for i in candidates]), rest
        for i in candidates:
            extra = min(most - counts[i], max(1, budget * loads[i] // pool), rest)
            counts[i] = counts[i] + extra
            rest = rest - extra
    return np.array(counts)


def gaussian(rng, extent, deviation, most, split=(), kind=jnp.bfloat16):
    values = deviation * jax.random.normal(rng, extent, jnp.float32)
    if split:
        values = values * block_scale(rng, extent, split, -0.22, 0.18)
    return jnp.clip(values, -most, most).astype(kind)


def bell_draw_with(own_key, dims, scale, most, cuts, heavy, held_as=jnp.bfloat16):
    values = scale * jax.random.normal(own_key, dims, jnp.float32)
    if cuts:
        values = values * block_scale(own_key, dims, cuts, -0.22, 0.18)
    return jnp.clip(raised(values, jax.random.fold_in(own_key, 3), *heavy), -most, most).astype(held_as)


def setup_inputs(seed: int = 0) -> dict:
    splits = jax.random.split(jax.random.key(seed), 22)
    decoder_layer_input = gaussian(splits[0], (TOKENS, D), 1.0, 6.0, ((0, 16),))
    encoder_states = gaussian(splits[1], (ENC, D), 1.0, 6.0, ((0, 16),))
    retrieved_owner_keys = jax.random.split(jax.random.fold_in(splits[2], 1), TOKENS // SEQ)
    retrieved_owner_turns = jax.random.permutation(jax.random.fold_in(splits[2], 3), TOKENS // SEQ)
    retrieved_owner = jax.vmap(lambda own, number: shared_out(jax.random.fold_in(splits[2], 2), own, number, SEQ, N_DP, KB, CAP, 2))(retrieved_owner_keys, retrieved_owner_turns).reshape((TOKENS, KB))
    retrieved_block = set_ends(jax.random.randint(splits[3], (TOKENS, KB), 0, BLOCKS_DEV), jax.random.fold_in(splits[3], 1), 0, BLOCKS_DEV - 1).astype(jnp.int32)
    self_query = gaussian(splits[4], (D, D), D ** -0.5, 0.21875, ((1, 2),))
    self_attention_key = gaussian(splits[5], (D, D), D ** -0.5, 0.21875, ((1, 2),))
    self_value = gaussian(splits[6], (D, D), D ** -0.5, 0.21875, ((1, 2),))
    self_out = gaussian(splits[7], (D, D), 6 ** -0.5, 2.5, ((0, 2),))
    gain_first = jnp.clip(1.0 + 0.1 * jax.random.normal(splits[8], (D,), jnp.float32), 0.5, 1.5)
    shift_first = gaussian(splits[9], (D,), 0.3, 2.0, (), jnp.float32)
    cross_query = gaussian(splits[10], (D, D), D ** -0.5, 0.21875, ((1, 2),))
    cross_key = gaussian(splits[11], (D, D), D ** -0.5, 0.21875, ((1, 2),))
    cross_value = gaussian(splits[12], (D, D), D ** -0.5, 0.21875, ((1, 2),))
    cross_out = gaussian(splits[13], (D, D), 4 ** -0.5, 3.0, ((0, 2),))
    gain_second = jnp.clip(1.0 + 0.1 * jax.random.normal(splits[14], (D,), jnp.float32), 0.5, 1.5)
    shift_second = gaussian(splits[15], (D,), 0.3, 2.0, (), jnp.float32)
    hidden_up = gaussian(splits[16], (D, FF), D ** -0.5, 0.21875, ((1, 2),))
    hidden_down = gaussian(splits[17], (FF, D), FF ** -0.5, 0.109375, ((0, 2),))
    gain_third = jnp.clip(1.0 + 0.1 * jax.random.normal(splits[18], (D,), jnp.float32), 0.5, 1.5)
    shift_third = gaussian(splits[19], (D,), 0.3, 2.0, (), jnp.float32)
    out_grad = bell_draw_with(splits[20], (TOKENS, D), 1.0, 6.0, ((0, 16),), (0, 1, 16, 2.0))
    return {"decoder_layer_input": decoder_layer_input, "encoder_states": encoder_states, "retrieved_owner": retrieved_owner, "retrieved_block": retrieved_block, "self_query": self_query, "self_attention_key": self_attention_key, "self_value": self_value, "self_out": self_out, "gain_first": gain_first, "shift_first": shift_first, "cross_query": cross_query, "cross_key": cross_key, "cross_value": cross_value, "cross_out": cross_out, "gain_second": gain_second, "shift_second": shift_second, "hidden_up": hidden_up, "hidden_down": hidden_down, "gain_third": gain_third, "shift_third": shift_third, "out_grad": out_grad}


HIGH = lax.Precision.HIGHEST
EPSILON = 1e-05
NEGATIVE = -1e+30

@jax.custom_vjp
def low(v):
    return lax.optimization_barrier(v.astype(jnp.bfloat16)).astype(jnp.float32)

@jax.custom_vjp
def low_back(v):
    return v

def low_keep(v):
    return (low(v), None)

def low_pass(kept, grad):
    return (grad,)

def back_keep(v):
    return (v, None)

def back_low(kept, grad):
    return (low(grad),)
low.defvjp(low_keep, low_pass)
low_back.defvjp(back_keep, back_low)

def rounded(values):
    return low_back(low(values))

def normalize(values, gain_row, shift_row):
    center = values - lax.optimization_barrier(jnp.mean(values, -1, keepdims=True))
    spread = lax.optimization_barrier(jnp.mean(center * center, -1, keepdims=True))
    return center * lax.rsqrt(spread + EPSILON) * gain_row + shift_row

def log_total(scores, axis):
    peak_row = lax.optimization_barrier(jnp.max(scores, axis, keepdims=True))
    return peak_row + jnp.log(lax.optimization_barrier(jnp.sum(jnp.exp(scores - peak_row), axis, keepdims=True)))

def reference(decoder_layer_input, encoder_states, retrieved_owner, retrieved_block, self_query, self_attention_key, self_value, self_out, gain_first, shift_first, cross_query, cross_key, cross_value, cross_out, gain_second, shift_second, hidden_up, hidden_down, gain_third, shift_third, out_grad):
    score_scale = DH ** (-0.5)
    slot_count = N_DP * CAP
    request_count = TOKENS * KB
    owner_flat = retrieved_owner.reshape(-1).astype(jnp.int32)
    owner_hot = (owner_flat[:, None] == jnp.arange(N_DP, dtype=jnp.int32)[None, :]).astype(jnp.int32)
    ranking = (lax.optimization_barrier(jnp.sum(jnp.cumsum(owner_hot, 0) * owner_hot, 1)) - 1).astype(jnp.int32)
    request_pos = (owner_flat * slot_count + ranking).astype(jnp.int32)
    request_token = (jnp.arange(request_count, dtype=jnp.int32) // KB).astype(jnp.int32)
    slot_token = jnp.zeros((N_DP * slot_count,), jnp.int32).at[request_pos].set(request_token)
    slot_block = jnp.full((N_DP * slot_count,), -1, jnp.int32).at[request_pos].set(retrieved_block.reshape(-1).astype(jnp.int32))
    key_block = (jnp.arange(ENC_DEV, dtype=jnp.int32) // BLOCK).astype(jnp.int32)
    causal = jnp.arange(SEQ)[:, None] >= jnp.arange(SEQ)[None, :]

    def forward(inputs, store, sq_weight, sk_weight, sv_weight, so_weight, gain_a, shift_a, cq_weight, ck_weight, cv_weight, co_weight, gain_b, shift_b, up_weight, down_weight, gain_c, shift_c):

        def self_sequence(rows):
            queries = rounded(jnp.dot(rows, sq_weight, precision=HIGH)).reshape(SEQ, H, DH)
            keys_all = rounded(jnp.dot(rows, sk_weight, precision=HIGH)).reshape(SEQ, H, DH)
            values_all = rounded(jnp.dot(rows, sv_weight, precision=HIGH)).reshape(SEQ, H, DH)
            scores = low_back(score_scale * jnp.einsum('qhd,khd->hqk', queries, keys_all, precision=HIGH))
            scores = jnp.where(causal[None], scores, NEGATIVE)
            prob_rows = low(jnp.exp(scores - log_total(scores, 2)))
            mixture = rounded(jnp.einsum('hqk,khd->qhd', prob_rows, values_all, precision=HIGH).reshape(SEQ, D))
            return jnp.dot(mixture, so_weight, precision=HIGH)
        self_branch = low_back(lax.map(jax.checkpoint(self_sequence), inputs.reshape(N_DP, SEQ, D)).reshape(TOKENS, D))
        first = normalize(inputs + self_branch, gain_a, shift_a)
        cross_queries = rounded(jnp.dot(low(first), cq_weight, precision=HIGH))
        store_keys = rounded(jnp.dot(store, ck_weight, precision=HIGH)).reshape(N_DP, ENC_DEV, H, DH)
        store_values = rounded(jnp.dot(store, cv_weight, precision=HIGH)).reshape(N_DP, ENC_DEV, H, DH)

        def owner_part(pieces):
            tokens_here, blocks_here, keys_here, values_here = pieces
            copies = low_back(cross_queries[tokens_here]).reshape(slot_count, H, DH)
            scores = low_back(score_scale * jnp.einsum('qhd,khd->hqk', copies, keys_here, precision=HIGH))
            allowed = blocks_here[:, None] == key_block[None, :]
            scores = jnp.where(allowed[None], scores, NEGATIVE)
            totals = log_total(scores, 2)
            prob_rows = low(jnp.exp(scores - totals))
            part_rows = low_back(jnp.einsum('hqk,khd->qhd', prob_rows, values_here, precision=HIGH).reshape(slot_count, D))
            return (part_rows, low_back(jnp.transpose(totals[:, :, 0])))
        part_rows, part_sums = lax.map(jax.checkpoint(owner_part), (slot_token.reshape(N_DP, slot_count), slot_block.reshape(N_DP, slot_count), store_keys, store_values))
        part_out = part_rows.reshape(N_DP * slot_count, D)[request_pos].reshape(TOKENS, KB, H, DH)
        part_total = part_sums.reshape(N_DP * slot_count, H)[request_pos].reshape(TOKENS, KB, H)
        merge_weight = jnp.exp(part_total - log_total(part_total, 1))
        cross_sum = lax.optimization_barrier(jnp.sum(merge_weight[..., None] * part_out, 1)).reshape(TOKENS, D)
        cross_branch = low_back(jnp.dot(low(cross_sum), co_weight, precision=HIGH))
        second = normalize(first + cross_branch, gain_b, shift_b)
        hidden_pre = low_back(jnp.dot(low(second), up_weight, precision=HIGH))
        hidden_act = low(jax.nn.gelu(hidden_pre, approximate=False))
        ffn_branch = low_back(jnp.dot(hidden_act, down_weight, precision=HIGH))
        return normalize(second + ffn_branch, gain_c, shift_c)
    floats = tuple((item.astype(jnp.float32) for item in (decoder_layer_input, encoder_states, self_query, self_attention_key, self_value, self_out, gain_first, shift_first, cross_query, cross_key, cross_value, cross_out, gain_second, shift_second, hidden_up, hidden_down, gain_third, shift_third)))
    third, pullback = jax.vjp(forward, *floats)
    grads = pullback(out_grad.astype(jnp.float32))
    return (third.astype(jnp.bfloat16), grads[0], grads[1], grads[2], grads[3], grads[4], grads[5], grads[6], grads[7], grads[8], grads[9], grads[10], grads[11], grads[12], grads[13], grads[14], grads[15], grads[16], grads[17])
```

```python
import functools

import jax
import jax.numpy as jnp
from jax import lax
from jax.experimental import pallas as pl
from jax.experimental.pallas import tpu as pltpu
from jax.sharding import PartitionSpec as P

DH = 64
BLOCK = 128
LANES = 128
EPSILON = 1e-05
NEGATIVE = -1e30
VMEM_LIMIT = 56 * 1024 * 1024
BF16, F32 = jnp.bfloat16, jnp.float32


def nn(left, right):
    return lax.dot_general(left, right, (((1,), (0,)), ((), ())), preferred_element_type=F32)


def nt(left, right):
    return lax.dot_general(left, right, (((1,), (1,)), ((), ())), preferred_element_type=F32)


def tn(left, right):
    return lax.dot_general(left, right, (((0,), (0,)), ((), ())), preferred_element_type=F32)


def low_half(shape):
    return lax.broadcasted_iota(jnp.int32, shape, 1) < DH


def pick(low, head, own, other):
    return jnp.where(low, own, other) if head == 0 else jnp.where(low, other, own)


def split_three(values):
    high = values.astype(BF16)
    rest = values - high.astype(F32)
    middle = rest.astype(BF16)
    last = (rest - middle.astype(F32)).astype(BF16)
    return high.astype(F32), middle.astype(F32), last.astype(F32)


def widen(base, extra):
    return base if extra is None else jnp.concatenate([base, extra], 1)


def cross_forward_kernel(chunk, wide, *refs):
    if wide:
        q_ref, mask_ref, wide_mask_ref, k_ref, hot_ref, wide_hot_ref, v_ref = refs[:7]
        refs = refs[7:]
    else:
        q_ref, mask_ref, k_ref, hot_ref, v_ref = refs[:5]
        refs = refs[5:]
    sum_ref, mix_ref, total_ref, k_wide, v_wide, s_ref = refs
    keys, rows = k_ref.shape[0], q_ref.shape[0]

    @pl.when(pl.program_id(1) == 0)
    def _():
        for at in range(0, keys, chunk):
            part = slice(at, at + chunk)
            low = low_half((chunk, LANES))
            k, hot, v = k_ref[part, :], hot_ref[part, :], v_ref[part, :]
            for head in range(2):
                k_wide[head, part, :] = pick(low, head, k, hot)
                v_wide[head, part, :] = pick(low, head, v, jnp.ones_like(v))

    low = low_half((rows, LANES))
    q, mask = q_ref[...], mask_ref[...]
    sums, totals = [], []
    for head in range(2):
        q_wide = widen(pick(low, head, q, mask), wide_mask_ref[...] if wide else None)
        peak = jnp.full((rows, LANES), NEGATIVE, F32)
        for at in range(0, keys, chunk):
            part = slice(at, at + chunk)
            k = widen(k_wide[head, part, :], wide_hot_ref[part, :] if wide else None)
            scores = nt(q_wide, k)
            s_ref[head, :, part] = scores
            for lane in range(0, chunk, LANES):
                peak = jnp.maximum(peak, scores[:, lane : lane + LANES])
        top = jnp.max(peak, -1, keepdims=True)
        mixed = jnp.zeros((rows, LANES), F32)
        for at in range(0, keys, chunk):
            part = slice(at, at + chunk)
            prob = jnp.exp(s_ref[head, :, part] - top).astype(BF16)
            mixed = mixed + nn(prob, v_wide[head, part, :])
        weight = mixed[:, DH : DH + 1] if head == 0 else mixed[:, 0:1]
        sums.append(mixed / weight)
        totals.append(top + jnp.log(weight))
    total = jnp.where(low, sums[0], sums[1])
    sum_ref[...] = total
    mix_ref[...] = total.astype(BF16)
    total_ref[...] = jnp.where(low, totals[1], totals[0])


def cross_forward(q, mask, wide_mask, k, hot, wide_hot, v):
    rows, width = q.shape
    keys = k.shape[0]
    wide = wide_mask is not None
    tile = min(rows, 256 if keys <= 4096 else 64)
    chunk = min(keys, 512)
    by_tile = pl.BlockSpec((tile, LANES), lambda pair, i: (i, pair))
    by_pair = pl.BlockSpec((keys, LANES), lambda pair, i: (0, pair))
    same = pl.BlockSpec((keys, LANES), lambda pair, i: (0, 0))
    operands = [q, mask] + [wide_mask] * wide + [k, hot] + [wide_hot] * wide + [v]
    specs = [by_tile, pl.BlockSpec((tile, LANES), lambda pair, i: (i, 0))]
    if wide:
        specs.append(pl.BlockSpec((tile, wide_mask.shape[1]), lambda pair, i: (i, 0)))
    specs += [by_pair, same]
    if wide:
        specs.append(pl.BlockSpec((keys, wide_hot.shape[1]), lambda pair, i: (0, 0)))
    specs.append(by_pair)
    return pl.pallas_call(
        functools.partial(cross_forward_kernel, chunk, wide),
        grid=(width // LANES, rows // tile),
        in_specs=specs,
        out_specs=[by_tile] * 3,
        out_shape=[
            jax.ShapeDtypeStruct((rows, width), F32),
            jax.ShapeDtypeStruct((rows, width), BF16),
            jax.ShapeDtypeStruct((rows, width), F32),
        ],
        scratch_shapes=[
            pltpu.VMEM((2, keys, LANES), BF16),
            pltpu.VMEM((2, keys, LANES), BF16),
            pltpu.VMEM((2, tile, keys), F32),
        ],
        compiler_params=pltpu.CompilerParams(vmem_limit_bytes=VMEM_LIMIT),
        cost_estimate=pl.CostEstimate(
            flops=8 * rows * keys * width, bytes_accessed=8 * keys * width, transcendentals=rows * keys * width // DH
        ),
        name="cross_forward",
    )(*operands)


def cross_backward_kernel(free, wide, *refs):
    if wide:
        q_ref, mask_ref, wide_mask_ref, k_ref, hot_ref, wide_hot_ref, v_ref = refs[:7]
        refs = refs[7:]
    else:
        q_ref, mask_ref, k_ref, hot_ref, v_ref = refs[:5]
        refs = refs[5:]
    grad_ref, sum_ref, total_ref, dq_ref, dk_ref, dv_ref, q_wide, q_only, g_wide, g_only, dq_sum = refs
    rows, chunk = q_ref.shape[0], k_ref.shape[0]
    step = pl.program_id(1)

    @pl.when(step == 0)
    def _():
        size = min(rows, 256)
        low = low_half((size, LANES))
        lane = lax.broadcasted_iota(jnp.int32, (size, LANES), 1) % DH
        zero = jnp.zeros((size, LANES), F32)
        for at in range(0, rows, size):
            part = slice(at, at + size)
            q, grad = q_ref[part, :].astype(F32), grad_ref[part, :].astype(F32)
            high, middle, last = split_three(total_ref[part, :])
            extra = mask_ref[part, :].astype(F32)
            extra = jnp.where(lane == free, -high, extra)
            extra = jnp.where(lane == free + 1, -middle, extra)
            extra = jnp.where(lane == free + 2, -last, extra)
            inner = grad * sum_ref[part, :]
            inner_0 = jnp.sum(jnp.where(low, inner, zero), -1, keepdims=True)
            inner_1 = jnp.sum(jnp.where(low, zero, inner), -1, keepdims=True)
            high, middle, last = split_three(jnp.where(low, inner_1, inner_0))
            less = jnp.where(lane == 0, -high, jnp.where(lane == 1, -middle, jnp.where(lane == 2, -last, zero)))
            for head in range(2):
                q_wide[head, part, :] = pick(low, head, q, extra).astype(BF16)
                q_only[head, part, :] = pick(low, head, q, zero).astype(BF16)
                g_wide[head, part, :] = pick(low, head, grad, less).astype(BF16)
                g_only[head, part, :] = pick(low, head, grad, zero).astype(BF16)
        dq_sum[...] = jnp.zeros_like(dq_sum)

    low = low_half((chunk, LANES))
    k, hot, v = k_ref[...], hot_ref[...], v_ref[...]
    dk = dv = None
    for head in range(2):
        k_wide = widen(pick(low, head, k, hot), wide_hot_ref[...] if wide else None)
        queries = widen(q_wide[head], wide_mask_ref[...] if wide else None)
        prob = jnp.exp(nt(k_wide, queries))
        prob_grad = nt(pick(low, head, v, jnp.ones_like(v)), g_wide[head])
        score_grad = (prob * prob_grad).astype(BF16)
        dv_head, dk_head = nn(prob.astype(BF16), g_only[head]), nn(score_grad, q_only[head])
        dv = dv_head if dv is None else dv + dv_head
        dk = dk_head if dk is None else dk + dk_head
        dq_sum[...] += tn(pick(low, head, k, jnp.zeros_like(k)), score_grad)
    dk_ref[...] = dk.astype(dk_ref.dtype)
    dv_ref[...] = dv.astype(dv_ref.dtype)

    @pl.when(step == pl.num_programs(1) - 1)
    def _():
        dq_ref[...] = (dq_sum[...].T * DH**-0.5).astype(dq_ref.dtype)


def cross_backward(q, mask, wide_mask, k, hot, wide_hot, v, grad, cross_sum, total, free):
    rows, width = q.shape
    keys = k.shape[0]
    wide = wide_mask is not None
    chunk = min(keys, 512)
    by_pair = pl.BlockSpec((rows, LANES), lambda pair, i: (0, pair))
    by_chunk = pl.BlockSpec((chunk, LANES), lambda pair, i: (i, pair))
    operands = [q, mask] + [wide_mask] * wide + [k, hot] + [wide_hot] * wide + [v, grad, cross_sum, total]
    specs = [by_pair, pl.BlockSpec((rows, LANES), lambda pair, i: (0, 0))]
    if wide:
        specs.append(pl.BlockSpec((rows, wide_mask.shape[1]), lambda pair, i: (0, 0)))
    specs += [by_chunk, pl.BlockSpec((chunk, LANES), lambda pair, i: (i, 0))]
    if wide:
        specs.append(pl.BlockSpec((chunk, wide_hot.shape[1]), lambda pair, i: (i, 0)))
    specs += [by_chunk, by_pair, by_pair, by_pair]
    return pl.pallas_call(
        functools.partial(cross_backward_kernel, free, wide),
        grid=(width // LANES, keys // chunk),
        in_specs=specs,
        out_specs=[by_pair, by_chunk, by_chunk],
        out_shape=[
            jax.ShapeDtypeStruct((rows, width), BF16),
            jax.ShapeDtypeStruct((keys, width), BF16),
            jax.ShapeDtypeStruct((keys, width), BF16),
        ],
        scratch_shapes=[pltpu.VMEM((2, rows, LANES), BF16)] * 4 + [pltpu.VMEM((LANES, rows), F32)],
        compiler_params=pltpu.CompilerParams(vmem_limit_bytes=VMEM_LIMIT),
        cost_estimate=pl.CostEstimate(
            flops=20 * rows * keys * width, bytes_accessed=8 * keys * width, transcendentals=rows * keys * width // DH
        ),
        name="cross_backward",
    )(*operands)


def self_forward_kernel(tile, q_ref, k_ref, v_ref, mix_ref, total_ref):
    rows = q_ref.shape[0]
    low_all = low_half((rows, LANES))
    low = low_half((tile, LANES))
    k, v = k_ref[...], v_ref[...]
    zero = jnp.zeros_like(k)
    keys = [pick(low_all, head, k, zero) for head in range(2)]
    values = [pick(low_all, head, v, jnp.ones_like(v)) for head in range(2)]
    ahead = lax.broadcasted_iota(jnp.int32, (tile, tile), 1) > lax.broadcasted_iota(jnp.int32, (tile, tile), 0)
    for at in range(0, rows, tile):
        q = q_ref[at : at + tile, :]
        sums, totals = [], []
        for head in range(2):
            edge = jnp.where(ahead, NEGATIVE, nt(q, keys[head][at : at + tile]))
            top = jnp.max(edge, -1, keepdims=True)
            if at:
                before = nt(q, keys[head][:at])
                top = jnp.maximum(top, jnp.max(before, -1, keepdims=True))
            mixed = nn(jnp.exp(edge - top).astype(BF16), values[head][at : at + tile])
            if at:
                mixed = mixed + nn(jnp.exp(before - top).astype(BF16), values[head][:at])
            weight = mixed[:, DH : DH + 1] if head == 0 else mixed[:, 0:1]
            sums.append(mixed / weight)
            totals.append(top + jnp.log(weight))
        mix_ref[at : at + tile, :] = jnp.where(low, sums[0], sums[1]).astype(BF16)
        total_ref[:, at : at + tile] = jnp.where(low, totals[0], totals[1]).T


def self_forward(q, k, v):
    rows, width = q.shape
    by_pair = pl.BlockSpec((rows, LANES), lambda pair: (0, pair))
    mix, total = pl.pallas_call(
        functools.partial(self_forward_kernel, min(rows, 256)),
        grid=(width // LANES,),
        in_specs=[by_pair] * 3,
        out_specs=[by_pair, pl.BlockSpec((LANES, rows), lambda pair: (pair, 0))],
        out_shape=[jax.ShapeDtypeStruct((rows, width), BF16), jax.ShapeDtypeStruct((width, rows), F32)],
        compiler_params=pltpu.CompilerParams(vmem_limit_bytes=VMEM_LIMIT),
        cost_estimate=pl.CostEstimate(
            flops=4 * rows * rows * width, bytes_accessed=8 * rows * width, transcendentals=rows * rows * width // DH
        ),
        name="self_forward",
    )(q, k, v)
    return mix, total.reshape(width // DH, DH, rows)[:, 0, :]


def self_backward_kernel(
    tile, shift_ref, q_ref, k_ref, v_ref, grad_ref, mix_ref, total_ref, out_ref, q_all, k_all, v_all, g_all, m_all
):
    rows = q_ref.shape[0]
    width = out_ref.shape[1] // 3
    pair = pl.program_id(0)
    tiles = rows // tile

    def place(i):
        return pl.ds(pl.multiple_of((i * tile + rows - shift_ref[0]) % rows, tile), tile)

    for i in range(tiles):
        part, here = slice(i * tile, (i + 1) * tile), place(i)
        for ref, held in ((q_ref, q_all), (k_ref, k_all), (v_ref, v_all), (grad_ref, g_all), (mix_ref, m_all)):
            held[part, :] = ref[here, :]
    low_all = low_half((rows, LANES))
    low = low_half((tile, LANES))
    q, grad = q_all[...], g_all[...]
    zero = jnp.zeros_like(q)
    q_only = [pick(low_all, head, q, zero) for head in range(2)]
    g_only = [pick(low_all, head, grad, zero) for head in range(2)]
    inner = grad.astype(F32) * m_all[...].astype(F32)
    mine = lax.broadcasted_iota(jnp.int32, (8, LANES), 1) < DH
    ones = lax.broadcasted_iota(jnp.int32, (8, LANES), 0) == jnp.where(mine, 0, 1)
    inners = lax.dot_general(
        ones.astype(F32), inner, (((1,), (1,)), ((), ())), precision=lax.Precision.HIGHEST, preferred_element_type=F32
    )
    behind = lax.broadcasted_iota(jnp.int32, (tile, tile), 0) > lax.broadcasted_iota(jnp.int32, (tile, tile), 1)
    dq = [None] * tiles
    for i in range(tiles):
        part = slice(i * tile, (i + 1) * tile)
        k, v = k_all[part, :], v_all[part, :]
        dk = dv = None
        for head in range(2):
            k_only = pick(low, head, k, jnp.zeros_like(k))
            v_only = pick(low, head, v, jnp.zeros_like(v))
            for j in range(i, tiles):
                at = slice(j * tile, (j + 1) * tile)
                scores = nt(k_only, q_all[at, :]) - total_ref[0, head : head + 1, at]
                if i == j:
                    scores = jnp.where(behind, NEGATIVE, scores)
                prob = jnp.exp(scores)
                prob_grad = nt(v_only, g_all[at, :])
                score_grad = (prob * (prob_grad - inners[head : head + 1, at])).astype(BF16)
                dv_part = nn(prob.astype(BF16), g_only[head][at])
                dk_part = nn(score_grad, q_only[head][at])
                dq_part = tn(score_grad, k_only)
                dv = dv_part if dv is None else dv + dv_part
                dk = dk_part if dk is None else dk + dk_part
                dq[j] = dq_part if dq[j] is None else dq[j] + dq_part
        for which, value in ((1, dk), (2, dv)):
            column = pl.multiple_of(which * width + pair * LANES, LANES)
            out_ref[place(i), pl.ds(column, LANES)] = value.astype(BF16)
    for i in range(tiles):
        out_ref[place(i), pl.ds(pl.multiple_of(pair * LANES, LANES), LANES)] = (dq[i] * DH**-0.5).astype(BF16)


def self_backward(shift, q, k, v, grad, mix, total):
    rows, width = q.shape
    pairs = width // LANES
    by_pair = pl.BlockSpec((rows, LANES), lambda pair, shift: (0, pair))
    return pl.pallas_call(
        functools.partial(self_backward_kernel, min(rows, 256)),
        grid_spec=pltpu.PrefetchScalarGridSpec(
            num_scalar_prefetch=1,
            grid=(pairs,),
            in_specs=[by_pair] * 5 + [pl.BlockSpec((1, 2, rows), lambda pair, shift: (pair, 0, 0))],
            out_specs=pl.BlockSpec((rows, 3 * width), lambda pair, shift: (0, 0)),
            scratch_shapes=[pltpu.VMEM((rows, LANES), BF16)] * 5,
        ),
        out_shape=jax.ShapeDtypeStruct((rows, 3 * width), BF16),
        compiler_params=pltpu.CompilerParams(vmem_limit_bytes=VMEM_LIMIT),
        cost_estimate=pl.CostEstimate(
            flops=10 * rows * rows * width, bytes_accessed=16 * rows * width, transcendentals=rows * rows * width // DH
        ),
        name="self_backward",
    )(shift.reshape(1), q, k, v, grad, mix, total.reshape(pairs, 2, rows))


def normalize(values):
    center = values - jnp.mean(values, -1, keepdims=True)
    scale = lax.rsqrt(jnp.mean(center * center, -1, keepdims=True) + EPSILON)
    return center * scale, scale


def norm_backward(unit, scale, gain, upstream):
    weighted = upstream * gain
    grad = weighted - jnp.mean(weighted, -1, keepdims=True) - unit * jnp.mean(weighted * unit, -1, keepdims=True)
    return grad * scale, jnp.sum(upstream * unit, 0), jnp.sum(upstream, 0)


def roll_chunks(rows, parts, shift):
    size = rows.shape[0] // parts
    result = rows
    for by in range(1, parts):
        rolled = jnp.concatenate([rows[by * size :], rows[: by * size]], 0)
        result = jnp.where(shift == by, rolled, result)
    return result


class Places:
    def __init__(self):
        self.mp, self.dp = lax.axis_size("mp"), lax.axis_size("dp")
        self.chips = self.dp // 2
        self.x, self.d = lax.axis_index("mp"), lax.axis_index("dp")
        self.core, self.chip = self.d % 2, self.d // 2
        self.line = self.x * 2 + self.core
        self.shard, self.seq = self.line % self.mp, self.line // self.mp

    def send(self, values, target):
        pairs = []
        for chip in range(self.chips):
            for x in range(self.mp):
                for core in range(2):
                    to_chip, to_x, to_core = target(chip, x, core)
                    pairs.append(
                        ((chip * 2 + core) * self.mp + x, (to_chip * 2 + to_core) * self.mp + to_x)
                    )
        return lax.ppermute(values, ("dp", "mp"), pairs)

    def to_work(self, values):
        return self.send(values, lambda chip, x, core: (chip, (core * self.mp + x) // 2, (core * self.mp + x) % 2))

    def from_work(self, values):
        mp = self.mp
        return self.send(values, lambda chip, x, core: (chip, (x * 2 + core) % mp, (x * 2 + core) // mp))

    def sequence(self, values):
        other = self.send(values, lambda chip, x, core: (chip, x, 1 - core))
        return jnp.where(self.core == self.seq, values, other)

    def along(self, values, shift):
        def target(chip, x, core):
            line = x * 2 + core
            line = line // self.mp * self.mp + (line + shift) % self.mp
            return chip, line // 2, line % 2

        return self.send(values, target)

    def scatter_sum(self, product, left):
        size = left.shape[0] // self.mp
        arrived = [
            self.along(product(left[by * size : (by + 1) * size]).astype(BF16), by) for by in range(1, self.mp)
        ]
        total = product(left[:size])
        for rows in arrived:
            total = total + rows.astype(F32)
        return total

    def gather(self, rows):
        return jnp.concatenate([rows] + [self.along(rows, -by) for by in range(1, self.mp)], 0)

    def spread(self, rows):
        mp = self.mp
        arrived = []
        for turn in range(mp):

            def target(chip, x, core, turn=turn):
                line = x * 2 + core
                return chip, (line % mp - turn) % mp, line // mp

            arrived.append(self.send(rows, target))
        return roll_chunks(jnp.concatenate(arrived, 0), mp, (mp - self.x) % mp)

    def bits(self):
        return self.chips.bit_length() - 1

    def meet(self, values, bit):
        mp = self.mp

        def target(chip, x, core):
            if bit == "sequence":
                line = (x * 2 + core + mp) % (2 * mp)
                return chip, line // 2, line % 2
            if bit == "core":
                return chip, x, 1 - core
            if isinstance(bit, tuple):
                return chip, x ^ (1 << bit[1]), core
            return chip ^ (1 << bit), x, core

        return self.send(values, target)

    def my_bit(self, bit):
        if bit == "sequence":
            return self.seq
        if bit == "core":
            return self.core
        return (self.chip >> bit) & 1

    def reduce_scatter(self, values, order, last):
        bits = self.bits()
        axes = [bits - 1 - i for i in range(bits)] + [last]
        values = values.reshape([2] * (bits + 1) + [values.shape[0] // 2 ** (bits + 1), values.shape[1]])
        for step, bit in enumerate(order):
            axis = axes.index(bit)
            mine = self.my_bit(bit)
            first = lax.index_in_dim(values, 0, axis, False)
            second = lax.index_in_dim(values, 1, axis, False)
            arrived = self.meet(jnp.where(mine == 0, second, first), bit)
            values = jnp.where(mine == 0, first, second).astype(F32) + arrived.astype(F32)
            if step < len(order) - 1:
                values = values.astype(BF16)
            axes.pop(axis)
        return values

    def weight_sum(self, grads, order):
        return self.from_work(self.reduce_scatter(grads, order, "sequence").astype(BF16)).astype(F32)


def per_device(
    decoder_layer_input,
    encoder_states,
    retrieved_owner,
    retrieved_block,
    self_query,
    self_attention_key,
    self_value,
    self_out,
    gain_first,
    shift_first,
    cross_query,
    cross_key,
    cross_value,
    cross_out,
    gain_second,
    shift_second,
    hidden_up,
    hidden_down,
    gain_third,
    shift_third,
    out_grad,
):
    at = Places()
    score_scale = jnp.asarray(DH**-0.5, BF16)
    seq_len, width = decoder_layer_input.shape
    shard_width = self_query.shape[1]
    chunk = seq_len // at.mp
    keys = encoder_states.shape[0] * at.dp
    bits = at.bits()

    def even(weight):
        extra = -weight.shape[1] % LANES
        return jnp.pad(weight, ((0, 0), (0, extra))) if extra else weight

    def even_rows(weight):
        extra = -weight.shape[0] % LANES
        return jnp.pad(weight, ((0, extra), (0, 0))) if extra else weight

    q_first = nn(decoder_layer_input, even(self_query)).astype(BF16) * score_scale
    k_first = nn(decoder_layer_input, even(self_attention_key)).astype(BF16)
    v_first = nn(decoder_layer_input, even(self_value)).astype(BF16)
    store = lax.all_gather(encoder_states, "dp", axis=0, tiled=True)
    mix_first, total_first = self_forward(q_first, k_first, v_first)
    self_mix = roll_chunks(at.to_work(mix_first), at.mp, at.shard)
    self_total = at.to_work(total_first)

    w_out = even_rows(at.to_work(self_out))
    w_cross_query = even(at.to_work(cross_query))
    w_cross_key = even(at.to_work(cross_key))
    w_cross_value = even(at.to_work(cross_value))
    w_cross_out = even_rows(at.to_work(cross_out))
    w_up = at.to_work(hidden_up)
    w_down = at.to_work(hidden_down)
    w_query = even(at.to_work(self_query))
    w_key = even(at.to_work(self_attention_key))
    w_value = even(at.to_work(self_value))
    rows_in = roll_chunks(at.sequence(decoder_layer_input), at.mp, at.shard)
    rows_grad = roll_chunks(at.sequence(out_grad), at.mp, at.shard)[:chunk].astype(F32)
    blocks = roll_chunks(
        at.sequence(retrieved_owner * (encoder_states.shape[0] // BLOCK) + retrieved_block), at.mp, at.shard
    )

    block_count = keys // BLOCK
    wanted = (blocks[:, :, None] == jnp.arange(block_count, dtype=jnp.int32)[None, None, :]).any(1)
    barred = jnp.where(wanted, 0.0, NEGATIVE).astype(BF16)
    hot = (jnp.arange(keys)[:, None] // BLOCK == jnp.arange(block_count)[None, :]).astype(BF16)
    wide = block_count + 3 > DH
    free = 0 if wide else block_count
    ones = jnp.ones((keys, 3), BF16)
    if wide:
        wide_mask, wide_hot = barred, hot
        half_mask = jnp.zeros((seq_len, DH), BF16)
        half_hot = jnp.pad(ones, ((0, 0), (0, DH - 3)))
    else:
        wide_mask = wide_hot = None
        half_mask = jnp.pad(barred, ((0, 0), (0, DH - block_count)))
        half_hot = jnp.pad(jnp.concatenate([hot, ones], 1), ((0, 0), (0, DH - 3 - block_count)))
    mask, hot = jnp.concatenate([half_mask] * 2, 1), jnp.concatenate([half_hot] * 2, 1)

    first_in = rows_in[:chunk].astype(F32) + at.scatter_sum(lambda rows: nn(rows, w_out), self_mix)
    first_unit, first_scale = normalize(first_in)
    first = first_unit * gain_first + shift_first
    first_low = at.gather(first.astype(BF16))
    store_keys = nn(store, w_cross_key).astype(BF16)
    store_values = nn(store, w_cross_value).astype(BF16)
    queries = nn(first_low, w_cross_query).astype(BF16) * score_scale
    cross_sum, cross_mix, cross_total = cross_forward(
        queries, mask, wide_mask, store_keys, hot, wide_hot, store_values
    )
    second_in = first + at.scatter_sum(lambda rows: nn(rows, w_cross_out), cross_mix)
    second_unit, second_scale = normalize(second_in)
    second = second_unit * gain_second + shift_second
    second_low = at.gather(second.astype(BF16))
    hidden_pre = nn(second_low, w_up)
    bell = 0.5 + 0.5 * lax.erf(hidden_pre * 0.5**0.5)
    hidden_act = (hidden_pre * bell).astype(BF16)
    slope = bell + hidden_pre * jnp.exp(-0.5 * hidden_pre * hidden_pre) * 0.3989422804014327
    third_in = second + at.scatter_sum(lambda rows: nn(rows, w_down), hidden_act)
    third_unit, third_scale = normalize(third_in)
    layer_out = at.spread((third_unit * gain_third + shift_third).astype(BF16))

    res3_grad, gain_third_grad, shift_third_grad = norm_backward(third_unit, third_scale, gain_third, rows_grad)
    ffn_grad = at.gather(res3_grad.astype(BF16))
    pre_grad = (slope * nt(ffn_grad, w_down)).astype(BF16)
    second_grad = res3_grad + at.scatter_sum(lambda rows: nt(rows, w_up), pre_grad)
    hidden_down_grad = at.weight_sum(tn(ffn_grad, hidden_act).astype(BF16), ["sequence"] + list(range(bits)))
    hidden_up_grad = at.weight_sum(tn(second_low, pre_grad).astype(BF16), list(range(bits)) + ["sequence"])
    res2_grad, gain_second_grad, shift_second_grad = norm_backward(
        second_unit, second_scale, gain_second, second_grad
    )
    cross_grad = at.gather(res2_grad.astype(BF16))
    mix_grad = nt(cross_grad, w_cross_out).astype(BF16)
    queries_grad, keys_grad, values_grad = cross_backward(
        queries, mask, wide_mask, store_keys, hot, wide_hot, store_values, mix_grad, cross_sum, cross_total, free
    )
    first_grad = res2_grad + at.scatter_sum(lambda rows: nt(rows, w_cross_query), queries_grad)
    res1_grad, gain_first_grad, shift_first_grad = norm_backward(first_unit, first_scale, gain_first, first_grad)
    self_grad = at.gather(res1_grad.astype(BF16))

    store_part = (nt(keys_grad, w_cross_key) + nt(values_grad, w_cross_value)).astype(BF16)
    encoder_grad = at.reduce_scatter(store_part, ["core"] + list(range(bits)), "core")
    for bit in range(at.mp.bit_length() - 1):
        encoder_grad = encoder_grad + at.meet(encoder_grad.astype(BF16), ("x", bit)).astype(F32)

    side_grads = [
        tn(cross_grad, cross_mix),
        tn(first_low, queries_grad),
        tn(store, keys_grad),
        tn(store, values_grad),
        tn(self_grad, self_mix),
    ]
    side_width = side_grads[0].shape[1]
    side = at.weight_sum(jnp.concatenate([g.astype(BF16) for g in side_grads], 1), ["sequence"] + list(range(bits)))
    cross_out_grad, cross_query_grad, cross_key_grad, cross_value_grad, self_out_grad = (
        side[:, i * side_width : i * side_width + shard_width] for i in range(5)
    )

    smix_grad = nt(self_grad, w_out).astype(BF16)
    seq_queries = nn(rows_in, w_query).astype(BF16) * score_scale
    seq_keys = nn(rows_in, w_key).astype(BF16)
    seq_values = nn(rows_in, w_value).astype(BF16)
    triple = self_backward(
        (at.shard * chunk).astype(jnp.int32), seq_queries, seq_keys, seq_values, smix_grad, self_mix, self_total
    )
    w_triple = jnp.concatenate([w_query, w_key, w_value], 1)
    input_grad = at.spread(
        (res1_grad + at.scatter_sum(lambda rows: nt(rows, w_triple), triple)).astype(BF16)
    ).astype(F32)
    triple_grad = at.weight_sum(tn(rows_in, triple).astype(BF16), list(range(bits)) + ["sequence"])
    side_width = triple.shape[1] // 3
    self_query_grad, self_key_grad, self_value_grad = (
        triple_grad[:, i * side_width : i * side_width + shard_width] for i in range(3)
    )

    norms = jnp.stack(
        [
            gain_first_grad,
            shift_first_grad,
            gain_second_grad,
            shift_second_grad,
            gain_third_grad,
            shift_third_grad,
        ]
    )
    for bit in ["core"] + [("x", i) for i in range(at.mp.bit_length() - 1)] + list(range(bits)):
        norms = norms + at.meet(norms, bit)
    share = width // at.dp
    norms = lax.dynamic_slice_in_dim(norms, at.d * share, share, 1)
    return (
        layer_out,
        input_grad,
        encoder_grad,
        self_query_grad,
        self_key_grad,
        self_value_grad,
        self_out_grad.T,
        norms[0],
        norms[1],
        cross_query_grad,
        cross_key_grad,
        cross_value_grad,
        cross_out_grad.T,
        norms[2],
        norms[3],
        hidden_up_grad,
        hidden_down_grad.T,
        norms[4],
        norms[5],
    )


def solution(mesh):
    rows, columns, parts, copied = P("dp", None), P(None, "mp"), P("mp", None), P()
    return jax.shard_map(
        per_device,
        mesh=mesh,
        in_specs=(rows,) * 4
        + (columns,) * 3
        + (parts, copied, copied)
        + (columns,) * 3
        + (parts, copied, copied)
        + (columns, parts, copied, copied, rows),
        out_specs=(rows,) * 3
        + (P("dp", "mp"),) * 3
        + (P("mp", "dp"), P("dp"), P("dp"))
        + (P("dp", "mp"),) * 3
        + (P("mp", "dp"), P("dp"), P("dp"))
        + (P("dp", "mp"), P("mp", "dp"), P("dp"), P("dp")),
        check_vma=False,
    )
```

```python
import functools

import jax
import jax.numpy as jnp
import numpy as np
from jax import lax
from jax.experimental import pallas as pl
from jax.experimental.pallas import tpu as pltpu
from jax.sharding import PartitionSpec as P

DH = 64
BLOCK = 128
LANES = 128
EPSILON = 1e-05
NEGATIVE = -1e30
VMEM_LIMIT = 56 * 1024 * 1024
BF16, F32 = jnp.bfloat16, jnp.float32


def nn(left, right):
    return lax.dot_general(left, right, (((1,), (0,)), ((), ())), preferred_element_type=F32)


def nt(left, right):
    return lax.dot_general(left, right, (((1,), (1,)), ((), ())), preferred_element_type=F32)


def tn(left, right):
    return lax.dot_general(left, right, (((0,), (0,)), ((), ())), preferred_element_type=F32)


def low_half(shape):
    return lax.broadcasted_iota(jnp.int32, shape, 1) < DH


def pick(low, head, own, other):
    return jnp.where(low, own, other) if head == 0 else jnp.where(low, other, own)


def split_three(values):
    high = values.astype(BF16)
    rest = values - high.astype(F32)
    middle = rest.astype(BF16)
    last = (rest - middle.astype(F32)).astype(BF16)
    return high.astype(F32), middle.astype(F32), last.astype(F32)


def widen(base, extra):
    return base if extra is None else jnp.concatenate([base, extra], 1)


def barred_lanes(names, blocks, period):
    shape = (names.shape[0], LANES)
    lane = lax.broadcasted_iota(jnp.int32, shape, 1) % period
    found = lane >= blocks
    for request in range(names.shape[1]):
        found = found | (names[:, request : request + 1] == lane)
    return jnp.where(found, 0.0, NEGATIVE)


def key_terms(keys, wide):
    blocks = keys // BLOCK
    free = 0 if wide else blocks
    block, lane = np.arange(keys)[:, None] // BLOCK, np.arange(LANES)[None, :]
    ones = (lane % DH >= free) & (lane % DH < free + 3)
    if wide:
        terms = np.concatenate([np.broadcast_to(ones, (keys, LANES)), block == lane], 1)
    else:
        terms = ones | (block == lane % DH)
    return jnp.asarray(terms.astype(np.float32), BF16)


def cross_forward_kernel(
    chunk, blocks, wide, q_ref, names_ref, kv_ref, terms_ref, sum_ref, mix_ref, total_ref, barred_ref, k_wide, v_wide, s_ref
):
    keys, rows = kv_ref.shape[0], q_ref.shape[0]

    @pl.when(pl.program_id(1) == 0)
    def _():
        for at in range(0, keys, chunk):
            part = slice(at, at + chunk)
            low = low_half((chunk, LANES))
            k, v = kv_ref[part, :LANES], kv_ref[part, LANES:]
            terms = terms_ref[part, :]
            for head in range(2):
                k_wide[head, part, :] = widen(
                    pick(low, head, k, terms[:, :LANES]), terms[:, LANES:] if wide else None
                )
                v_wide[head, part, :] = pick(low, head, v, jnp.ones_like(v))

    low = low_half((rows, LANES))
    q = q_ref[...]
    here = pl.ds(pl.multiple_of(pl.program_id(1) * rows, rows), rows)

    @pl.when(pl.program_id(0) == 0)
    def _():
        barred_ref[here, :] = barred_lanes(names_ref[...], blocks, LANES if wide else DH).astype(BF16)

    barred = barred_ref[here, :]
    sums, totals = [], []
    for head in range(2):
        q_wide = widen(pick(low, head, q, jnp.zeros_like(q)), barred) if wide else pick(low, head, q, barred)
        peak = jnp.full((rows, LANES), -jnp.inf, F32)
        for at in range(0, keys, chunk):
            part = slice(at, at + chunk)
            scores = nt(q_wide, k_wide[head, part, :])
            s_ref[head, :, part] = scores
            for lane in range(0, chunk, LANES):
                peak = jnp.maximum(peak, scores[:, lane : lane + LANES])
        top = jnp.max(peak, -1, keepdims=True)
        mixed = jnp.zeros((rows, LANES), F32)
        for at in range(0, keys, chunk):
            part = slice(at, at + chunk)
            prob = jnp.exp(s_ref[head, :, part] - top).astype(BF16)
            mixed = mixed + nn(prob, v_wide[head, part, :])
        weight = mixed[:, DH : DH + 1] if head == 0 else mixed[:, 0:1]
        sums.append(mixed / weight)
        totals.append(top + jnp.log(weight))
    sums, totals = jnp.where(low, sums[0], sums[1]), jnp.where(low, totals[0], totals[1])
    sum_ref[...] = sums
    mix_ref[...] = sums.astype(BF16)
    total_ref[...] = totals


def cross_forward(q, names, kv, terms):
    rows, width = q.shape
    keys = kv.shape[0]
    blocks = keys // BLOCK
    wide = blocks + 3 > DH
    tile = min(rows, 256 if keys <= 4096 else 64)
    chunk = min(keys, 512)
    by_tile = pl.BlockSpec((tile, LANES), lambda pair, i: (i, pair))
    return pl.pallas_call(
        functools.partial(cross_forward_kernel, chunk, blocks, wide),
        grid=(width // LANES, rows // tile),
        in_specs=[
            by_tile,
            pl.BlockSpec((tile, names.shape[1]), lambda pair, i: (i, 0)),
            pl.BlockSpec((keys, 2 * LANES), lambda pair, i: (0, pair)),
            pl.BlockSpec(terms.shape, lambda pair, i: (0, 0)),
        ],
        out_specs=[by_tile] * 3 + [pl.BlockSpec((rows, LANES), lambda pair, i: (0, 0))],
        out_shape=[
            jax.ShapeDtypeStruct((rows, width), F32),
            jax.ShapeDtypeStruct((rows, width), BF16),
            jax.ShapeDtypeStruct((rows, width), F32),
            jax.ShapeDtypeStruct((rows, LANES), BF16),
        ],
        scratch_shapes=[
            pltpu.VMEM((2, keys, 2 * LANES if wide else LANES), BF16),
            pltpu.VMEM((2, keys, LANES), BF16),
            pltpu.VMEM((2, tile, keys), F32),
        ],
        compiler_params=pltpu.CompilerParams(vmem_limit_bytes=VMEM_LIMIT),
        cost_estimate=pl.CostEstimate(flops=2 * rows * keys * width, bytes_accessed=8 * keys * width, transcendentals=0),
        name="cross_forward",
    )(q, names, kv, terms)


def cross_backward_kernel(blocks, wide, merge, *refs):
    q_ref, barred_ref, kv_ref, terms_ref, grad_ref, sum_ref, total_ref = refs[:7]
    refs = refs[7:]
    if merge:
        old_ref, refs = refs[0], refs[1:]
    dq_ref, dkv_ref, q_wide, q_only, g_wide, g_only, dq_sum = refs
    rows, chunk = q_ref.shape[0], kv_ref.shape[0]
    step = pl.program_id(1)
    free = 0 if wide else blocks

    @pl.when(step == 0)
    def _():
        size = min(rows, 256)
        low = low_half((size, LANES))
        lane = lax.broadcasted_iota(jnp.int32, (size, LANES), 1) % DH
        zero = jnp.zeros((size, LANES), F32)
        for at in range(0, rows, size):
            part = slice(at, at + size)
            q, grad = q_ref[part, :].astype(F32), grad_ref[part, :].astype(F32)
            total = total_ref[part, :]
            high, middle, last = split_three(jnp.where(low, total[:, DH : DH + 1], total[:, 0:1]))
            barred = barred_ref[part, :].astype(F32)
            extra = zero if wide else barred
            extra = jnp.where(lane == free, -high, extra)
            extra = jnp.where(lane == free + 1, -middle, extra)
            extra = jnp.where(lane == free + 2, -last, extra)
            inner = grad * sum_ref[part, :]
            inner_0 = jnp.sum(jnp.where(low, inner, zero), -1, keepdims=True)
            inner_1 = jnp.sum(jnp.where(low, zero, inner), -1, keepdims=True)
            high, middle, last = split_three(jnp.where(low, inner_1, inner_0))
            less = jnp.where(lane == 0, -high, jnp.where(lane == 1, -middle, jnp.where(lane == 2, -last, zero)))
            for head in range(2):
                q_wide[head, part, :] = widen(pick(low, head, q, extra), barred if wide else None).astype(BF16)
                q_only[head, part, :] = pick(low, head, q, zero).astype(BF16)
                g_wide[head, part, :] = pick(low, head, grad, less).astype(BF16)
                g_only[head, part, :] = pick(low, head, grad, zero).astype(BF16)
        dq_sum[...] = jnp.zeros_like(dq_sum)

    low = low_half((chunk, LANES))
    k, v = kv_ref[:, :LANES], kv_ref[:, LANES:]
    terms, own_terms = terms_ref[:, :LANES], terms_ref[:, LANES:] if wide else None
    dk = dv = None
    for head in range(2):
        prob = jnp.exp(nt(widen(pick(low, head, k, terms), own_terms), q_wide[head]))
        prob_grad = nt(pick(low, head, v, jnp.ones_like(v)), g_wide[head])
        score_grad = (prob * prob_grad).astype(BF16)
        dv_head, dk_head = nn(prob.astype(BF16), g_only[head]), nn(score_grad, q_only[head])
        dv = dv_head if dv is None else dv + dv_head
        dk = dk_head if dk is None else dk + dk_head
        dq_sum[...] += tn(pick(low, head, k, jnp.zeros_like(k)), score_grad)
    dkv_ref[:, :LANES] = dk.astype(dkv_ref.dtype)
    dkv_ref[:, LANES:] = dv.astype(dkv_ref.dtype)

    @pl.when(step == pl.num_programs(1) - 1)
    def _():
        dq = dq_sum[...].T * DH**-0.5
        if merge:
            dq = dq + old_ref[...]
        dq_ref[...] = dq.astype(dq_ref.dtype)


def cross_backward(q, barred, kv, terms, start, keys, grad, cross_sum, total, old, final):
    rows, width = q.shape
    blocks = kv.shape[0] // BLOCK
    wide = blocks + 3 > DH
    chunk = min(keys, 512)
    by_pair = pl.BlockSpec((rows, LANES), lambda pair, i: (0, pair))
    return pl.pallas_call(
        functools.partial(cross_backward_kernel, blocks, wide, bool(old)),
        grid=(width // LANES, keys // chunk),
        in_specs=[
            by_pair,
            pl.BlockSpec((rows, LANES), lambda pair, i: (0, 0)),
            pl.BlockSpec((chunk, 2 * LANES), lambda pair, i: (i + start // chunk, pair)),
            pl.BlockSpec((chunk, terms.shape[1]), lambda pair, i: (i + start // chunk, 0)),
        ]
        + [by_pair] * (3 + len(old)),
        out_specs=[by_pair, pl.BlockSpec((chunk, 2 * LANES), lambda pair, i: (i, pair))],
        out_shape=[
            jax.ShapeDtypeStruct((rows, width), BF16 if final else F32),
            jax.ShapeDtypeStruct((keys, 2 * width), BF16),
        ],
        scratch_shapes=[pltpu.VMEM((2, rows, 2 * LANES if wide else LANES), BF16)]
        + [pltpu.VMEM((2, rows, LANES), BF16)] * 3
        + [pltpu.VMEM((LANES, rows), F32)],
        compiler_params=pltpu.CompilerParams(vmem_limit_bytes=VMEM_LIMIT),
        cost_estimate=pl.CostEstimate(flops=2 * rows * keys * width, bytes_accessed=8 * keys * width, transcendentals=0),
        name="cross_backward",
    )(q, barred, kv, terms, grad, cross_sum, total, *old)


def self_forward_kernel(tile, q_ref, k_ref, v_ref, mix_ref, total_ref):
    rows = q_ref.shape[0]
    low_all = low_half((rows, LANES))
    low = low_half((tile, LANES))
    k, v = k_ref[...], v_ref[...]
    zero = jnp.zeros_like(k)
    keys = [pick(low_all, head, k, zero) for head in range(2)]
    values = [pick(low_all, head, v, jnp.ones_like(v)) for head in range(2)]
    ahead = lax.broadcasted_iota(jnp.int32, (tile, tile), 1) > lax.broadcasted_iota(jnp.int32, (tile, tile), 0)
    for at in range(0, rows, tile):
        q = q_ref[at : at + tile, :] * jnp.asarray(DH**-0.5, BF16)
        sums, totals = [], []
        for head in range(2):
            edge = jnp.where(ahead, NEGATIVE, nt(q, keys[head][at : at + tile]))
            top = jnp.max(edge, -1, keepdims=True)
            if at:
                before = nt(q, keys[head][:at])
                top = jnp.maximum(top, jnp.max(before, -1, keepdims=True))
            mixed = nn(jnp.exp(edge - top).astype(BF16), values[head][at : at + tile])
            if at:
                mixed = mixed + nn(jnp.exp(before - top).astype(BF16), values[head][:at])
            weight = mixed[:, DH : DH + 1] if head == 0 else mixed[:, 0:1]
            sums.append(mixed / weight)
            totals.append(top + jnp.log(weight))
        mix_ref[at : at + tile, :] = jnp.where(low, sums[0], sums[1]).astype(BF16)
        columns = jnp.where(low, totals[0], totals[1]).T
        total_ref[0, 0:1, at : at + tile] = columns[0:1]
        total_ref[0, 1:2, at : at + tile] = columns[DH : DH + 1]


def self_forward(q, k, v):
    rows, width = q.shape
    return pl.pallas_call(
        functools.partial(self_forward_kernel, min(rows, 256)),
        grid=(width // LANES,),
        in_specs=[pl.BlockSpec((rows, LANES), lambda pair: (0, pair))] * 3,
        out_specs=[
            pl.BlockSpec((rows, LANES), lambda pair: (0, pair)),
            pl.BlockSpec((1, 2, rows), lambda pair: (pair, 0, 0)),
        ],
        out_shape=[
            jax.ShapeDtypeStruct((rows, width), BF16),
            jax.ShapeDtypeStruct((width // LANES, 2, rows), F32),
        ],
        compiler_params=pltpu.CompilerParams(vmem_limit_bytes=VMEM_LIMIT),
        cost_estimate=pl.CostEstimate(flops=2 * rows * rows * width, bytes_accessed=8 * rows * width, transcendentals=0),
        name="self_forward",
    )(q, k, v)


def self_backward_kernel(tile, qkv_ref, grad_ref, mix_ref, total_ref, out_ref):
    rows = qkv_ref.shape[0]
    tiles = rows // tile
    low_all = low_half((rows, LANES))
    low = low_half((tile, LANES))
    q, grad = qkv_ref[:, :LANES] * jnp.asarray(DH**-0.5, BF16), grad_ref[...]
    zero = jnp.zeros_like(q)
    q_only = [pick(low_all, head, q, zero) for head in range(2)]
    g_only = [pick(low_all, head, grad, zero) for head in range(2)]
    inner = grad.astype(F32) * mix_ref[...].astype(F32)
    mine = lax.broadcasted_iota(jnp.int32, (8, LANES), 1) < DH
    ones = lax.broadcasted_iota(jnp.int32, (8, LANES), 0) == jnp.where(mine, 0, 1)
    inners = lax.dot_general(
        ones.astype(F32), inner, (((1,), (1,)), ((), ())), precision=lax.Precision.HIGHEST, preferred_element_type=F32
    )
    behind = lax.broadcasted_iota(jnp.int32, (tile, tile), 0) > lax.broadcasted_iota(jnp.int32, (tile, tile), 1)
    dq = [None] * tiles
    for i in range(tiles):
        part = slice(i * tile, (i + 1) * tile)
        k, v = qkv_ref[part, LANES : 2 * LANES], qkv_ref[part, 2 * LANES :]
        dk = dv = None
        for head in range(2):
            k_only = pick(low, head, k, jnp.zeros_like(k))
            v_only = pick(low, head, v, jnp.zeros_like(v))
            for j in range(i, tiles):
                at = slice(j * tile, (j + 1) * tile)
                scores = nt(k_only, q[at]) - total_ref[0, head : head + 1, at]
                if i == j:
                    scores = jnp.where(behind, NEGATIVE, scores)
                prob = jnp.exp(scores)
                prob_grad = nt(v_only, grad[at])
                score_grad = (prob * (prob_grad - inners[head : head + 1, at])).astype(BF16)
                dv_part = nn(prob.astype(BF16), g_only[head][at])
                dk_part = nn(score_grad, q_only[head][at])
                dq_part = tn(score_grad, k_only)
                dv = dv_part if dv is None else dv + dv_part
                dk = dk_part if dk is None else dk + dk_part
                dq[j] = dq_part if dq[j] is None else dq[j] + dq_part
        out_ref[part, LANES : 2 * LANES] = dk.astype(BF16)
        out_ref[part, 2 * LANES :] = dv.astype(BF16)
    for i in range(tiles):
        out_ref[i * tile : (i + 1) * tile, :LANES] = (dq[i] * DH**-0.5).astype(BF16)


def self_backward(qkv, grad, mix, total):
    rows = qkv.shape[0]
    by_pair = pl.BlockSpec((rows, LANES), lambda pair: (0, pair))
    by_three = pl.BlockSpec((rows, 3 * LANES), lambda pair: (0, pair))
    return pl.pallas_call(
        functools.partial(self_backward_kernel, min(rows, 256)),
        grid=(grad.shape[1] // LANES,),
        in_specs=[by_three, by_pair, by_pair, pl.BlockSpec((1, 2, rows), lambda pair: (pair, 0, 0))],
        out_specs=by_three,
        out_shape=jax.ShapeDtypeStruct(qkv.shape, BF16),
        compiler_params=pltpu.CompilerParams(vmem_limit_bytes=VMEM_LIMIT),
        cost_estimate=pl.CostEstimate(flops=2 * rows * rows * LANES, bytes_accessed=8 * rows * LANES, transcendentals=0),
        name="self_backward",
    )(qkv, grad, mix, total)


def normalize(values):
    center = values - jnp.mean(values, -1, keepdims=True)
    scale = lax.rsqrt(jnp.mean(center * center, -1, keepdims=True) + EPSILON)
    return center * scale, scale


def norm_backward(unit, scale, gain, upstream):
    weighted = upstream * gain
    grad = weighted - jnp.mean(weighted, -1, keepdims=True) - unit * jnp.mean(weighted * unit, -1, keepdims=True)
    return grad * scale, jnp.sum(upstream * unit, 0), jnp.sum(upstream, 0)


def chunk_of(rows, index, size):
    return lax.dynamic_slice_in_dim(rows, index * size, size, 0)


def assemble(chunks):
    size, width = chunks[0][1].shape
    result = jnp.zeros((size * len(chunks), width), chunks[0][1].dtype)
    for index, rows in chunks:
        result = lax.dynamic_update_slice_in_dim(result, rows, index * size, 0)
    return result


class Places:
    def __init__(self):
        self.mp, self.dp = lax.axis_size("mp"), lax.axis_size("dp")
        self.chips = self.dp // 2
        self.x, self.d = lax.axis_index("mp"), lax.axis_index("dp")
        self.core, self.chip = self.d % 2, self.d // 2
        self.line = self.x * 2 + self.core
        self.shard, self.seq = self.line % self.mp, self.line // self.mp

    def send(self, values, target):
        pairs = []
        for chip in range(self.chips):
            for x in range(self.mp):
                for core in range(2):
                    to_chip, to_x, to_core = target(chip, x, core)
                    pair = ((chip * 2 + core) * self.mp + x, (to_chip * 2 + to_core) * self.mp + to_x)
                    if pair[0] != pair[1]:
                        pairs.append(pair)
        return lax.ppermute(values, ("dp", "mp"), pairs)

    def weight(self, values):
        def target(chip, x, core):
            line = x if core else self.mp + x
            return chip, line // 2, line % 2

        return self.send(values, target)

    def to_work(self, values):
        arrived = self.send(values, lambda chip, x, core: (chip, (core * self.mp + x) // 2, (core * self.mp + x) % 2))
        return jnp.where((self.shard == self.x) & (self.seq == self.core), values, arrived)

    def from_work(self, values):
        mp = self.mp
        arrived = self.send(values, lambda chip, x, core: (chip, (x * 2 + core) % mp, (x * 2 + core) // mp))
        return jnp.where((self.shard == self.x) & (self.seq == self.core), values, arrived)

    def to_partner(self, values):
        def target(chip, x, core):
            return chip, x, 1 - core if (x * 2 + 1 - core) // self.mp == core else core

        return self.send(values, target)

    def sequence(self, values):
        return jnp.where(self.core == self.seq, values, self.to_partner(values))

    def sequence_chunk(self, values):
        size = values.shape[0] // self.mp
        partner = (self.x * 2 + 1 - self.core) % self.mp
        arrived = self.to_partner(chunk_of(values, partner, size))
        return jnp.where(self.core == self.seq, chunk_of(values, self.shard, size), arrived)

    def sum_group(self, grads):
        groups = [
            [
                (chip * 2 + line % 2) * self.mp + line // 2
                for chip in range(self.chips)
                for line in (shard, self.mp + shard)
            ]
            for shard in range(self.mp)
        ]
        return lax.psum_scatter(grads, ("dp", "mp"), scatter_dimension=0, axis_index_groups=groups, tiled=True)

    def along(self, values, shift):
        def target(chip, x, core):
            line = x * 2 + core
            line = line // self.mp * self.mp + (line + shift) % self.mp
            return chip, line // 2, line % 2

        return self.send(values, target)

    def scatter_parts(self, product, lefts, kind=BF16):
        size = lefts[0].shape[0] // self.mp

        def part(by):
            return product(*(chunk_of(left, (self.shard + by) % self.mp, size) for left in lefts))

        return [self.along(part(by).astype(kind), by) for by in range(1, self.mp)], part(0)

    def scatter_sum(self, product, lefts, kind=BF16):
        arrived, own = self.scatter_parts(product, lefts, kind)
        return sum((rows.astype(F32) for rows in arrived), own)

    def gather(self, rows):
        chunks = [(self.shard, rows)]
        chunks += [((self.shard + by) % self.mp, self.along(rows, -by)) for by in range(1, self.mp)]
        return assemble(chunks)

    def spread(self, rows, kind):
        return assemble(self.spread_chunks(rows, kind))

    def spread_chunks(self, rows, kind):
        mp = self.mp
        chunks = []
        for turn in range(mp):

            def target(chip, x, core, turn=turn):
                line = x * 2 + core
                return chip, (line % mp - turn) % mp, line // mp

            mine = (self.seq == self.core) & ((self.shard - turn) % mp == self.x)
            arrived = jnp.where(mine, rows, self.send(rows, target))
            chunks.append(((self.x + turn) % mp, arrived.astype(kind)))
        return chunks

    def bits(self):
        return self.chips.bit_length() - 1

    def meet(self, values, bits):
        mp = self.mp

        def target(chip, x, core):
            for bit in bits:
                if bit == "sequence":
                    line = (x * 2 + core + mp) % (2 * mp)
                    x, core = line // 2, line % 2
                elif bit == "core":
                    core = 1 - core
                elif isinstance(bit, tuple):
                    x = x ^ (1 << bit[1])
                else:
                    chip = chip ^ (1 << bit)
            return chip, x, core

        return self.send(values, target)

    def my_bit(self, bit):
        if bit == "sequence":
            return self.seq
        if bit == "core":
            return self.core
        return (self.chip >> bit) & 1


class Scatter:
    def __init__(self, at, values, stages, last):
        bits = at.bits()
        self.at, self.order, self.axes = at, [stage for stage in stages if stage], list(range(bits))[::-1] + [last]
        self.values = values.reshape((2,) * (bits + 1) + (values.shape[0] // 2 ** (bits + 1), values.shape[1]))
        self.arrived = None

    def pieces(self):
        stage = self.order.pop(0)
        if isinstance(stage[0], tuple):
            self.sets = [tuple(stage)]
            return self.values, [self.values]
        sets = [()]
        for bit in stage:
            sets += [some + (bit,) for some in sets]
        axes = self.axes
        self.axes = [axis for axis in axes if axis not in stage]
        self.sets = sets[1:]
        size = [1 if axis in stage else 2 for axis in axes] + list(self.values.shape[-2:])
        shape = [2] * len(self.axes) + list(self.values.shape[-2:])
        parts = []
        for some in sets:
            start = [0] * len(size)
            for bit in stage:
                mine = self.at.my_bit(bit)
                start[axes.index(bit)] = 1 - mine if bit in some else mine
            parts.append(lax.dynamic_slice(self.values, start, size).reshape(shape))
        return parts[0], parts[1:]

    def prepare(self):
        self.kept, sent = self.pieces()
        self.sent = [part.astype(BF16) for part in sent]

    def start(self):
        self.arrived = [self.at.meet(part, some) for part, some in zip(self.sent, self.sets)]

    def finish(self):
        self.values = sum((part.astype(F32) for part in self.arrived), self.kept.astype(F32))
        self.arrived = None


def launch(chains, *values):
    moving = []
    for chain in chains:
        if chain.arrived is not None:
            chain.finish()
        if chain.order:
            chain.prepare()
            moving.append(chain)
    values, sents = lax.optimization_barrier((values, [chain.sent for chain in moving]))
    for chain, sent in zip(moving, sents):
        chain.sent = sent
        chain.start()
    return values[0] if len(values) == 1 else values


def settle(chains, *values):
    moving = [chain for chain in chains if chain.arrived is not None]
    values, arrivals = lax.optimization_barrier((values, [chain.arrived for chain in moving]))
    for chain, arrived in zip(moving, arrivals):
        chain.arrived = arrived
    return values[0] if len(values) == 1 else values


def per_device(
    decoder_layer_input,
    encoder_states,
    retrieved_owner,
    retrieved_block,
    self_query,
    self_attention_key,
    self_value,
    self_out,
    gain_first,
    shift_first,
    cross_query,
    cross_key,
    cross_value,
    cross_out,
    gain_second,
    shift_second,
    hidden_up,
    hidden_down,
    gain_third,
    shift_third,
    out_grad,
):
    at = Places()
    score_scale = jnp.asarray(DH**-0.5, BF16)
    seq_len, width = decoder_layer_input.shape
    shard_width = self_query.shape[1]
    chunk = seq_len // at.mp
    blocks_here = encoder_states.shape[0] // BLOCK
    chip_bits = list(range(at.bits()))
    x_bits = [("x", i) for i in range(at.mp.bit_length() - 1)]
    tie = lambda *values: lax.optimization_barrier(values)

    def even(weight):
        extra = -weight.shape[1] % LANES
        return jnp.pad(weight, ((0, 0), (0, extra))) if extra else weight

    def even_rows(weight):
        extra = -weight.shape[0] % LANES
        return jnp.pad(weight, ((0, extra), (0, 0))) if extra else weight

    def interleave(*weights):
        weights = [even(weight) for weight in weights]
        return jnp.concatenate(
            [w[:, i : i + LANES] for i in range(0, weights[0].shape[1], LANES) for w in weights], 1
        )

    def separate(values, count):
        size = values.shape[1] // count
        return [
            jnp.concatenate([values[:, (i * count + j) * LANES :][:, :LANES] for i in range(size // LANES)], 1)[
                :, :shard_width
            ]
            for j in range(count)
        ]

    store = lax.all_gather(encoder_states, "dp", axis=0, tiled=True)
    keys = store.shape[0]

    w_out, w_cross_query = at.weight(self_out), at.weight(cross_query)
    mix_first, total_first = self_forward(
        *(nn(decoder_layer_input, even(w)).astype(BF16) for w in (self_query, self_attention_key, self_value))
    )
    mix_first, w_out, w_cross_query, own_rows, next_key, next_value, owner, block = tie(
        mix_first,
        w_out,
        w_cross_query,
        decoder_layer_input,
        cross_key,
        cross_value,
        retrieved_owner,
        retrieved_block,
    )
    w_out, w_cross_query = even_rows(w_out), even(w_cross_query)
    self_mix = at.to_work(mix_first)
    own_rows = at.sequence_chunk(own_rows).astype(F32)
    names = at.sequence(owner * blocks_here + block)
    w_cross_key, w_cross_value = at.weight(next_key), at.weight(next_value)

    self_mix, own_rows, names, next_out = tie(self_mix, own_rows, names, cross_out)
    w_cross_out = at.weight(next_out)
    first_in = own_rows + at.scatter_sum(lambda rows: nn(rows, w_out), [self_mix], F32)
    first_unit, first_scale = normalize(first_in)
    first = first_unit * gain_first + shift_first
    first_low = at.gather(first.astype(BF16))
    first_low, w_cross_key, w_cross_value = tie(first_low, w_cross_key, w_cross_value)
    w_store = interleave(w_cross_key, w_cross_value)
    queries = nn(first_low, w_cross_query).astype(BF16) * score_scale
    queries, store, w_store, w_cross_out, next_up, next_down, rows_grad, rows_in = tie(
        queries, store, w_store, w_cross_out, hidden_up, hidden_down, out_grad, decoder_layer_input
    )
    w_up, w_down = at.weight(next_up), at.weight(next_down)
    rows_grad = at.sequence_chunk(rows_grad)
    rows_in = at.sequence(rows_in)
    store_kv = nn(store, w_store).astype(BF16)
    terms = key_terms(keys, keys // BLOCK + 3 > DH)
    cross_sum, cross_mix, cross_total, barred = cross_forward(queries, names, store_kv, terms)
    cross_mix, w_up, w_down, rows_grad, rows_in = tie(cross_mix, w_up, w_down, rows_grad, rows_in)
    w_cross_out, rows_grad = even_rows(w_cross_out), rows_grad.astype(F32)
    second_in = first + at.scatter_sum(lambda rows: nn(rows, w_cross_out), [cross_mix], F32)
    second_unit, second_scale = normalize(second_in)
    second = second_unit * gain_second + shift_second
    second_low = at.gather(second.astype(BF16))
    hidden_pre = nn(second_low, w_up)
    bell = 0.5 + 0.5 * lax.erf(hidden_pre * 0.5**0.5)
    hidden_act = (hidden_pre * bell).astype(BF16)
    slope = bell + hidden_pre * jnp.exp(-0.5 * hidden_pre * hidden_pre) * 0.3989422804014327
    third_in = second + at.scatter_sum(lambda rows: nn(rows, w_down), [hidden_act])
    third_unit, third_scale = normalize(third_in)
    layer_out = (third_unit * gain_third + shift_third).astype(BF16)

    res3_grad, gain_third_grad, shift_third_grad = norm_backward(third_unit, third_scale, gain_third, rows_grad)
    ffn_grad = at.gather(res3_grad.astype(BF16))
    pre_grad = (slope * nt(ffn_grad, w_down)).astype(BF16)
    second_grad = res3_grad + at.scatter_sum(lambda rows: nt(rows, w_up), [pre_grad])
    res2_grad, gain_second_grad, shift_second_grad = norm_backward(
        second_unit, second_scale, gain_second, second_grad
    )
    cross_grad = at.gather(res2_grad.astype(BF16))
    mix_grad = nt(cross_grad, w_cross_out).astype(BF16)
    early = jnp.concatenate(
        [
            tn(ffn_grad, hidden_act).astype(BF16),
            tn(second_low, pre_grad).astype(BF16),
            tn(cross_grad, cross_mix).astype(BF16),
        ],
        1,
    )
    w_triple = interleave(self_query, self_attention_key, self_value)
    mix_grad, early, layer_out, w_triple, self_total = tie(mix_grad, early, layer_out, w_triple, total_first)
    early = at.sum_group(early)
    layer_chunks = at.spread_chunks(layer_out, BF16)
    w_triple = at.weight(w_triple)
    self_total = at.to_work(self_total)
    queries_grad, kv_grad = cross_backward(
        queries, barred, store_kv, terms, 0, keys, mix_grad, cross_sum, cross_total, (), True
    )
    queries_grad, kv_grad, layer_chunks, w_triple, self_total = tie(
        queries_grad, kv_grad, layer_chunks, w_triple, self_total
    )
    encoder = Scatter(at, kv_grad, [["core"], chip_bits[:2], chip_bits[2:]], "core")
    kept, sent = encoder.pieces()
    shape = kept.shape[:-1] + (width,)
    encoder.sent = [nt(part.reshape(-1, part.shape[-1]), w_store).astype(BF16).reshape(shape) for part in sent]
    encoder.start()
    encoder.kept = nt(kept.reshape(-1, kept.shape[-1]), w_store).reshape(shape)
    first_grad = res2_grad + at.scatter_sum(lambda rows: nt(rows, w_cross_query), [queries_grad])
    res1_grad, gain_first_grad, shift_first_grad = norm_backward(first_unit, first_scale, gain_first, first_grad)
    res1_grad = launch([encoder], res1_grad)
    self_grad = at.gather(res1_grad.astype(BF16))
    side = Scatter(
        at,
        jnp.concatenate(
            [
                tn(store, kv_grad).astype(BF16),
                tn(first_low, queries_grad).astype(BF16),
                tn(self_grad, self_mix).astype(BF16),
            ],
            1,
        ),
        [["sequence"], chip_bits[:2], chip_bits[2:]],
        "sequence",
    )
    smix_grad = nt(self_grad, w_out).astype(BF16)
    self_qkv = nn(rows_in, w_triple).astype(BF16)
    smix_grad = launch([side], smix_grad)
    norms = jnp.stack(
        [
            gain_first_grad,
            shift_first_grad,
            gain_second_grad,
            shift_second_grad,
            gain_third_grad,
            shift_third_grad,
        ],
        0,
    )
    norms = sum((at.along(norms, by) for by in range(1, at.mp)), norms)
    norms = tn(norms.astype(BF16), jnp.eye(6, LANES, dtype=BF16)).astype(BF16)
    triple = self_backward(self_qkv, smix_grad, self_mix, self_total)
    triple, early = settle([encoder, side], triple, early)
    arrived, own = at.scatter_parts(lambda rows: nt(rows, w_triple), [triple])
    last = jnp.concatenate([tn(rows_in, triple).astype(BF16), norms], 1)
    last = Scatter(at, last, [chip_bits[:1], ["sequence"], chip_bits[1:]], "sequence")
    input_rows = (sum((rows.astype(F32) for rows in arrived), own) + res1_grad).astype(BF16)
    encoder.order += [[bit] for bit in x_bits]
    chains = [encoder, side, last]
    input_rows = launch(chains, input_rows)
    input_chunks = at.spread_chunks(input_rows, F32)
    input_chunks = settle(chains, input_chunks)
    input_chunks = launch(chains, input_chunks)
    input_grad, layer_out = assemble(input_chunks), assemble(layer_chunks)
    while any(chain.order or chain.arrived is not None for chain in chains):
        settle(chains)
        launch(chains)

    encoder_grad = encoder.values
    ends = [chain.values.astype(BF16) for chain in (last, side)]
    gathered = at.from_work(jnp.concatenate(ends + [early.astype(BF16)], 1)).astype(F32)
    cuts = np.cumsum([0] + [end.shape[1] for end in ends])
    last, side, early = gathered[:, : cuts[1]], gathered[:, cuts[1] : cuts[2]], gathered[:, cuts[2] :]
    part_width = triple.shape[1] // 3
    norms = last[:, 3 * part_width :][:, :6].T
    self_query_grad, self_key_grad, self_value_grad = separate(last[:, : 3 * part_width], 3)
    cross_key_grad, cross_value_grad = separate(side[:, : 2 * part_width], 2)
    cross_query_grad = side[:, 2 * part_width : 2 * part_width + shard_width]
    self_out_grad = side[:, 3 * part_width : 3 * part_width + shard_width]
    hidden = hidden_act.shape[1]
    hidden_down_grad, hidden_up_grad = early[:, :hidden], early[:, hidden : 2 * hidden]
    cross_out_grad = early[:, 2 * hidden : 2 * hidden + shard_width]
    share = width // at.dp
    return (
        layer_out,
        input_grad,
        encoder_grad,
        self_query_grad,
        self_key_grad,
        self_value_grad,
        self_out_grad.T,
        norms[0],
        norms[1],
        cross_query_grad,
        cross_key_grad,
        cross_value_grad,
        cross_out_grad.T,
        norms[2],
        norms[3],
        hidden_up_grad,
        hidden_down_grad.T,
        norms[4],
        norms[5],
    )


def solution(mesh):
    rows, columns, parts, copied = P("dp", None), P(None, "mp"), P("mp", None), P()
    return jax.shard_map(
        per_device,
        mesh=mesh,
        in_specs=(rows,) * 4
        + (columns,) * 3
        + (parts, copied, copied)
        + (columns,) * 3
        + (parts, copied, copied)
        + (columns, parts, copied, copied, rows),
        out_specs=(rows,) * 3
        + (P("dp", "mp"),) * 3
        + (P("mp", "dp"), P("dp"), P("dp"))
        + (P("dp", "mp"),) * 3
        + (P("mp", "dp"), P("dp"), P("dp"))
        + (P("dp", "mp"), P("mp", "dp"), P("dp"), P("dp")),
        check_vma=False,
    )
```

```python
import functools

import jax
import jax.numpy as jnp
import numpy as np
from jax import lax
from jax.experimental import pallas as pl
from jax.experimental.pallas import tpu as pltpu
from jax.sharding import PartitionSpec as P

DH = 64
BLOCK = 128
LANES = 128
EPSILON = 1e-05
NEGATIVE = -1e30
VMEM_LIMIT = 56 * 1024 * 1024
BF16, F32 = jnp.bfloat16, jnp.float32


def nn(left, right):
    return lax.dot_general(left, right, (((1,), (0,)), ((), ())), preferred_element_type=F32)


def nt(left, right):
    return lax.dot_general(left, right, (((1,), (1,)), ((), ())), preferred_element_type=F32)


def tn(left, right):
    return lax.dot_general(left, right, (((0,), (0,)), ((), ())), preferred_element_type=F32)


def low_half(shape):
    return lax.broadcasted_iota(jnp.int32, shape, 1) < DH


def pick(low, head, own, other):
    return jnp.where(low, own, other) if head == 0 else jnp.where(low, other, own)


def split_three(values):
    high = values.astype(BF16)
    rest = values - high.astype(F32)
    middle = rest.astype(BF16)
    last = (rest - middle.astype(F32)).astype(BF16)
    return high.astype(F32), middle.astype(F32), last.astype(F32)


def widen(base, extra):
    return base if extra is None else jnp.concatenate([base, extra], 1)


def barred_lanes(names, blocks, period):
    shape = (names.shape[0], LANES)
    lane = lax.broadcasted_iota(jnp.int32, shape, 1) % period
    found = lane >= blocks
    for request in range(names.shape[1]):
        found = found | (names[:, request : request + 1] == lane)
    return jnp.where(found, 0.0, NEGATIVE)


def key_terms(keys, wide):
    blocks = keys // BLOCK
    free = 0 if wide else blocks
    block, lane = np.arange(keys)[:, None] // BLOCK, np.arange(LANES)[None, :]
    ones = (lane % DH >= free) & (lane % DH < free + 3)
    if wide:
        terms = np.concatenate([np.broadcast_to(ones, (keys, LANES)), block == lane], 1)
    else:
        terms = ones | (block == lane % DH)
    return jnp.asarray(terms.astype(np.float32), BF16)


def cross_forward_kernel(
    chunk, blocks, wide, q_ref, names_ref, kv_ref, terms_ref, sum_ref, mix_ref, total_ref, barred_ref, k_wide, v_wide, s_ref
):
    keys, rows = kv_ref.shape[0], q_ref.shape[0]

    @pl.when(pl.program_id(1) == 0)
    def _():
        for at in range(0, keys, chunk):
            part = slice(at, at + chunk)
            low = low_half((chunk, LANES))
            k, v = kv_ref[part, :LANES], kv_ref[part, LANES:]
            terms = terms_ref[part, :]
            for head in range(2):
                k_wide[head, part, :] = widen(
                    pick(low, head, k, terms[:, :LANES]), terms[:, LANES:] if wide else None
                )
                v_wide[head, part, :] = pick(low, head, v, jnp.ones_like(v))

    size = s_ref.shape[1]
    low = low_half((size, LANES))
    here = pl.ds(pl.multiple_of(pl.program_id(1) * rows, rows), rows)

    @pl.when(pl.program_id(0) == 0)
    def _():
        barred_ref[here, :] = barred_lanes(names_ref[...], blocks, LANES if wide else DH).astype(BF16)

    units = [(head, at) for at in range(0, rows, size) for head in range(2)]

    def begin(unit):
        head, at = units[unit]
        q = q_ref[at : at + size, :]
        barred = barred_ref[pl.ds(pl.multiple_of(pl.program_id(1) * rows + at, size), size), :]
        return widen(pick(low, head, q, jnp.zeros_like(q)), barred) if wide else pick(low, head, q, barred)

    def score(unit, q_wide, part, peak):
        scores = nt(q_wide, k_wide[units[unit][0], part, :])
        s_ref[unit % 2, :, part] = scores
        for lane in range(0, chunk, LANES):
            peak = jnp.maximum(peak, scores[:, lane : lane + LANES])
        return peak

    parts = [slice(at, at + chunk) for at in range(0, keys, chunk)]
    nothing = jnp.full((size, LANES), -jnp.inf, F32)
    peak, q_wide = nothing, begin(0)
    for part in parts:
        peak = score(0, q_wide, part, peak)
    done = []
    for unit, (head, at) in enumerate(units):
        top = jnp.max(peak, -1, keepdims=True)
        more = unit + 1 < len(units)
        peak, q_wide = nothing, begin(unit + 1) if more else None
        mixed = jnp.zeros((size, LANES), F32)
        for part in parts:
            if more:
                peak = score(unit + 1, q_wide, part, peak)
            prob = jnp.exp(s_ref[unit % 2, :, part] - top).astype(BF16)
            mixed = mixed + nn(prob, v_wide[head, part, :])
        weight = mixed[:, DH : DH + 1] if head == 0 else mixed[:, 0:1]
        done.append((mixed / weight, top + jnp.log(weight)))
        if head == 1:
            sums = jnp.where(low, done[-2][0], done[-1][0])
            sum_ref[at : at + size, :] = sums
            mix_ref[at : at + size, :] = sums.astype(BF16)
            total_ref[at : at + size, :] = jnp.where(low, done[-2][1], done[-1][1])


def cross_forward(q, names, kv, terms):
    rows, width = q.shape
    keys = kv.shape[0]
    blocks = keys // BLOCK
    wide = blocks + 3 > DH
    tile, size = (rows, min(rows, 256)) if keys <= 4096 else (64, 64)
    chunk = min(keys, 512)
    by_tile = pl.BlockSpec((tile, LANES), lambda pair, i: (i, pair))
    return pl.pallas_call(
        functools.partial(cross_forward_kernel, chunk, blocks, wide),
        grid=(width // LANES, rows // tile),
        in_specs=[
            by_tile,
            pl.BlockSpec((tile, names.shape[1]), lambda pair, i: (i, 0)),
            pl.BlockSpec((keys, 2 * LANES), lambda pair, i: (0, pair)),
            pl.BlockSpec(terms.shape, lambda pair, i: (0, 0)),
        ],
        out_specs=[by_tile] * 3 + [pl.BlockSpec((rows, LANES), lambda pair, i: (0, 0))],
        out_shape=[
            jax.ShapeDtypeStruct((rows, width), F32),
            jax.ShapeDtypeStruct((rows, width), BF16),
            jax.ShapeDtypeStruct((rows, width), F32),
            jax.ShapeDtypeStruct((rows, LANES), BF16),
        ],
        scratch_shapes=[
            pltpu.VMEM((2, keys, 2 * LANES if wide else LANES), BF16),
            pltpu.VMEM((2, keys, LANES), BF16),
            pltpu.VMEM((2, size, keys), F32),
        ],
        compiler_params=pltpu.CompilerParams(vmem_limit_bytes=VMEM_LIMIT),
        cost_estimate=pl.CostEstimate(flops=2 * rows * keys * width, bytes_accessed=8 * keys * width, transcendentals=0),
        name="cross_forward",
    )(q, names, kv, terms)


def cross_backward_kernel(blocks, wide, merge, *refs):
    q_ref, barred_ref, kv_ref, terms_ref, grad_ref, sum_ref, total_ref = refs[:7]
    refs = refs[7:]
    if merge:
        old_ref, refs = refs[0], refs[1:]
    dq_ref, dkv_ref, q_wide, q_only, g_wide, g_only, dq_sum = refs
    rows, chunk = q_ref.shape[0], kv_ref.shape[0]
    step = pl.program_id(1)
    free = 0 if wide else blocks

    @pl.when(step == 0)
    def _():
        size = min(rows, 256)
        low = low_half((size, LANES))
        lane = lax.broadcasted_iota(jnp.int32, (size, LANES), 1) % DH
        zero = jnp.zeros((size, LANES), F32)
        for at in range(0, rows, size):
            part = slice(at, at + size)
            q, grad = q_ref[part, :].astype(F32), grad_ref[part, :].astype(F32)
            total = total_ref[part, :]
            high, middle, last = split_three(jnp.where(low, total[:, DH : DH + 1], total[:, 0:1]))
            barred = barred_ref[part, :].astype(F32)
            extra = zero if wide else barred
            extra = jnp.where(lane == free, -high, extra)
            extra = jnp.where(lane == free + 1, -middle, extra)
            extra = jnp.where(lane == free + 2, -last, extra)
            inner = grad * sum_ref[part, :]
            inner_0 = jnp.sum(jnp.where(low, inner, zero), -1, keepdims=True)
            inner_1 = jnp.sum(jnp.where(low, zero, inner), -1, keepdims=True)
            high, middle, last = split_three(jnp.where(low, inner_1, inner_0))
            less = jnp.where(lane == 0, -high, jnp.where(lane == 1, -middle, jnp.where(lane == 2, -last, zero)))
            for head in range(2):
                q_wide[head, part, :] = widen(pick(low, head, q, extra), barred if wide else None).astype(BF16)
                q_only[head, part, :] = pick(low, head, q, zero).astype(BF16)
                g_wide[head, part, :] = pick(low, head, grad, less).astype(BF16)
                g_only[head, part, :] = pick(low, head, grad, zero).astype(BF16)
        dq_sum[...] = jnp.zeros_like(dq_sum)

    low = low_half((chunk, LANES))
    k, v = kv_ref[:, :LANES], kv_ref[:, LANES:]
    terms, own_terms = terms_ref[:, :LANES], terms_ref[:, LANES:] if wide else None
    dk = dv = None
    for head in range(2):
        prob = jnp.exp(nt(widen(pick(low, head, k, terms), own_terms), q_wide[head]))
        prob_grad = nt(pick(low, head, v, jnp.ones_like(v)), g_wide[head])
        score_grad = (prob * prob_grad).astype(BF16)
        dv_head, dk_head = nn(prob.astype(BF16), g_only[head]), nn(score_grad, q_only[head])
        dv = dv_head if dv is None else dv + dv_head
        dk = dk_head if dk is None else dk + dk_head
        dq_sum[...] += tn(pick(low, head, k, jnp.zeros_like(k)), score_grad)
    dkv_ref[:, :LANES] = dk.astype(dkv_ref.dtype)
    dkv_ref[:, LANES:] = dv.astype(dkv_ref.dtype)

    @pl.when(step == pl.num_programs(1) - 1)
    def _():
        dq = dq_sum[...].T * DH**-0.5
        if merge:
            dq = dq + old_ref[...]
        dq_ref[...] = dq.astype(dq_ref.dtype)


def cross_backward(q, barred, kv, terms, start, keys, grad, cross_sum, total, old, final):
    rows, width = q.shape
    blocks = kv.shape[0] // BLOCK
    wide = blocks + 3 > DH
    chunk = min(keys, 512 if wide else 1024)
    by_pair = pl.BlockSpec((rows, LANES), lambda pair, i: (0, pair))
    return pl.pallas_call(
        functools.partial(cross_backward_kernel, blocks, wide, bool(old)),
        grid=(width // LANES, keys // chunk),
        in_specs=[
            by_pair,
            pl.BlockSpec((rows, LANES), lambda pair, i: (0, 0)),
            pl.BlockSpec((chunk, 2 * LANES), lambda pair, i: (i + start // chunk, pair)),
            pl.BlockSpec((chunk, terms.shape[1]), lambda pair, i: (i + start // chunk, 0)),
        ]
        + [by_pair] * (3 + len(old)),
        out_specs=[by_pair, pl.BlockSpec((chunk, 2 * LANES), lambda pair, i: (i, pair))],
        out_shape=[
            jax.ShapeDtypeStruct((rows, width), BF16 if final else F32),
            jax.ShapeDtypeStruct((keys, 2 * width), BF16),
        ],
        scratch_shapes=[pltpu.VMEM((2, rows, 2 * LANES if wide else LANES), BF16)]
        + [pltpu.VMEM((2, rows, LANES), BF16)] * 3
        + [pltpu.VMEM((LANES, rows), F32)],
        compiler_params=pltpu.CompilerParams(vmem_limit_bytes=VMEM_LIMIT),
        cost_estimate=pl.CostEstimate(flops=2 * rows * keys * width, bytes_accessed=8 * keys * width, transcendentals=0),
        name="cross_backward",
    )(q, barred, kv, terms, grad, cross_sum, total, *old)


def self_forward_kernel(tile, q_ref, k_ref, v_ref, mix_ref, total_ref):
    rows = q_ref.shape[0]
    low_all = low_half((rows, LANES))
    low = low_half((tile, LANES))
    k, v = k_ref[...], v_ref[...]
    zero = jnp.zeros_like(k)
    keys = [pick(low_all, head, k, zero) for head in range(2)]
    values = [pick(low_all, head, v, jnp.ones_like(v)) for head in range(2)]
    ahead = lax.broadcasted_iota(jnp.int32, (tile, tile), 1) > lax.broadcasted_iota(jnp.int32, (tile, tile), 0)
    for at in range(0, rows, tile):
        q = q_ref[at : at + tile, :] * jnp.asarray(DH**-0.5, BF16)
        sums, totals = [], []
        for head in range(2):
            edge = jnp.where(ahead, NEGATIVE, nt(q, keys[head][at : at + tile]))
            top = jnp.max(edge, -1, keepdims=True)
            if at:
                before = nt(q, keys[head][:at])
                top = jnp.maximum(top, jnp.max(before, -1, keepdims=True))
            mixed = nn(jnp.exp(edge - top).astype(BF16), values[head][at : at + tile])
            if at:
                mixed = mixed + nn(jnp.exp(before - top).astype(BF16), values[head][:at])
            weight = mixed[:, DH : DH + 1] if head == 0 else mixed[:, 0:1]
            sums.append(mixed / weight)
            totals.append(top + jnp.log(weight))
        mix_ref[at : at + tile, :] = jnp.where(low, sums[0], sums[1]).astype(BF16)
        columns = jnp.where(low, totals[0], totals[1]).T
        total_ref[0, 0:1, at : at + tile] = columns[0:1]
        total_ref[0, 1:2, at : at + tile] = columns[DH : DH + 1]


def self_forward(q, k, v):
    rows, width = q.shape
    return pl.pallas_call(
        functools.partial(self_forward_kernel, min(rows, 512)),
        grid=(width // LANES,),
        in_specs=[pl.BlockSpec((rows, LANES), lambda pair: (0, pair))] * 3,
        out_specs=[
            pl.BlockSpec((rows, LANES), lambda pair: (0, pair)),
            pl.BlockSpec((1, 2, rows), lambda pair: (pair, 0, 0)),
        ],
        out_shape=[
            jax.ShapeDtypeStruct((rows, width), BF16),
            jax.ShapeDtypeStruct((width // LANES, 2, rows), F32),
        ],
        compiler_params=pltpu.CompilerParams(vmem_limit_bytes=VMEM_LIMIT),
        cost_estimate=pl.CostEstimate(flops=2 * rows * rows * width, bytes_accessed=8 * rows * width, transcendentals=0),
        name="self_forward",
    )(q, k, v)


def self_backward_kernel(tile, qkv_ref, grad_ref, mix_ref, total_ref, out_ref):
    rows = qkv_ref.shape[0]
    tiles = rows // tile
    low_all = low_half((rows, LANES))
    low = low_half((tile, LANES))
    q, grad = qkv_ref[:, :LANES] * jnp.asarray(DH**-0.5, BF16), grad_ref[...]
    zero = jnp.zeros_like(q)
    q_only = [pick(low_all, head, q, zero) for head in range(2)]
    g_only = [pick(low_all, head, grad, zero) for head in range(2)]
    inner = grad.astype(F32) * mix_ref[...].astype(F32)
    mine = lax.broadcasted_iota(jnp.int32, (8, LANES), 1) < DH
    ones = lax.broadcasted_iota(jnp.int32, (8, LANES), 0) == jnp.where(mine, 0, 1)
    inners = lax.dot_general(
        ones.astype(F32), inner, (((1,), (1,)), ((), ())), precision=lax.Precision.HIGHEST, preferred_element_type=F32
    )
    behind = lax.broadcasted_iota(jnp.int32, (tile, tile), 0) > lax.broadcasted_iota(jnp.int32, (tile, tile), 1)
    dq = [None] * tiles
    for i in range(tiles):
        part = slice(i * tile, (i + 1) * tile)
        k, v = qkv_ref[part, LANES : 2 * LANES], qkv_ref[part, 2 * LANES :]
        dk = dv = None
        for head in range(2):
            k_only = pick(low, head, k, jnp.zeros_like(k))
            v_only = pick(low, head, v, jnp.zeros_like(v))
            for j in range(i, tiles):
                at = slice(j * tile, (j + 1) * tile)
                scores = nt(k_only, q[at]) - total_ref[0, head : head + 1, at]
                if i == j:
                    scores = jnp.where(behind, NEGATIVE, scores)
                prob = jnp.exp(scores)
                prob_grad = nt(v_only, grad[at])
                score_grad = (prob * (prob_grad - inners[head : head + 1, at])).astype(BF16)
                dv_part = nn(prob.astype(BF16), g_only[head][at])
                dk_part = nn(score_grad, q_only[head][at])
                dq_part = tn(score_grad, k_only)
                dv = dv_part if dv is None else dv + dv_part
                dk = dk_part if dk is None else dk + dk_part
                dq[j] = dq_part if dq[j] is None else dq[j] + dq_part
        out_ref[part, LANES : 2 * LANES] = dk.astype(BF16)
        out_ref[part, 2 * LANES :] = dv.astype(BF16)
    for i in range(tiles):
        out_ref[i * tile : (i + 1) * tile, :LANES] = (dq[i] * DH**-0.5).astype(BF16)


def self_backward(qkv, grad, mix, total):
    rows = qkv.shape[0]
    by_pair = pl.BlockSpec((rows, LANES), lambda pair: (0, pair))
    by_three = pl.BlockSpec((rows, 3 * LANES), lambda pair: (0, pair))
    return pl.pallas_call(
        functools.partial(self_backward_kernel, min(rows, 512)),
        grid=(grad.shape[1] // LANES,),
        in_specs=[by_three, by_pair, by_pair, pl.BlockSpec((1, 2, rows), lambda pair: (pair, 0, 0))],
        out_specs=by_three,
        out_shape=jax.ShapeDtypeStruct(qkv.shape, BF16),
        compiler_params=pltpu.CompilerParams(vmem_limit_bytes=VMEM_LIMIT),
        cost_estimate=pl.CostEstimate(flops=2 * rows * rows * LANES, bytes_accessed=8 * rows * LANES, transcendentals=0),
        name="self_backward",
    )(qkv, grad, mix, total)


def normalize(values):
    center = values - jnp.mean(values, -1, keepdims=True)
    scale = lax.rsqrt(jnp.mean(center * center, -1, keepdims=True) + EPSILON)
    return center * scale, scale


def norm_backward(unit, scale, gain, upstream):
    weighted = upstream * gain
    grad = weighted - jnp.mean(weighted, -1, keepdims=True) - unit * jnp.mean(weighted * unit, -1, keepdims=True)
    return grad * scale, jnp.sum(upstream * unit, 0), jnp.sum(upstream, 0)


def chunk_of(rows, index, size):
    return lax.dynamic_slice_in_dim(rows, index * size, size, 0)


def assemble(chunks):
    size, width = chunks[0][1].shape
    result = jnp.zeros((size * len(chunks), width), chunks[0][1].dtype)
    for index, rows in chunks:
        result = lax.dynamic_update_slice_in_dim(result, rows, index * size, 0)
    return result


class Places:
    def __init__(self):
        self.mp, self.dp = lax.axis_size("mp"), lax.axis_size("dp")
        self.chips = self.dp // 2
        self.x, self.d = lax.axis_index("mp"), lax.axis_index("dp")
        self.core, self.chip = self.d % 2, self.d // 2
        self.line = self.x * 2 + self.core
        self.shard, self.seq = self.line % self.mp, self.line // self.mp

    def send(self, values, target):
        pairs = []
        for chip in range(self.chips):
            for x in range(self.mp):
                for core in range(2):
                    to_chip, to_x, to_core = target(chip, x, core)
                    pair = ((chip * 2 + core) * self.mp + x, (to_chip * 2 + to_core) * self.mp + to_x)
                    if pair[0] != pair[1]:
                        pairs.append(pair)
        return lax.ppermute(values, ("dp", "mp"), pairs)

    def weight(self, values):
        def target(chip, x, core):
            line = x if core else self.mp + x
            return chip, line // 2, line % 2

        return self.send(values, target)

    def to_work(self, values):
        arrived = self.send(values, lambda chip, x, core: (chip, (core * self.mp + x) // 2, (core * self.mp + x) % 2))
        return jnp.where((self.shard == self.x) & (self.seq == self.core), values, arrived)

    def from_work(self, values):
        mp = self.mp
        arrived = self.send(values, lambda chip, x, core: (chip, (x * 2 + core) % mp, (x * 2 + core) // mp))
        return jnp.where((self.shard == self.x) & (self.seq == self.core), values, arrived)

    def to_partner(self, values):
        def target(chip, x, core):
            return chip, x, 1 - core if (x * 2 + 1 - core) // self.mp == core else core

        return self.send(values, target)

    def sequence(self, values):
        return jnp.where(self.core == self.seq, values, self.to_partner(values))

    def sequence_chunk(self, values):
        size = values.shape[0] // self.mp
        partner = (self.x * 2 + 1 - self.core) % self.mp
        arrived = self.to_partner(chunk_of(values, partner, size))
        return jnp.where(self.core == self.seq, chunk_of(values, self.shard, size), arrived)

    def sum_group(self, grads):
        groups = [
            [
                (chip * 2 + line % 2) * self.mp + line // 2
                for chip in range(self.chips)
                for line in (shard, self.mp + shard)
            ]
            for shard in range(self.mp)
        ]
        return lax.psum_scatter(grads, ("dp", "mp"), scatter_dimension=0, axis_index_groups=groups, tiled=True)

    def along(self, values, shift):
        def target(chip, x, core):
            line = x * 2 + core
            line = line // self.mp * self.mp + (line + shift) % self.mp
            return chip, line // 2, line % 2

        return self.send(values, target)

    def scatter_parts(self, product, lefts, kind=BF16):
        size = lefts[0].shape[0] // self.mp

        def part(by):
            return product(*(chunk_of(left, (self.shard + by) % self.mp, size) for left in lefts))

        return [self.along(part(by).astype(kind), by) for by in range(1, self.mp)], part(0)

    def scatter_sum(self, product, lefts, kind=BF16):
        arrived, own = self.scatter_parts(product, lefts, kind)
        return sum((rows.astype(F32) for rows in arrived), own)

    def gather(self, rows):
        chunks = [(self.shard, rows)]
        chunks += [((self.shard + by) % self.mp, self.along(rows, -by)) for by in range(1, self.mp)]
        return assemble(chunks)

    def spread(self, rows):
        mp = self.mp
        arrived = []
        for turn in range(mp):

            def target(chip, x, core, turn=turn):
                line = x * 2 + core
                return chip, (line % mp - turn) % mp, line // mp

            arrived.append(self.send(rows, target))
        return arrived

    def spread_out(self, rows, arrived, kind):
        chunks = []
        for turn, chunk in enumerate(arrived):
            mine = (self.seq == self.core) & ((self.shard - turn) % self.mp == self.x)
            chunks.append(((self.x + turn) % self.mp, jnp.where(mine, rows, chunk).astype(kind)))
        return assemble(chunks)

    def bits(self):
        return self.chips.bit_length() - 1

    def meet(self, values, bits):
        mp = self.mp

        def target(chip, x, core):
            for bit in bits:
                if bit == "sequence":
                    line = (x * 2 + core + mp) % (2 * mp)
                    x, core = line // 2, line % 2
                elif bit == "core":
                    core = 1 - core
                elif isinstance(bit, tuple):
                    x = x ^ (1 << bit[1])
                else:
                    chip = chip ^ (1 << bit)
            return chip, x, core

        return self.send(values, target)

    def my_bit(self, bit):
        if bit == "sequence":
            return self.seq
        if bit == "core":
            return self.core
        return (self.chip >> bit) & 1


class Scatter:
    def __init__(self, at, values, stages, last):
        bits = at.bits()
        self.at, self.order, self.axes = at, [stage for stage in stages if stage], list(range(bits))[::-1] + [last]
        self.values = values.reshape((2,) * (bits + 1) + (values.shape[0] // 2 ** (bits + 1), values.shape[1]))
        self.arrived = None

    def pieces(self):
        stage = self.order.pop(0)
        if isinstance(stage[0], tuple):
            self.sets = [tuple(stage)]
            return self.values, [self.values]
        sets = [()]
        for bit in stage:
            sets += [some + (bit,) for some in sets]
        axes = self.axes
        self.axes = [axis for axis in axes if axis not in stage]
        self.sets = sets[1:]
        size = [1 if axis in stage else 2 for axis in axes] + list(self.values.shape[-2:])
        shape = [2] * len(self.axes) + list(self.values.shape[-2:])
        parts = []
        for some in sets:
            start = [0] * len(size)
            for bit in stage:
                mine = self.at.my_bit(bit)
                start[axes.index(bit)] = 1 - mine if bit in some else mine
            parts.append(lax.dynamic_slice(self.values, start, size).reshape(shape))
        return parts[0], parts[1:]

    def prepare(self):
        self.kept, sent = self.pieces()
        self.sent = [part.astype(BF16) for part in sent]

    def start(self):
        self.arrived = [self.at.meet(part, some) for part, some in zip(self.sent, self.sets)]

    def finish(self):
        self.values = sum((part.astype(F32) for part in self.arrived), self.kept.astype(F32))
        self.arrived = None


def launch(chains, *values):
    moving = []
    for chain in chains:
        if chain.arrived is not None:
            chain.finish()
        if chain.order:
            chain.prepare()
            moving.append(chain)
    values, sents = lax.optimization_barrier((values, [chain.sent for chain in moving]))
    for chain, sent in zip(moving, sents):
        chain.sent = sent
        chain.start()
    return values[0] if len(values) == 1 else values


def settle(chains, *values):
    moving = [chain for chain in chains if chain.arrived is not None]
    values, arrivals = lax.optimization_barrier((values, [chain.arrived for chain in moving]))
    for chain, arrived in zip(moving, arrivals):
        chain.arrived = arrived
    return values[0] if len(values) == 1 else values


def per_device(
    decoder_layer_input,
    encoder_states,
    retrieved_owner,
    retrieved_block,
    self_query,
    self_attention_key,
    self_value,
    self_out,
    gain_first,
    shift_first,
    cross_query,
    cross_key,
    cross_value,
    cross_out,
    gain_second,
    shift_second,
    hidden_up,
    hidden_down,
    gain_third,
    shift_third,
    out_grad,
):
    at = Places()
    score_scale = jnp.asarray(DH**-0.5, BF16)
    seq_len, width = decoder_layer_input.shape
    shard_width = self_query.shape[1]
    chunk = seq_len // at.mp
    blocks_here = encoder_states.shape[0] // BLOCK
    chip_bits = list(range(at.bits()))
    x_bits = [("x", i) for i in range(at.mp.bit_length() - 1)]
    tie = lambda *values: lax.optimization_barrier(values)

    def even(weight):
        extra = -weight.shape[1] % LANES
        return jnp.pad(weight, ((0, 0), (0, extra))) if extra else weight

    def even_rows(weight):
        extra = -weight.shape[0] % LANES
        return jnp.pad(weight, ((0, extra), (0, 0))) if extra else weight

    def interleave(*weights):
        weights = [even(weight) for weight in weights]
        return jnp.concatenate(
            [w[:, i : i + LANES] for i in range(0, weights[0].shape[1], LANES) for w in weights], 1
        )

    def separate(values, count):
        size = values.shape[1] // count
        return [
            jnp.concatenate([values[:, (i * count + j) * LANES :][:, :LANES] for i in range(size // LANES)], 1)[
                :, :shard_width
            ]
            for j in range(count)
        ]

    store = lax.all_gather(encoder_states, "dp", axis=0, tiled=True)
    keys = store.shape[0]

    w_out, w_cross_query = at.weight(self_out), at.weight(cross_query)
    mix_first, total_first = self_forward(
        *(nn(decoder_layer_input, even(w)).astype(BF16) for w in (self_query, self_attention_key, self_value))
    )
    mix_first, w_out, w_cross_query, own_rows, next_key, next_value, owner, block = tie(
        mix_first,
        w_out,
        w_cross_query,
        decoder_layer_input,
        cross_key,
        cross_value,
        retrieved_owner,
        retrieved_block,
    )
    w_out, w_cross_query = even_rows(w_out), even(w_cross_query)
    self_mix = at.to_work(mix_first)
    own_rows = at.sequence_chunk(own_rows).astype(F32)
    names = at.sequence(owner * blocks_here + block)
    w_cross_key, w_cross_value = at.weight(next_key), at.weight(next_value)

    self_mix, own_rows, names, next_out = tie(self_mix, own_rows, names, cross_out)
    w_cross_out = at.weight(next_out)
    first_in = own_rows + at.scatter_sum(lambda rows: nn(rows, w_out), [self_mix], F32)
    first_unit, first_scale = normalize(first_in)
    first = first_unit * gain_first + shift_first
    first_low = at.gather(first.astype(BF16))
    first_low, w_cross_key, w_cross_value = tie(first_low, w_cross_key, w_cross_value)
    w_store = interleave(w_cross_key, w_cross_value)
    queries = nn(first_low, w_cross_query).astype(BF16) * score_scale
    queries, store, w_store, next_up, next_down, rows_grad = tie(
        queries, store, w_store, hidden_up, hidden_down, out_grad
    )
    w_up, w_down = at.weight(next_up), at.weight(next_down)
    rows_grad = at.sequence_chunk(rows_grad)
    store_kv = nn(store, w_store).astype(BF16)
    terms = key_terms(keys, keys // BLOCK + 3 > DH)
    cross_sum, cross_mix, cross_total, barred = cross_forward(queries, names, store_kv, terms)
    cross_mix, w_cross_out, w_up, w_down, rows_grad = tie(cross_mix, w_cross_out, w_up, w_down, rows_grad)
    w_cross_out, rows_grad = even_rows(w_cross_out), rows_grad.astype(F32)
    second_in = first + at.scatter_sum(lambda rows: nn(rows, w_cross_out), [cross_mix], F32)
    second_unit, second_scale = normalize(second_in)
    second = second_unit * gain_second + shift_second
    second_low = at.gather(second.astype(BF16))
    hidden_pre = nn(second_low, w_up)
    bell = 0.5 + 0.5 * lax.erf(hidden_pre * 0.5**0.5)
    hidden_act = (hidden_pre * bell).astype(BF16)
    slope = bell + hidden_pre * jnp.exp(-0.5 * hidden_pre * hidden_pre) * 0.3989422804014327
    third_in = second + at.scatter_sum(lambda rows: nn(rows, w_down), [hidden_act])
    third_unit, third_scale = normalize(third_in)
    layer_out = (third_unit * gain_third + shift_third).astype(BF16)

    res3_grad, gain_third_grad, shift_third_grad = norm_backward(third_unit, third_scale, gain_third, rows_grad)
    ffn_grad = at.gather(res3_grad.astype(BF16))
    pre_grad = (slope * nt(ffn_grad, w_down)).astype(BF16)
    second_grad = res3_grad + at.scatter_sum(lambda rows: nt(rows, w_up), [pre_grad])
    res2_grad, gain_second_grad, shift_second_grad = norm_backward(
        second_unit, second_scale, gain_second, second_grad
    )
    cross_grad = at.gather(res2_grad.astype(BF16))
    mix_grad = nt(cross_grad, w_cross_out).astype(BF16)
    early = jnp.concatenate(
        [
            tn(ffn_grad, hidden_act).astype(BF16),
            tn(second_low, pre_grad).astype(BF16),
            tn(cross_grad, cross_mix).astype(BF16),
        ],
        1,
    )
    w_triple = interleave(self_query, self_attention_key, self_value)
    mix_grad, early, layer_out, w_triple, self_total, rows_in = tie(
        mix_grad, early, layer_out, w_triple, total_first, decoder_layer_input
    )
    rows_in = at.sequence(rows_in)
    early = at.sum_group(early)
    layer_arrived = at.spread(layer_out)
    w_triple = at.weight(w_triple)
    self_total = at.to_work(self_total)
    queries_grad, kv_grad = cross_backward(
        queries, barred, store_kv, terms, 0, keys, mix_grad, cross_sum, cross_total, (), True
    )
    queries_grad, kv_grad, layer_arrived, w_triple, self_total, rows_in = tie(
        queries_grad, kv_grad, layer_arrived, w_triple, self_total, rows_in
    )
    encoder = Scatter(at, kv_grad, [["core"], chip_bits[:2], chip_bits[2:]], "core")
    kept, sent = encoder.pieces()
    shape = kept.shape[:-1] + (width,)
    encoder.sent = [nt(part.reshape(-1, part.shape[-1]), w_store).astype(BF16).reshape(shape) for part in sent]
    encoder.start()
    encoder.kept = nt(kept.reshape(-1, kept.shape[-1]), w_store).reshape(shape)
    first_grad = res2_grad + at.scatter_sum(lambda rows: nt(rows, w_cross_query), [queries_grad])
    res1_grad, gain_first_grad, shift_first_grad = norm_backward(first_unit, first_scale, gain_first, first_grad)
    res1_grad = launch([encoder], res1_grad)
    self_grad = at.gather(res1_grad.astype(BF16))
    side = Scatter(
        at,
        jnp.concatenate(
            [
                tn(store, kv_grad).astype(BF16),
                tn(first_low, queries_grad).astype(BF16),
                tn(self_grad, self_mix).astype(BF16),
            ],
            1,
        ),
        [["sequence"], chip_bits[1:2], chip_bits[:1], chip_bits[2:]],
        "sequence",
    )
    smix_grad = nt(self_grad, w_out).astype(BF16)
    self_qkv = nn(rows_in, w_triple).astype(BF16)
    smix_grad = launch([side], smix_grad)
    norms = jnp.stack(
        [
            gain_first_grad,
            shift_first_grad,
            gain_second_grad,
            shift_second_grad,
            gain_third_grad,
            shift_third_grad,
        ],
        0,
    )
    norms = sum((at.along(norms, by) for by in range(1, at.mp)), norms)
    norms = tn(norms.astype(BF16), jnp.eye(6, LANES, dtype=BF16)).astype(BF16)
    triple = self_backward(self_qkv, smix_grad, self_mix, self_total)
    triple, early, layer_out, layer_arrived = settle([side], triple, early, layer_out, layer_arrived)
    arrived, own = at.scatter_parts(lambda rows: nt(rows, w_triple), [triple])
    last = jnp.concatenate([tn(rows_in, triple).astype(BF16), norms], 1)
    last = Scatter(at, last, [chip_bits[:1], ["sequence"], chip_bits[1:]], "sequence")
    input_rows = (sum((rows.astype(F32) for rows in arrived), own) + res1_grad).astype(BF16)
    input_rows = launch([last, side, encoder], input_rows)
    input_arrived = at.spread(input_rows)
    layer_out = at.spread_out(layer_out, layer_arrived, BF16)
    input_arrived = settle([last, side], input_arrived)
    input_arrived = launch([last, side], input_arrived)
    input_grad = at.spread_out(input_rows, input_arrived, F32)
    encoder.order += [[bit] for bit in x_bits]
    chains = [last, side, encoder]
    while any(chain.order or chain.arrived is not None for chain in chains):
        settle(chains)
        launch(chains)

    encoder_grad = encoder.values
    ends = [chain.values.astype(BF16) for chain in (last, side)]
    gathered = at.from_work(jnp.concatenate(ends + [early.astype(BF16)], 1)).astype(F32)
    cuts = np.cumsum([0] + [end.shape[1] for end in ends])
    last, side, early = gathered[:, : cuts[1]], gathered[:, cuts[1] : cuts[2]], gathered[:, cuts[2] :]
    part_width = triple.shape[1] // 3
    norms = last[:, 3 * part_width :][:, :6].T
    self_query_grad, self_key_grad, self_value_grad = separate(last[:, : 3 * part_width], 3)
    cross_key_grad, cross_value_grad = separate(side[:, : 2 * part_width], 2)
    cross_query_grad = side[:, 2 * part_width : 2 * part_width + shard_width]
    self_out_grad = side[:, 3 * part_width : 3 * part_width + shard_width]
    hidden = hidden_act.shape[1]
    hidden_down_grad, hidden_up_grad = early[:, :hidden], early[:, hidden : 2 * hidden]
    cross_out_grad = early[:, 2 * hidden : 2 * hidden + shard_width]
    share = width // at.dp
    return (
        layer_out,
        input_grad,
        encoder_grad,
        self_query_grad,
        self_key_grad,
        self_value_grad,
        self_out_grad.T,
        norms[0],
        norms[1],
        cross_query_grad,
        cross_key_grad,
        cross_value_grad,
        cross_out_grad.T,
        norms[2],
        norms[3],
        hidden_up_grad,
        hidden_down_grad.T,
        norms[4],
        norms[5],
    )


def solution(mesh):
    rows, columns, parts, copied = P("dp", None), P(None, "mp"), P("mp", None), P()
    return jax.shard_map(
        per_device,
        mesh=mesh,
        in_specs=(rows,) * 4
        + (columns,) * 3
        + (parts, copied, copied)
        + (columns,) * 3
        + (parts, copied, copied)
        + (columns, parts, copied, copied, rows),
        out_specs=(rows,) * 3
        + (P("dp", "mp"),) * 3
        + (P("mp", "dp"), P("dp"), P("dp"))
        + (P("dp", "mp"),) * 3
        + (P("mp", "dp"), P("dp"), P("dp"))
        + (P("dp", "mp"), P("mp", "dp"), P("dp"), P("dp")),
        check_vma=False,
    )
```

```python
import functools

import jax
import jax.numpy as jnp
import numpy as np
from jax import lax
from jax.experimental import pallas as pl
from jax.experimental.pallas import tpu as pltpu
from jax.sharding import PartitionSpec as P

DH = 64
BLOCK = 128
LANES = 128
EPSILON = 1e-05
NEGATIVE = -1e30
VMEM_LIMIT = 56 * 1024 * 1024
BF16, F32 = jnp.bfloat16, jnp.float32


def nn(left, right):
    return lax.dot_general(left, right, (((1,), (0,)), ((), ())), preferred_element_type=F32)


def nt(left, right):
    return lax.dot_general(left, right, (((1,), (1,)), ((), ())), preferred_element_type=F32)


def tn(left, right):
    return lax.dot_general(left, right, (((0,), (0,)), ((), ())), preferred_element_type=F32)


def low_half(shape):
    return lax.broadcasted_iota(jnp.int32, shape, 1) < DH


def pick(low, head, own, other):
    return jnp.where(low, own, other) if head == 0 else jnp.where(low, other, own)


def split_three(values):
    high = values.astype(BF16)
    rest = values - high.astype(F32)
    middle = rest.astype(BF16)
    last = (rest - middle.astype(F32)).astype(BF16)
    return high.astype(F32), middle.astype(F32), last.astype(F32)


def widen(base, extra):
    return base if extra is None else jnp.concatenate([base, extra], 1)


def barred_lanes(names, blocks, period):
    shape = (names.shape[0], LANES)
    lane = lax.broadcasted_iota(jnp.int32, shape, 1) % period
    found = lane >= blocks
    for request in range(names.shape[1]):
        found = found | (names[:, request : request + 1] == lane)
    return jnp.where(found, 0.0, NEGATIVE)


def key_terms(keys, wide):
    blocks = keys // BLOCK
    free = 0 if wide else blocks
    block, lane = np.arange(keys)[:, None] // BLOCK, np.arange(LANES)[None, :]
    ones = (lane % DH >= free) & (lane % DH < free + 3)
    if wide:
        terms = np.concatenate([np.broadcast_to(ones, (keys, LANES)), block == lane], 1)
    else:
        terms = ones | (block == lane % DH)
    return jnp.asarray(terms.astype(np.float32), BF16)


def cross_forward_kernel(
    chunk, blocks, wide, q_ref, names_ref, kv_ref, terms_ref, sum_ref, mix_ref, total_ref, barred_ref, k_wide, v_wide, s_ref
):
    keys, rows = kv_ref.shape[0], q_ref.shape[0]

    @pl.when(pl.program_id(1) == 0)
    def _():
        for at in range(0, keys, chunk):
            part = slice(at, at + chunk)
            low = low_half((chunk, LANES))
            k, v = kv_ref[part, :LANES], kv_ref[part, LANES:]
            terms = terms_ref[part, :]
            for head in range(2):
                k_wide[head, part, :] = widen(
                    pick(low, head, k, terms[:, :LANES]), terms[:, LANES:] if wide else None
                )
                v_wide[head, part, :] = pick(low, head, v, jnp.ones_like(v))

    size = s_ref.shape[1]
    low = low_half((size, LANES))
    here = pl.ds(pl.multiple_of(pl.program_id(1) * rows, rows), rows)

    @pl.when(pl.program_id(0) == 0)
    def _():
        barred_ref[here, :] = barred_lanes(names_ref[...], blocks, LANES if wide else DH).astype(BF16)

    units = [(head, at) for at in range(0, rows, size) for head in range(2)]

    def begin(unit):
        head, at = units[unit]
        q = q_ref[at : at + size, :]
        barred = barred_ref[pl.ds(pl.multiple_of(pl.program_id(1) * rows + at, size), size), :]
        return widen(pick(low, head, q, jnp.zeros_like(q)), barred) if wide else pick(low, head, q, barred)

    def score(unit, q_wide, part, peak):
        scores = nt(q_wide, k_wide[units[unit][0], part, :])
        s_ref[unit % 2, :, part] = scores
        for lane in range(0, chunk, LANES):
            peak = jnp.maximum(peak, scores[:, lane : lane + LANES])
        return peak

    parts = [slice(at, at + chunk) for at in range(0, keys, chunk)]
    nothing = jnp.full((size, LANES), -jnp.inf, F32)
    peak, q_wide = nothing, begin(0)
    for part in parts:
        peak = score(0, q_wide, part, peak)
    done = []
    for unit, (head, at) in enumerate(units):
        top = jnp.max(peak, -1, keepdims=True)
        more = unit + 1 < len(units)
        peak, q_wide = nothing, begin(unit + 1) if more else None
        mixed = jnp.zeros((size, LANES), F32)
        for part in parts:
            if more:
                peak = score(unit + 1, q_wide, part, peak)
            prob = jnp.exp(s_ref[unit % 2, :, part] - top).astype(BF16)
            mixed = mixed + nn(prob, v_wide[head, part, :])
        weight = mixed[:, DH : DH + 1] if head == 0 else mixed[:, 0:1]
        done.append((mixed / weight, top + jnp.log(weight)))
        if head == 1:
            sums = jnp.where(low, done[-2][0], done[-1][0])
            sum_ref[at : at + size, :] = sums
            mix_ref[at : at + size, :] = sums.astype(BF16)
            total_ref[at : at + size, :] = jnp.where(low, done[-2][1], done[-1][1])


def cross_forward(q, names, kv, terms):
    rows, width = q.shape
    keys = kv.shape[0]
    blocks = keys // BLOCK
    wide = blocks + 3 > DH
    tile, size = (rows, min(rows, 256)) if keys <= 4096 else (64, 64)
    chunk = min(keys, 512)
    by_tile = pl.BlockSpec((tile, LANES), lambda pair, i: (i, pair))
    return pl.pallas_call(
        functools.partial(cross_forward_kernel, chunk, blocks, wide),
        grid=(width // LANES, rows // tile),
        in_specs=[
            by_tile,
            pl.BlockSpec((tile, names.shape[1]), lambda pair, i: (i, 0)),
            pl.BlockSpec((keys, 2 * LANES), lambda pair, i: (0, pair)),
            pl.BlockSpec(terms.shape, lambda pair, i: (0, 0)),
        ],
        out_specs=[by_tile] * 3 + [pl.BlockSpec((rows, LANES), lambda pair, i: (0, 0))],
        out_shape=[
            jax.ShapeDtypeStruct((rows, width), F32),
            jax.ShapeDtypeStruct((rows, width), BF16),
            jax.ShapeDtypeStruct((rows, width), F32),
            jax.ShapeDtypeStruct((rows, LANES), BF16),
        ],
        scratch_shapes=[
            pltpu.VMEM((2, keys, 2 * LANES if wide else LANES), BF16),
            pltpu.VMEM((2, keys, LANES), BF16),
            pltpu.VMEM((2, size, keys), F32),
        ],
        compiler_params=pltpu.CompilerParams(vmem_limit_bytes=VMEM_LIMIT),
        cost_estimate=pl.CostEstimate(flops=2 * rows * keys * width, bytes_accessed=8 * keys * width, transcendentals=0),
        name="cross_forward",
    )(q, names, kv, terms)


def cross_backward_kernel(blocks, wide, merge, *refs):
    q_ref, barred_ref, kv_ref, terms_ref, grad_ref, sum_ref, total_ref = refs[:7]
    refs = refs[7:]
    if merge:
        old_ref, refs = refs[0], refs[1:]
    dq_ref, dkv_ref, q_wide, q_only, g_wide, g_only, dq_sum = refs
    rows, chunk = q_ref.shape[0], kv_ref.shape[0]
    step = pl.program_id(1)
    free = 0 if wide else blocks

    @pl.when(step == 0)
    def _():
        size = min(rows, 256)
        low = low_half((size, LANES))
        lane = lax.broadcasted_iota(jnp.int32, (size, LANES), 1) % DH
        zero = jnp.zeros((size, LANES), F32)
        for at in range(0, rows, size):
            part = slice(at, at + size)
            q, grad = q_ref[part, :].astype(F32), grad_ref[part, :].astype(F32)
            total = total_ref[part, :]
            high, middle, last = split_three(jnp.where(low, total[:, DH : DH + 1], total[:, 0:1]))
            barred = barred_ref[part, :].astype(F32)
            extra = zero if wide else barred
            extra = jnp.where(lane == free, -high, extra)
            extra = jnp.where(lane == free + 1, -middle, extra)
            extra = jnp.where(lane == free + 2, -last, extra)
            inner = grad * sum_ref[part, :]
            inner_0 = jnp.sum(jnp.where(low, inner, zero), -1, keepdims=True)
            inner_1 = jnp.sum(jnp.where(low, zero, inner), -1, keepdims=True)
            high, middle, last = split_three(jnp.where(low, inner_1, inner_0))
            less = jnp.where(lane == 0, -high, jnp.where(lane == 1, -middle, jnp.where(lane == 2, -last, zero)))
            for head in range(2):
                q_wide[head, part, :] = widen(pick(low, head, q, extra), barred if wide else None).astype(BF16)
                q_only[head, part, :] = pick(low, head, q, zero).astype(BF16)
                g_wide[head, part, :] = pick(low, head, grad, less).astype(BF16)
                g_only[head, part, :] = pick(low, head, grad, zero).astype(BF16)
        dq_sum[...] = jnp.zeros_like(dq_sum)

    low = low_half((chunk, LANES))
    k, v = kv_ref[:, :LANES], kv_ref[:, LANES:]
    terms, own_terms = terms_ref[:, :LANES], terms_ref[:, LANES:] if wide else None
    dk = dv = None
    for head in range(2):
        prob = jnp.exp(nt(widen(pick(low, head, k, terms), own_terms), q_wide[head]))
        prob_grad = nt(pick(low, head, v, jnp.ones_like(v)), g_wide[head])
        score_grad = (prob * prob_grad).astype(BF16)
        dv_head, dk_head = nn(prob.astype(BF16), g_only[head]), nn(score_grad, q_only[head])
        dv = dv_head if dv is None else dv + dv_head
        dk = dk_head if dk is None else dk + dk_head
        dq_sum[...] += tn(pick(low, head, k, jnp.zeros_like(k)), score_grad)
    dkv_ref[:, :LANES] = dk.astype(dkv_ref.dtype)
    dkv_ref[:, LANES:] = dv.astype(dkv_ref.dtype)

    @pl.when(step == pl.num_programs(1) - 1)
    def _():
        dq = dq_sum[...].T * DH**-0.5
        if merge:
            dq = dq + old_ref[...]
        dq_ref[...] = dq.astype(dq_ref.dtype)


def cross_backward(q, barred, kv, terms, start, keys, grad, cross_sum, total, old, final):
    rows, width = q.shape
    blocks = kv.shape[0] // BLOCK
    wide = blocks + 3 > DH
    chunk = min(keys, 512 if wide else 1024)
    by_pair = pl.BlockSpec((rows, LANES), lambda pair, i: (0, pair))
    return pl.pallas_call(
        functools.partial(cross_backward_kernel, blocks, wide, bool(old)),
        grid=(width // LANES, keys // chunk),
        in_specs=[
            by_pair,
            pl.BlockSpec((rows, LANES), lambda pair, i: (0, 0)),
            pl.BlockSpec((chunk, 2 * LANES), lambda pair, i: (i + start // chunk, pair)),
            pl.BlockSpec((chunk, terms.shape[1]), lambda pair, i: (i + start // chunk, 0)),
        ]
        + [by_pair] * (3 + len(old)),
        out_specs=[by_pair, pl.BlockSpec((chunk, 2 * LANES), lambda pair, i: (i, pair))],
        out_shape=[
            jax.ShapeDtypeStruct((rows, width), BF16 if final else F32),
            jax.ShapeDtypeStruct((keys, 2 * width), BF16),
        ],
        scratch_shapes=[pltpu.VMEM((2, rows, 2 * LANES if wide else LANES), BF16)]
        + [pltpu.VMEM((2, rows, LANES), BF16)] * 3
        + [pltpu.VMEM((LANES, rows), F32)],
        compiler_params=pltpu.CompilerParams(vmem_limit_bytes=VMEM_LIMIT),
        cost_estimate=pl.CostEstimate(flops=2 * rows * keys * width, bytes_accessed=8 * keys * width, transcendentals=0),
        name="cross_backward",
    )(q, barred, kv, terms, grad, cross_sum, total, *old)


def self_forward_kernel(tile, q_ref, k_ref, v_ref, mix_ref, total_ref):
    rows = q_ref.shape[0]
    low_all = low_half((rows, LANES))
    low = low_half((tile, LANES))
    k, v = k_ref[...], v_ref[...]
    zero = jnp.zeros_like(k)
    keys = [pick(low_all, head, k, zero) for head in range(2)]
    values = [pick(low_all, head, v, jnp.ones_like(v)) for head in range(2)]
    ahead = lax.broadcasted_iota(jnp.int32, (tile, tile), 1) > lax.broadcasted_iota(jnp.int32, (tile, tile), 0)
    for at in range(0, rows, tile):
        q = q_ref[at : at + tile, :] * jnp.asarray(DH**-0.5, BF16)
        sums, totals = [], []
        for head in range(2):
            edge = jnp.where(ahead, NEGATIVE, nt(q, keys[head][at : at + tile]))
            top = jnp.max(edge, -1, keepdims=True)
            if at:
                before = nt(q, keys[head][:at])
                top = jnp.maximum(top, jnp.max(before, -1, keepdims=True))
            mixed = nn(jnp.exp(edge - top).astype(BF16), values[head][at : at + tile])
            if at:
                mixed = mixed + nn(jnp.exp(before - top).astype(BF16), values[head][:at])
            weight = mixed[:, DH : DH + 1] if head == 0 else mixed[:, 0:1]
            sums.append(mixed / weight)
            totals.append(top + jnp.log(weight))
        mix_ref[at : at + tile, :] = jnp.where(low, sums[0], sums[1]).astype(BF16)
        columns = jnp.where(low, totals[0], totals[1]).T
        total_ref[0, 0:1, at : at + tile] = columns[0:1]
        total_ref[0, 1:2, at : at + tile] = columns[DH : DH + 1]


def self_forward(q, k, v):
    rows, width = q.shape
    return pl.pallas_call(
        functools.partial(self_forward_kernel, min(rows, 512)),
        grid=(width // LANES,),
        in_specs=[pl.BlockSpec((rows, LANES), lambda pair: (0, pair))] * 3,
        out_specs=[
            pl.BlockSpec((rows, LANES), lambda pair: (0, pair)),
            pl.BlockSpec((1, 2, rows), lambda pair: (pair, 0, 0)),
        ],
        out_shape=[
            jax.ShapeDtypeStruct((rows, width), BF16),
            jax.ShapeDtypeStruct((width // LANES, 2, rows), F32),
        ],
        compiler_params=pltpu.CompilerParams(vmem_limit_bytes=VMEM_LIMIT),
        cost_estimate=pl.CostEstimate(flops=2 * rows * rows * width, bytes_accessed=8 * rows * width, transcendentals=0),
        name="self_forward",
    )(q, k, v)


def self_backward_kernel(
    tile, rows_ref, w_ref, self_grad_ref, w_out_ref, mix_ref, total_ref, norms_ref, part_ref, last_ref, out_ref, qkv_ref, grad_ref
):
    rows = rows_ref.shape[0]
    tiles = rows // tile
    pair = pl.program_id(0)
    for at in range(0, rows, tile):
        part = slice(at, at + tile)
        qkv_ref[part, :] = nn(rows_ref[part, :], w_ref[...]).astype(BF16)
        grad_ref[part, :] = nt(self_grad_ref[part, :], w_out_ref[...]).astype(BF16)
    low_all = low_half((rows, LANES))
    low = low_half((tile, LANES))
    q, grad = qkv_ref[:, :LANES] * jnp.asarray(DH**-0.5, BF16), grad_ref[...]
    zero = jnp.zeros_like(q)
    q_only = [pick(low_all, head, q, zero) for head in range(2)]
    g_only = [pick(low_all, head, grad, zero) for head in range(2)]
    inner = grad.astype(F32) * mix_ref[...].astype(F32)
    mine = lax.broadcasted_iota(jnp.int32, (8, LANES), 1) < DH
    ones = lax.broadcasted_iota(jnp.int32, (8, LANES), 0) == jnp.where(mine, 0, 1)
    inners = lax.dot_general(
        ones.astype(F32), inner, (((1,), (1,)), ((), ())), precision=lax.Precision.HIGHEST, preferred_element_type=F32
    )
    behind = lax.broadcasted_iota(jnp.int32, (tile, tile), 0) > lax.broadcasted_iota(jnp.int32, (tile, tile), 1)
    dq = [None] * tiles
    for i in range(tiles):
        part = slice(i * tile, (i + 1) * tile)
        k, v = qkv_ref[part, LANES : 2 * LANES], qkv_ref[part, 2 * LANES :]
        dk = dv = None
        for head in range(2):
            k_only = pick(low, head, k, jnp.zeros_like(k))
            v_only = pick(low, head, v, jnp.zeros_like(v))
            for j in range(i, tiles):
                at = slice(j * tile, (j + 1) * tile)
                scores = nt(k_only, q[at]) - total_ref[0, head : head + 1, at]
                if i == j:
                    scores = jnp.where(behind, NEGATIVE, scores)
                prob = jnp.exp(scores)
                prob_grad = nt(v_only, grad[at])
                score_grad = (prob * (prob_grad - inners[head : head + 1, at])).astype(BF16)
                dv_part = nn(prob.astype(BF16), g_only[head][at])
                dk_part = nn(score_grad, q_only[head][at])
                dq_part = tn(score_grad, k_only)
                dv = dv_part if dv is None else dv + dv_part
                dk = dk_part if dk is None else dk + dk_part
                dq[j] = dq_part if dq[j] is None else dq[j] + dq_part
        out_ref[part, LANES : 2 * LANES] = dk.astype(BF16)
        out_ref[part, 2 * LANES :] = dv.astype(BF16)
    for i in range(tiles):
        out_ref[i * tile : (i + 1) * tile, :LANES] = (dq[i] * DH**-0.5).astype(BF16)
    size = 3 * LANES
    for i in range(tiles):
        part = slice(i * tile, (i + 1) * tile)
        rows_part = nt(out_ref[part, :], w_ref[...])

        @pl.when(pair == 0)
        def _():
            part_ref[part, :] = rows_part

        @pl.when(pair > 0)
        def _():
            part_ref[part, :] += rows_part

    last_ref[:, pl.ds(pl.multiple_of(pair * size, size), size)] = tn(rows_ref[...], out_ref[...]).astype(BF16)
    last_ref[:, last_ref.shape[1] - LANES :] = norms_ref[...]


def self_backward(rows_in, w_triple, self_grad, w_out, mix, total, norms):
    rows, width = rows_in.shape
    size = 3 * LANES
    by_pair = pl.BlockSpec((rows, LANES), lambda pair: (0, pair))
    whole = lambda array: pl.BlockSpec(array.shape, lambda pair: (0, 0))
    last = jax.ShapeDtypeStruct((width, w_triple.shape[1] + LANES), BF16)
    return pl.pallas_call(
        functools.partial(self_backward_kernel, min(rows, 512)),
        grid=(w_triple.shape[1] // size,),
        in_specs=[
            whole(rows_in),
            pl.BlockSpec((width, size), lambda pair: (0, pair)),
            whole(self_grad),
            pl.BlockSpec((LANES, width), lambda pair: (pair, 0)),
            by_pair,
            pl.BlockSpec((1, 2, rows), lambda pair: (pair, 0, 0)),
            whole(norms),
        ],
        out_specs=[whole(rows_in), whole(last)],
        out_shape=[jax.ShapeDtypeStruct((rows, width), F32), last],
        scratch_shapes=[pltpu.VMEM((rows, size), BF16)] * 2 + [pltpu.VMEM((rows, LANES), BF16)],
        compiler_params=pltpu.CompilerParams(vmem_limit_bytes=VMEM_LIMIT),
        cost_estimate=pl.CostEstimate(flops=rows * rows * LANES, bytes_accessed=rows * width, transcendentals=0),
        name="self_backward",
    )(rows_in, w_triple, self_grad, w_out, mix, total, norms)


def normalize(values):
    center = values - jnp.mean(values, -1, keepdims=True)
    scale = lax.rsqrt(jnp.mean(center * center, -1, keepdims=True) + EPSILON)
    return center * scale, scale


def norm_backward(unit, scale, gain, upstream):
    weighted = upstream * gain
    grad = weighted - jnp.mean(weighted, -1, keepdims=True) - unit * jnp.mean(weighted * unit, -1, keepdims=True)
    return grad * scale, jnp.sum(upstream * unit, 0), jnp.sum(upstream, 0)


def chunk_of(rows, index, size):
    return lax.dynamic_slice_in_dim(rows, index * size, size, 0)


def assemble(chunks):
    size, width = chunks[0][1].shape
    result = jnp.zeros((size * len(chunks), width), chunks[0][1].dtype)
    for index, rows in chunks:
        result = lax.dynamic_update_slice_in_dim(result, rows, index * size, 0)
    return result


class Places:
    def __init__(self):
        self.mp, self.dp = lax.axis_size("mp"), lax.axis_size("dp")
        self.chips = self.dp // 2
        self.x, self.d = lax.axis_index("mp"), lax.axis_index("dp")
        self.core, self.chip = self.d % 2, self.d // 2
        self.line = self.x * 2 + self.core
        self.shard, self.seq = self.line % self.mp, self.line // self.mp

    def send(self, values, target):
        pairs = []
        for chip in range(self.chips):
            for x in range(self.mp):
                for core in range(2):
                    to_chip, to_x, to_core = target(chip, x, core)
                    pair = ((chip * 2 + core) * self.mp + x, (to_chip * 2 + to_core) * self.mp + to_x)
                    if pair[0] != pair[1]:
                        pairs.append(pair)
        return lax.ppermute(values, ("dp", "mp"), pairs)

    def weight(self, values):
        def target(chip, x, core):
            line = x if core else self.mp + x
            return chip, line // 2, line % 2

        return self.send(values, target)

    def to_work(self, values):
        arrived = self.send(values, lambda chip, x, core: (chip, (core * self.mp + x) // 2, (core * self.mp + x) % 2))
        return jnp.where((self.shard == self.x) & (self.seq == self.core), values, arrived)

    def from_work(self, values):
        mp = self.mp
        arrived = self.send(values, lambda chip, x, core: (chip, (x * 2 + core) % mp, (x * 2 + core) // mp))
        return jnp.where((self.shard == self.x) & (self.seq == self.core), values, arrived)

    def to_partner(self, values):
        def target(chip, x, core):
            return chip, x, 1 - core if (x * 2 + 1 - core) // self.mp == core else core

        return self.send(values, target)

    def sequence(self, values):
        return jnp.where(self.core == self.seq, values, self.to_partner(values))

    def sequence_chunk(self, values):
        size = values.shape[0] // self.mp
        partner = (self.x * 2 + 1 - self.core) % self.mp
        arrived = self.to_partner(chunk_of(values, partner, size))
        return jnp.where(self.core == self.seq, chunk_of(values, self.shard, size), arrived)

    def sum_group(self, grads):
        groups = [
            [
                (chip * 2 + line % 2) * self.mp + line // 2
                for chip in range(self.chips)
                for line in (shard, self.mp + shard)
            ]
            for shard in range(self.mp)
        ]
        return lax.psum_scatter(grads, ("dp", "mp"), scatter_dimension=0, axis_index_groups=groups, tiled=True)

    def along(self, values, shift):
        def target(chip, x, core):
            line = x * 2 + core
            line = line // self.mp * self.mp + (line + shift) % self.mp
            return chip, line // 2, line % 2

        return self.send(values, target)

    def scatter_parts(self, product, lefts, kind=BF16):
        size = lefts[0].shape[0] // self.mp

        def part(by):
            return product(*(chunk_of(left, (self.shard + by) % self.mp, size) for left in lefts))

        return [self.along(part(by).astype(kind), by) for by in range(1, self.mp)], part(0)

    def scatter_sum(self, product, lefts, kind=BF16):
        arrived, own = self.scatter_parts(product, lefts, kind)
        return sum((rows.astype(F32) for rows in arrived), own)

    def gather(self, rows):
        chunks = [(self.shard, rows)]
        chunks += [((self.shard + by) % self.mp, self.along(rows, -by)) for by in range(1, self.mp)]
        return assemble(chunks)

    def spread(self, rows):
        mp = self.mp
        arrived = []
        for turn in range(mp):

            def target(chip, x, core, turn=turn):
                line = x * 2 + core
                return chip, (line % mp - turn) % mp, line // mp

            arrived.append(self.send(rows, target))
        return arrived

    def spread_out(self, rows, arrived, kind):
        chunks = []
        for turn, chunk in enumerate(arrived):
            mine = (self.seq == self.core) & ((self.shard - turn) % self.mp == self.x)
            chunks.append(((self.x + turn) % self.mp, jnp.where(mine, rows, chunk).astype(kind)))
        return assemble(chunks)

    def bits(self):
        return self.chips.bit_length() - 1

    def meet(self, values, bits):
        mp = self.mp

        def target(chip, x, core):
            for bit in bits:
                if bit == "sequence":
                    line = (x * 2 + core + mp) % (2 * mp)
                    x, core = line // 2, line % 2
                elif bit == "core":
                    core = 1 - core
                elif isinstance(bit, tuple):
                    x = x ^ (1 << bit[1])
                else:
                    chip = chip ^ (1 << bit)
            return chip, x, core

        return self.send(values, target)

    def my_bit(self, bit):
        if bit == "sequence":
            return self.seq
        if bit == "core":
            return self.core
        return (self.chip >> bit) & 1


class Scatter:
    def __init__(self, at, values, stages, last):
        bits = at.bits()
        self.at, self.order, self.axes = at, [stage for stage in stages if stage], list(range(bits))[::-1] + [last]
        self.values = values.reshape((2,) * (bits + 1) + (values.shape[0] // 2 ** (bits + 1), values.shape[1]))
        self.arrived = None

    def pieces(self):
        stage = self.order.pop(0)
        if isinstance(stage[0], tuple):
            self.sets = [tuple(stage)]
            return self.values, [self.values]
        sets = [()]
        for bit in stage:
            sets += [some + (bit,) for some in sets]
        axes = self.axes
        self.axes = [axis for axis in axes if axis not in stage]
        self.sets = sets[1:]
        size = [1 if axis in stage else 2 for axis in axes] + list(self.values.shape[-2:])
        shape = [2] * len(self.axes) + list(self.values.shape[-2:])
        parts = []
        for some in sets:
            start = [0] * len(size)
            for bit in stage:
                mine = self.at.my_bit(bit)
                start[axes.index(bit)] = 1 - mine if bit in some else mine
            parts.append(lax.dynamic_slice(self.values, start, size).reshape(shape))
        return parts[0], parts[1:]

    def prepare(self):
        self.kept, sent = self.pieces()
        self.sent = [part.astype(BF16) for part in sent]

    def start(self):
        self.arrived = [self.at.meet(part, some) for part, some in zip(self.sent, self.sets)]

    def finish(self):
        self.values = sum((part.astype(F32) for part in self.arrived), self.kept.astype(F32))
        self.arrived = None


def launch(chains, *values):
    moving = []
    for chain in chains:
        if chain.arrived is not None:
            chain.finish()
        if chain.order:
            chain.prepare()
            moving.append(chain)
    values, sents = lax.optimization_barrier((values, [chain.sent for chain in moving]))
    for chain, sent in zip(moving, sents):
        chain.sent = sent
        chain.start()
    return values[0] if len(values) == 1 else values


def settle(chains, *values):
    moving = [chain for chain in chains if chain.arrived is not None]
    values, arrivals = lax.optimization_barrier((values, [chain.arrived for chain in moving]))
    for chain, arrived in zip(moving, arrivals):
        chain.arrived = arrived
    return values[0] if len(values) == 1 else values


def per_device(
    decoder_layer_input,
    encoder_states,
    retrieved_owner,
    retrieved_block,
    self_query,
    self_attention_key,
    self_value,
    self_out,
    gain_first,
    shift_first,
    cross_query,
    cross_key,
    cross_value,
    cross_out,
    gain_second,
    shift_second,
    hidden_up,
    hidden_down,
    gain_third,
    shift_third,
    out_grad,
):
    at = Places()
    score_scale = jnp.asarray(DH**-0.5, BF16)
    seq_len, width = decoder_layer_input.shape
    shard_width = self_query.shape[1]
    chunk = seq_len // at.mp
    blocks_here = encoder_states.shape[0] // BLOCK
    chip_bits = list(range(at.bits()))
    x_bits = [("x", i) for i in range(at.mp.bit_length() - 1)]
    tie = lambda *values: lax.optimization_barrier(values)

    def even(weight):
        extra = -weight.shape[1] % LANES
        return jnp.pad(weight, ((0, 0), (0, extra))) if extra else weight

    def even_rows(weight):
        extra = -weight.shape[0] % LANES
        return jnp.pad(weight, ((0, extra), (0, 0))) if extra else weight

    def interleave(*weights):
        weights = [even(weight) for weight in weights]
        return jnp.concatenate(
            [w[:, i : i + LANES] for i in range(0, weights[0].shape[1], LANES) for w in weights], 1
        )

    def separate(values, count):
        size = values.shape[1] // count
        return [
            jnp.concatenate([values[:, (i * count + j) * LANES :][:, :LANES] for i in range(size // LANES)], 1)[
                :, :shard_width
            ]
            for j in range(count)
        ]

    store = lax.all_gather(encoder_states, "dp", axis=0, tiled=True)
    keys = store.shape[0]

    w_out, w_cross_query = at.weight(self_out), at.weight(cross_query)
    mix_first, total_first = self_forward(
        *(nn(decoder_layer_input, even(w)).astype(BF16) for w in (self_query, self_attention_key, self_value))
    )
    mix_first, w_out, w_cross_query, own_rows, next_key, next_value, owner, block = tie(
        mix_first,
        w_out,
        w_cross_query,
        decoder_layer_input,
        cross_key,
        cross_value,
        retrieved_owner,
        retrieved_block,
    )
    w_out, w_cross_query = even_rows(w_out), even(w_cross_query)
    self_mix = at.to_work(mix_first)
    own_rows = at.sequence_chunk(own_rows).astype(F32)
    names = at.sequence(owner * blocks_here + block)
    w_cross_key, w_cross_value = at.weight(next_key), at.weight(next_value)

    self_mix, own_rows, names, next_out = tie(self_mix, own_rows, names, cross_out)
    w_cross_out = at.weight(next_out)
    first_in = own_rows + at.scatter_sum(lambda rows: nn(rows, w_out), [self_mix], F32)
    first_unit, first_scale = normalize(first_in)
    first = first_unit * gain_first + shift_first
    first_low = at.gather(first.astype(BF16))
    first_low, w_cross_key, w_cross_value = tie(first_low, w_cross_key, w_cross_value)
    w_store = interleave(w_cross_key, w_cross_value)
    queries = nn(first_low, w_cross_query).astype(BF16) * score_scale
    queries, store, w_store, next_up, next_down, rows_grad = tie(
        queries, store, w_store, hidden_up, hidden_down, out_grad
    )
    w_up, w_down = at.weight(next_up), at.weight(next_down)
    rows_grad = at.sequence_chunk(rows_grad)
    store_kv = nn(store, w_store).astype(BF16)
    terms = key_terms(keys, keys // BLOCK + 3 > DH)
    cross_sum, cross_mix, cross_total, barred = cross_forward(queries, names, store_kv, terms)
    cross_mix, w_cross_out, w_up, w_down, rows_grad = tie(cross_mix, w_cross_out, w_up, w_down, rows_grad)
    w_cross_out, rows_grad = even_rows(w_cross_out), rows_grad.astype(F32)
    second_in = first + at.scatter_sum(lambda rows: nn(rows, w_cross_out), [cross_mix], F32)
    second_unit, second_scale = normalize(second_in)
    second = second_unit * gain_second + shift_second
    second_low = at.gather(second.astype(BF16))
    hidden_pre = nn(second_low, w_up)
    bell = 0.5 + 0.5 * lax.erf(hidden_pre * 0.5**0.5)
    hidden_act = (hidden_pre * bell).astype(BF16)
    slope = bell + hidden_pre * jnp.exp(-0.5 * hidden_pre * hidden_pre) * 0.3989422804014327
    third_in = second + at.scatter_sum(lambda rows: nn(rows, w_down), [hidden_act])
    third_unit, third_scale = normalize(third_in)
    layer_out = (third_unit * gain_third + shift_third).astype(BF16)

    res3_grad, gain_third_grad, shift_third_grad = norm_backward(third_unit, third_scale, gain_third, rows_grad)
    ffn_grad = at.gather(res3_grad.astype(BF16))
    pre_grad = (slope * nt(ffn_grad, w_down)).astype(BF16)
    second_grad = res3_grad + at.scatter_sum(lambda rows: nt(rows, w_up), [pre_grad])
    res2_grad, gain_second_grad, shift_second_grad = norm_backward(
        second_unit, second_scale, gain_second, second_grad
    )
    cross_grad = at.gather(res2_grad.astype(BF16))
    mix_grad = nt(cross_grad, w_cross_out).astype(BF16)
    early = jnp.concatenate(
        [
            tn(ffn_grad, hidden_act).astype(BF16),
            tn(second_low, pre_grad).astype(BF16),
            tn(cross_grad, cross_mix).astype(BF16),
        ],
        1,
    )
    w_triple = interleave(self_query, self_attention_key, self_value)
    mix_grad, early, layer_out, w_triple, self_total, rows_in = tie(
        mix_grad, early, layer_out, w_triple, total_first, decoder_layer_input
    )
    rows_in = at.sequence(rows_in)
    early = at.sum_group(early)
    layer_arrived = at.spread(layer_out)
    w_triple = at.weight(w_triple)
    self_total = at.to_work(self_total)
    queries_grad, kv_grad = cross_backward(
        queries, barred, store_kv, terms, 0, keys, mix_grad, cross_sum, cross_total, (), True
    )
    queries_grad, kv_grad, layer_arrived, w_triple, self_total, rows_in = tie(
        queries_grad, kv_grad, layer_arrived, w_triple, self_total, rows_in
    )
    encoder = Scatter(at, kv_grad, [["core"], chip_bits[:2], chip_bits[2:]], "core")
    kept, sent = encoder.pieces()
    shape = kept.shape[:-1] + (width,)
    encoder.sent = [nt(part.reshape(-1, part.shape[-1]), w_store).astype(BF16).reshape(shape) for part in sent]
    encoder.start()
    encoder.kept = nt(kept.reshape(-1, kept.shape[-1]), w_store).reshape(shape)
    first_grad = res2_grad + at.scatter_sum(lambda rows: nt(rows, w_cross_query), [queries_grad])
    res1_grad, gain_first_grad, shift_first_grad = norm_backward(first_unit, first_scale, gain_first, first_grad)
    res1_grad = launch([encoder], res1_grad)
    self_grad = at.gather(res1_grad.astype(BF16))
    side = Scatter(
        at,
        jnp.concatenate(
            [
                tn(store, kv_grad).astype(BF16),
                tn(first_low, queries_grad).astype(BF16),
                tn(self_grad, self_mix).astype(BF16),
            ],
            1,
        ),
        [["sequence"], chip_bits[1:2], chip_bits[:1], chip_bits[2:]],
        "sequence",
    )
    self_grad = launch([side], self_grad)
    norms = jnp.stack(
        [
            gain_first_grad,
            shift_first_grad,
            gain_second_grad,
            shift_second_grad,
            gain_third_grad,
            shift_third_grad,
        ],
        0,
    )
    norms = sum((at.along(norms, by) for by in range(1, at.mp)), norms)
    norms = tn(norms.astype(BF16), jnp.eye(6, LANES, dtype=BF16)).astype(BF16)
    part, last = self_backward(rows_in, w_triple, self_grad, w_out, self_mix, self_total, norms)
    part, last, early, layer_out, layer_arrived = settle(
        [side, encoder], part, last, early, layer_out, layer_arrived
    )
    input_rows = (res1_grad + at.scatter_sum(lambda rows: rows, [part])).astype(BF16)
    last = Scatter(at, last, [chip_bits[:1], ["sequence"], chip_bits[1:]], "sequence")
    launch([last, side, encoder])
    input_arrived = at.spread(input_rows)
    early = at.from_work(early.astype(BF16))
    layer_out = at.spread_out(layer_out, layer_arrived, BF16)
    input_arrived, early = settle([last, side, encoder], input_arrived, early)
    early = early.astype(F32)
    input_arrived = launch([last, side], input_arrived)
    input_grad = at.spread_out(input_rows, input_arrived, F32)
    encoder.order += [[bit] for bit in x_bits]
    chains = [last, side, encoder]
    while any(chain.order or chain.arrived is not None for chain in chains):
        settle(chains)
        launch(chains)

    encoder_grad = encoder.values
    last_width = last.values.shape[1]
    gathered = at.from_work(jnp.concatenate([chain.values.astype(BF16) for chain in (last, side)], 1)).astype(F32)
    last, side = gathered[:, :last_width], gathered[:, last_width:]
    part_width = w_triple.shape[1] // 3
    norms = last[:, 3 * part_width :][:, :6].T
    self_query_grad, self_key_grad, self_value_grad = separate(last[:, : 3 * part_width], 3)
    cross_key_grad, cross_value_grad = separate(side[:, : 2 * part_width], 2)
    cross_query_grad = side[:, 2 * part_width : 2 * part_width + shard_width]
    self_out_grad = side[:, 3 * part_width : 3 * part_width + shard_width]
    hidden = hidden_act.shape[1]
    hidden_down_grad, hidden_up_grad = early[:, :hidden], early[:, hidden : 2 * hidden]
    cross_out_grad = early[:, 2 * hidden : 2 * hidden + shard_width]
    share = width // at.dp
    return (
        layer_out,
        input_grad,
        encoder_grad,
        self_query_grad,
        self_key_grad,
        self_value_grad,
        self_out_grad.T,
        norms[0],
        norms[1],
        cross_query_grad,
        cross_key_grad,
        cross_value_grad,
        cross_out_grad.T,
        norms[2],
        norms[3],
        hidden_up_grad,
        hidden_down_grad.T,
        norms[4],
        norms[5],
    )


def solution(mesh):
    rows, columns, parts, copied = P("dp", None), P(None, "mp"), P("mp", None), P()
    return jax.shard_map(
        per_device,
        mesh=mesh,
        in_specs=(rows,) * 4
        + (columns,) * 3
        + (parts, copied, copied)
        + (columns,) * 3
        + (parts, copied, copied)
        + (columns, parts, copied, copied, rows),
        out_specs=(rows,) * 3
        + (P("dp", "mp"),) * 3
        + (P("mp", "dp"), P("dp"), P("dp"))
        + (P("dp", "mp"),) * 3
        + (P("mp", "dp"), P("dp"), P("dp"))
        + (P("dp", "mp"), P("mp", "dp"), P("dp"), P("dp")),
        check_vma=False,
    )
```

```python
import functools

import jax
import jax.numpy as jnp
import numpy as np
from jax import lax
from jax.experimental import pallas as pl
from jax.experimental.pallas import tpu as pltpu
from jax.sharding import PartitionSpec as P

DH = 64
BLOCK = 128
LANES = 128
EPSILON = 1e-05
NEGATIVE = -1e30
VMEM_LIMIT = 56 * 1024 * 1024
BF16, F32 = jnp.bfloat16, jnp.float32


def nn(left, right):
    return lax.dot_general(left, right, (((1,), (0,)), ((), ())), preferred_element_type=F32)


def nt(left, right):
    return lax.dot_general(left, right, (((1,), (1,)), ((), ())), preferred_element_type=F32)


def tn(left, right):
    return lax.dot_general(left, right, (((0,), (0,)), ((), ())), preferred_element_type=F32)


def low_half(shape):
    return lax.broadcasted_iota(jnp.int32, shape, 1) < DH


def pick(low, head, own, other):
    return jnp.where(low, own, other) if head == 0 else jnp.where(low, other, own)


def split_three(values):
    high = values.astype(BF16)
    rest = values - high.astype(F32)
    middle = rest.astype(BF16)
    last = (rest - middle.astype(F32)).astype(BF16)
    return high.astype(F32), middle.astype(F32), last.astype(F32)


def widen(base, extra):
    return base if extra is None else jnp.concatenate([base, extra], 1)


def barred_lanes(names, blocks, period):
    shape = (names.shape[0], LANES)
    lane = lax.broadcasted_iota(jnp.int32, shape, 1) % period
    found = lane >= blocks
    for request in range(names.shape[1]):
        found = found | (names[:, request : request + 1] == lane)
    return jnp.where(found, 0.0, NEGATIVE)


def key_terms(keys, wide):
    blocks = keys // BLOCK
    free = 0 if wide else blocks
    block, lane = np.arange(keys)[:, None] // BLOCK, np.arange(LANES)[None, :]
    ones = (lane % DH >= free) & (lane % DH < free + 3)
    if wide:
        terms = np.concatenate([np.broadcast_to(ones, (keys, LANES)), block == lane], 1)
    else:
        terms = ones | (block == lane % DH)
    return jnp.asarray(terms.astype(np.float32), BF16)


def cross_forward_kernel(
    chunk, blocks, wide, q_ref, names_ref, kv_ref, terms_ref, sum_ref, mix_ref, total_ref, barred_ref, k_wide, v_wide, s_ref
):
    keys, rows = kv_ref.shape[0], q_ref.shape[0]

    @pl.when(pl.program_id(1) == 0)
    def _():
        for at in range(0, keys, chunk):
            part = slice(at, at + chunk)
            low = low_half((chunk, LANES))
            k, v = kv_ref[part, :LANES], kv_ref[part, LANES:]
            terms = terms_ref[part, :]
            for head in range(2):
                k_wide[head, part, :] = widen(
                    pick(low, head, k, terms[:, :LANES]), terms[:, LANES:] if wide else None
                )
                v_wide[head, part, :] = pick(low, head, v, jnp.ones_like(v))

    size = s_ref.shape[1]
    low = low_half((size, LANES))
    here = pl.ds(pl.multiple_of(pl.program_id(1) * rows, rows), rows)

    @pl.when(pl.program_id(0) == 0)
    def _():
        barred_ref[here, :] = barred_lanes(names_ref[...], blocks, LANES if wide else DH).astype(BF16)

    units = [(head, at) for at in range(0, rows, size) for head in range(2)]

    def begin(unit):
        head, at = units[unit]
        q = q_ref[at : at + size, :]
        barred = barred_ref[pl.ds(pl.multiple_of(pl.program_id(1) * rows + at, size), size), :]
        return widen(pick(low, head, q, jnp.zeros_like(q)), barred) if wide else pick(low, head, q, barred)

    def score(unit, q_wide, part, peak):
        scores = nt(q_wide, k_wide[units[unit][0], part, :])
        s_ref[unit % 2, :, part] = scores
        for lane in range(0, chunk, LANES):
            peak = jnp.maximum(peak, scores[:, lane : lane + LANES])
        return peak

    parts = [slice(at, at + chunk) for at in range(0, keys, chunk)]
    nothing = jnp.full((size, LANES), -jnp.inf, F32)
    peak, q_wide = nothing, begin(0)
    for part in parts:
        peak = score(0, q_wide, part, peak)
    done = []
    for unit, (head, at) in enumerate(units):
        top = jnp.max(peak, -1, keepdims=True)
        more = unit + 1 < len(units)
        peak, q_wide = nothing, begin(unit + 1) if more else None
        mixed = jnp.zeros((size, LANES), F32)
        for part in parts:
            if more:
                peak = score(unit + 1, q_wide, part, peak)
            prob = jnp.exp(s_ref[unit % 2, :, part] - top).astype(BF16)
            mixed = mixed + nn(prob, v_wide[head, part, :])
        weight = mixed[:, DH : DH + 1] if head == 0 else mixed[:, 0:1]
        done.append((mixed / weight, top + jnp.log(weight)))
        if head == 1:
            sums = jnp.where(low, done[-2][0], done[-1][0])
            sum_ref[at : at + size, :] = sums
            mix_ref[at : at + size, :] = sums.astype(BF16)
            total_ref[at : at + size, :] = jnp.where(low, done[-2][1], done[-1][1])


def cross_forward(q, names, kv, terms):
    rows, width = q.shape
    keys = kv.shape[0]
    blocks = keys // BLOCK
    wide = blocks + 3 > DH
    tile, size = (rows, min(rows, 256)) if keys <= 4096 else (64, 64)
    chunk = min(keys, 512)
    by_tile = pl.BlockSpec((tile, LANES), lambda pair, i: (i, pair))
    return pl.pallas_call(
        functools.partial(cross_forward_kernel, chunk, blocks, wide),
        grid=(width // LANES, rows // tile),
        in_specs=[
            by_tile,
            pl.BlockSpec((tile, names.shape[1]), lambda pair, i: (i, 0)),
            pl.BlockSpec((keys, 2 * LANES), lambda pair, i: (0, pair)),
            pl.BlockSpec(terms.shape, lambda pair, i: (0, 0)),
        ],
        out_specs=[by_tile] * 3 + [pl.BlockSpec((rows, LANES), lambda pair, i: (0, 0))],
        out_shape=[
            jax.ShapeDtypeStruct((rows, width), F32),
            jax.ShapeDtypeStruct((rows, width), BF16),
            jax.ShapeDtypeStruct((rows, width), F32),
            jax.ShapeDtypeStruct((rows, LANES), BF16),
        ],
        scratch_shapes=[
            pltpu.VMEM((2, keys, 2 * LANES if wide else LANES), BF16),
            pltpu.VMEM((2, keys, LANES), BF16),
            pltpu.VMEM((2, size, keys), F32),
        ],
        compiler_params=pltpu.CompilerParams(vmem_limit_bytes=VMEM_LIMIT),
        cost_estimate=pl.CostEstimate(flops=2 * rows * keys * width, bytes_accessed=8 * keys * width, transcendentals=0),
        name="cross_forward",
    )(q, names, kv, terms)


def cross_backward_kernel(blocks, wide, merge, *refs):
    q_ref, barred_ref, kv_ref, terms_ref, grad_ref, sum_ref, total_ref = refs[:7]
    refs = refs[7:]
    if merge:
        old_ref, refs = refs[0], refs[1:]
    dq_ref, dkv_ref, q_wide, q_only, g_wide, g_only, dq_sum = refs
    rows, chunk = q_ref.shape[0], kv_ref.shape[0]
    step = pl.program_id(1)
    free = 0 if wide else blocks

    @pl.when(step == 0)
    def _():
        size = min(rows, 256)
        low = low_half((size, LANES))
        lane = lax.broadcasted_iota(jnp.int32, (size, LANES), 1) % DH
        zero = jnp.zeros((size, LANES), F32)
        for at in range(0, rows, size):
            part = slice(at, at + size)
            q, grad = q_ref[part, :].astype(F32), grad_ref[part, :].astype(F32)
            total = total_ref[part, :]
            high, middle, last = split_three(jnp.where(low, total[:, DH : DH + 1], total[:, 0:1]))
            barred = barred_ref[part, :].astype(F32)
            extra = zero if wide else barred
            extra = jnp.where(lane == free, -high, extra)
            extra = jnp.where(lane == free + 1, -middle, extra)
            extra = jnp.where(lane == free + 2, -last, extra)
            inner = grad * sum_ref[part, :]
            inner_0 = jnp.sum(jnp.where(low, inner, zero), -1, keepdims=True)
            inner_1 = jnp.sum(jnp.where(low, zero, inner), -1, keepdims=True)
            high, middle, last = split_three(jnp.where(low, inner_1, inner_0))
            less = jnp.where(lane == 0, -high, jnp.where(lane == 1, -middle, jnp.where(lane == 2, -last, zero)))
            for head in range(2):
                q_wide[head, part, :] = widen(pick(low, head, q, extra), barred if wide else None).astype(BF16)
                q_only[head, part, :] = pick(low, head, q, zero).astype(BF16)
                g_wide[head, part, :] = pick(low, head, grad, less).astype(BF16)
                g_only[head, part, :] = pick(low, head, grad, zero).astype(BF16)
        dq_sum[...] = jnp.zeros_like(dq_sum)

    low = low_half((chunk, LANES))
    k, v = kv_ref[:, :LANES], kv_ref[:, LANES:]
    terms, own_terms = terms_ref[:, :LANES], terms_ref[:, LANES:] if wide else None
    dk = dv = None
    for head in range(2):
        prob = jnp.exp(nt(widen(pick(low, head, k, terms), own_terms), q_wide[head]))
        prob_grad = nt(pick(low, head, v, jnp.ones_like(v)), g_wide[head])
        score_grad = (prob * prob_grad).astype(BF16)
        dv_head, dk_head = nn(prob.astype(BF16), g_only[head]), nn(score_grad, q_only[head])
        dv = dv_head if dv is None else dv + dv_head
        dk = dk_head if dk is None else dk + dk_head
        dq_sum[...] += tn(pick(low, head, k, jnp.zeros_like(k)), score_grad)
    dkv_ref[:, :LANES] = dk.astype(dkv_ref.dtype)
    dkv_ref[:, LANES:] = dv.astype(dkv_ref.dtype)

    @pl.when(step == pl.num_programs(1) - 1)
    def _():
        dq = dq_sum[...].T * DH**-0.5
        if merge:
            dq = dq + old_ref[...]
        dq_ref[...] = dq.astype(dq_ref.dtype)


def cross_backward(q, barred, kv, terms, start, keys, grad, cross_sum, total, old, final):
    rows, width = q.shape
    blocks = kv.shape[0] // BLOCK
    wide = blocks + 3 > DH
    chunk = min(keys, 512 if wide else 1024)
    by_pair = pl.BlockSpec((rows, LANES), lambda pair, i: (0, pair))
    return pl.pallas_call(
        functools.partial(cross_backward_kernel, blocks, wide, bool(old)),
        grid=(width // LANES, keys // chunk),
        in_specs=[
            by_pair,
            pl.BlockSpec((rows, LANES), lambda pair, i: (0, 0)),
            pl.BlockSpec((chunk, 2 * LANES), lambda pair, i: (i + start // chunk, pair)),
            pl.BlockSpec((chunk, terms.shape[1]), lambda pair, i: (i + start // chunk, 0)),
        ]
        + [by_pair] * (3 + len(old)),
        out_specs=[by_pair, pl.BlockSpec((chunk, 2 * LANES), lambda pair, i: (i, pair))],
        out_shape=[
            jax.ShapeDtypeStruct((rows, width), BF16 if final else F32),
            jax.ShapeDtypeStruct((keys, 2 * width), BF16),
        ],
        scratch_shapes=[pltpu.VMEM((2, rows, 2 * LANES if wide else LANES), BF16)]
        + [pltpu.VMEM((2, rows, LANES), BF16)] * 3
        + [pltpu.VMEM((LANES, rows), F32)],
        compiler_params=pltpu.CompilerParams(vmem_limit_bytes=VMEM_LIMIT),
        cost_estimate=pl.CostEstimate(flops=2 * rows * keys * width, bytes_accessed=8 * keys * width, transcendentals=0),
        name="cross_backward",
    )(q, barred, kv, terms, grad, cross_sum, total, *old)


def self_forward_kernel(tile, q_ref, k_ref, v_ref, mix_ref, total_ref):
    rows = q_ref.shape[0]
    low_all = low_half((rows, LANES))
    low = low_half((tile, LANES))
    k, v = k_ref[...], v_ref[...]
    zero = jnp.zeros_like(k)
    keys = [pick(low_all, head, k, zero) for head in range(2)]
    values = [pick(low_all, head, v, jnp.ones_like(v)) for head in range(2)]
    ahead = lax.broadcasted_iota(jnp.int32, (tile, tile), 1) > lax.broadcasted_iota(jnp.int32, (tile, tile), 0)
    for at in range(0, rows, tile):
        q = q_ref[at : at + tile, :] * jnp.asarray(DH**-0.5, BF16)
        sums, totals = [], []
        for head in range(2):
            edge = jnp.where(ahead, NEGATIVE, nt(q, keys[head][at : at + tile]))
            top = jnp.max(edge, -1, keepdims=True)
            if at:
                before = nt(q, keys[head][:at])
                top = jnp.maximum(top, jnp.max(before, -1, keepdims=True))
            mixed = nn(jnp.exp(edge - top).astype(BF16), values[head][at : at + tile])
            if at:
                mixed = mixed + nn(jnp.exp(before - top).astype(BF16), values[head][:at])
            weight = mixed[:, DH : DH + 1] if head == 0 else mixed[:, 0:1]
            sums.append(mixed / weight)
            totals.append(top + jnp.log(weight))
        mix_ref[at : at + tile, :] = jnp.where(low, sums[0], sums[1]).astype(BF16)
        columns = jnp.where(low, totals[0], totals[1]).T
        total_ref[0, 0:1, at : at + tile] = columns[0:1]
        total_ref[0, 1:2, at : at + tile] = columns[DH : DH + 1]


def self_forward(q, k, v):
    rows, width = q.shape
    return pl.pallas_call(
        functools.partial(self_forward_kernel, min(rows, 512)),
        grid=(width // LANES,),
        in_specs=[pl.BlockSpec((rows, LANES), lambda pair: (0, pair))] * 3,
        out_specs=[
            pl.BlockSpec((rows, LANES), lambda pair: (0, pair)),
            pl.BlockSpec((1, 2, rows), lambda pair: (pair, 0, 0)),
        ],
        out_shape=[
            jax.ShapeDtypeStruct((rows, width), BF16),
            jax.ShapeDtypeStruct((width // LANES, 2, rows), F32),
        ],
        compiler_params=pltpu.CompilerParams(vmem_limit_bytes=VMEM_LIMIT),
        cost_estimate=pl.CostEstimate(flops=2 * rows * rows * width, bytes_accessed=8 * rows * width, transcendentals=0),
        name="self_forward",
    )(q, k, v)


def self_backward_kernel(
    tile, rows_ref, w_ref, self_grad_ref, w_out_ref, mix_ref, total_ref, norms_ref, part_ref, last_ref, out_ref, qkv_ref, grad_ref
):
    rows = rows_ref.shape[0]
    tiles = rows // tile
    pair = pl.program_id(0)
    for at in range(0, rows, tile):
        part = slice(at, at + tile)
        qkv_ref[part, :] = nn(rows_ref[part, :], w_ref[...]).astype(BF16)
        grad_ref[part, :] = nt(self_grad_ref[part, :], w_out_ref[...]).astype(BF16)
    low_all = low_half((rows, LANES))
    low = low_half((tile, LANES))
    q, grad = qkv_ref[:, :LANES] * jnp.asarray(DH**-0.5, BF16), grad_ref[...]
    zero = jnp.zeros_like(q)
    q_only = [pick(low_all, head, q, zero) for head in range(2)]
    g_only = [pick(low_all, head, grad, zero) for head in range(2)]
    inner = grad.astype(F32) * mix_ref[...].astype(F32)
    mine = lax.broadcasted_iota(jnp.int32, (8, LANES), 1) < DH
    ones = lax.broadcasted_iota(jnp.int32, (8, LANES), 0) == jnp.where(mine, 0, 1)
    inners = lax.dot_general(
        ones.astype(F32), inner, (((1,), (1,)), ((), ())), precision=lax.Precision.HIGHEST, preferred_element_type=F32
    )
    behind = lax.broadcasted_iota(jnp.int32, (tile, tile), 0) > lax.broadcasted_iota(jnp.int32, (tile, tile), 1)
    dq = [None] * tiles
    for i in range(tiles):
        part = slice(i * tile, (i + 1) * tile)
        k, v = qkv_ref[part, LANES : 2 * LANES], qkv_ref[part, 2 * LANES :]
        dk = dv = None
        for head in range(2):
            k_only = pick(low, head, k, jnp.zeros_like(k))
            v_only = pick(low, head, v, jnp.zeros_like(v))
            for j in range(i, tiles):
                at = slice(j * tile, (j + 1) * tile)
                scores = nt(k_only, q[at]) - total_ref[0, head : head + 1, at]
                if i == j:
                    scores = jnp.where(behind, NEGATIVE, scores)
                prob = jnp.exp(scores)
                prob_grad = nt(v_only, grad[at])
                score_grad = (prob * (prob_grad - inners[head : head + 1, at])).astype(BF16)
                dv_part = nn(prob.astype(BF16), g_only[head][at])
                dk_part = nn(score_grad, q_only[head][at])
                dq_part = tn(score_grad, k_only)
                dv = dv_part if dv is None else dv + dv_part
                dk = dk_part if dk is None else dk + dk_part
                dq[j] = dq_part if dq[j] is None else dq[j] + dq_part
        out_ref[part, LANES : 2 * LANES] = dk.astype(BF16)
        out_ref[part, 2 * LANES :] = dv.astype(BF16)
    for i in range(tiles):
        out_ref[i * tile : (i + 1) * tile, :LANES] = (dq[i] * DH**-0.5).astype(BF16)
    size = 3 * LANES
    for i in range(tiles):
        part = slice(i * tile, (i + 1) * tile)
        rows_part = nt(out_ref[part, :], w_ref[...])

        @pl.when(pair == 0)
        def _():
            part_ref[part, :] = rows_part

        @pl.when(pair > 0)
        def _():
            part_ref[part, :] += rows_part

    last_ref[:, pl.ds(pl.multiple_of(pair * size, size), size)] = tn(rows_ref[...], out_ref[...]).astype(BF16)
    last_ref[:, last_ref.shape[1] - LANES :] = norms_ref[...]


def self_backward(rows_in, w_triple, self_grad, w_out, mix, total, norms):
    rows, width = rows_in.shape
    size = 3 * LANES
    by_pair = pl.BlockSpec((rows, LANES), lambda pair: (0, pair))
    whole = lambda array: pl.BlockSpec(array.shape, lambda pair: (0, 0))
    last = jax.ShapeDtypeStruct((width, w_triple.shape[1] + LANES), BF16)
    return pl.pallas_call(
        functools.partial(self_backward_kernel, min(rows, 512)),
        grid=(w_triple.shape[1] // size,),
        in_specs=[
            whole(rows_in),
            pl.BlockSpec((width, size), lambda pair: (0, pair)),
            whole(self_grad),
            pl.BlockSpec((LANES, width), lambda pair: (pair, 0)),
            by_pair,
            pl.BlockSpec((1, 2, rows), lambda pair: (pair, 0, 0)),
            whole(norms),
        ],
        out_specs=[whole(rows_in), whole(last)],
        out_shape=[jax.ShapeDtypeStruct((rows, width), F32), last],
        scratch_shapes=[pltpu.VMEM((rows, size), BF16)] * 2 + [pltpu.VMEM((rows, LANES), BF16)],
        compiler_params=pltpu.CompilerParams(vmem_limit_bytes=VMEM_LIMIT),
        cost_estimate=pl.CostEstimate(flops=rows * rows * LANES, bytes_accessed=rows * width, transcendentals=0),
        name="self_backward",
    )(rows_in, w_triple, self_grad, w_out, mix, total, norms)


def normalize(values):
    center = values - jnp.mean(values, -1, keepdims=True)
    scale = lax.rsqrt(jnp.mean(center * center, -1, keepdims=True) + EPSILON)
    return center * scale, scale


def norm_backward(unit, scale, gain, upstream):
    weighted = upstream * gain
    grad = weighted - jnp.mean(weighted, -1, keepdims=True) - unit * jnp.mean(weighted * unit, -1, keepdims=True)
    return grad * scale, jnp.sum(upstream * unit, 0), jnp.sum(upstream, 0)


def chunk_of(rows, index, size):
    return lax.dynamic_slice_in_dim(rows, index * size, size, 0)


def assemble(chunks):
    size, width = chunks[0][1].shape
    result = jnp.zeros((size * len(chunks), width), chunks[0][1].dtype)
    for index, rows in chunks:
        result = lax.dynamic_update_slice_in_dim(result, rows, index * size, 0)
    return result


class Places:
    def __init__(self):
        self.mp, self.dp = lax.axis_size("mp"), lax.axis_size("dp")
        self.chips = self.dp // 2
        self.x, self.d = lax.axis_index("mp"), lax.axis_index("dp")
        self.core, self.chip = self.d % 2, self.d // 2
        self.line = self.x * 2 + self.core
        self.shard, self.seq = self.line % self.mp, self.line // self.mp

    def send(self, values, target):
        pairs = []
        for chip in range(self.chips):
            for x in range(self.mp):
                for core in range(2):
                    to_chip, to_x, to_core = target(chip, x, core)
                    pair = ((chip * 2 + core) * self.mp + x, (to_chip * 2 + to_core) * self.mp + to_x)
                    if pair[0] != pair[1]:
                        pairs.append(pair)
        return lax.ppermute(values, ("dp", "mp"), pairs)

    def weight(self, values):
        def target(chip, x, core):
            line = x if core else self.mp + x
            return chip, line // 2, line % 2

        return self.send(values, target)

    def to_work(self, values):
        arrived = self.send(values, lambda chip, x, core: (chip, (core * self.mp + x) // 2, (core * self.mp + x) % 2))
        return jnp.where((self.shard == self.x) & (self.seq == self.core), values, arrived)

    def from_work(self, values):
        mp = self.mp
        arrived = self.send(values, lambda chip, x, core: (chip, (x * 2 + core) % mp, (x * 2 + core) // mp))
        return jnp.where((self.shard == self.x) & (self.seq == self.core), values, arrived)

    def to_partner(self, values):
        def target(chip, x, core):
            return chip, x, 1 - core if (x * 2 + 1 - core) // self.mp == core else core

        return self.send(values, target)

    def sequence(self, values):
        return jnp.where(self.core == self.seq, values, self.to_partner(values))

    def sequence_chunk(self, values):
        size = values.shape[0] // self.mp
        partner = (self.x * 2 + 1 - self.core) % self.mp
        arrived = self.to_partner(chunk_of(values, partner, size))
        return jnp.where(self.core == self.seq, chunk_of(values, self.shard, size), arrived)

    def sum_group(self, grads):
        groups = [
            [
                (chip * 2 + line % 2) * self.mp + line // 2
                for chip in range(self.chips)
                for line in (shard, self.mp + shard)
            ]
            for shard in range(self.mp)
        ]
        return lax.psum_scatter(grads, ("dp", "mp"), scatter_dimension=0, axis_index_groups=groups, tiled=True)

    def along(self, values, shift):
        def target(chip, x, core):
            line = x * 2 + core
            line = line // self.mp * self.mp + (line + shift) % self.mp
            return chip, line // 2, line % 2

        return self.send(values, target)

    def scatter_parts(self, product, lefts, kind=BF16):
        size = lefts[0].shape[0] // self.mp

        def part(by):
            return product(*(chunk_of(left, (self.shard + by) % self.mp, size) for left in lefts))

        return [self.along(part(by).astype(kind), by) for by in range(1, self.mp)], part(0)

    def scatter_sum(self, product, lefts, kind=BF16):
        arrived, own = self.scatter_parts(product, lefts, kind)
        return sum((rows.astype(F32) for rows in arrived), own)

    def gather(self, rows):
        chunks = [(self.shard, rows)]
        chunks += [((self.shard + by) % self.mp, self.along(rows, -by)) for by in range(1, self.mp)]
        return assemble(chunks)

    def spread(self, rows):
        mp = self.mp
        arrived = []
        for turn in range(mp):

            def target(chip, x, core, turn=turn):
                line = x * 2 + core
                return chip, (line % mp - turn) % mp, line // mp

            arrived.append(self.send(rows, target))
        return arrived

    def spread_out(self, rows, arrived, kind):
        chunks = []
        for turn, chunk in enumerate(arrived):
            mine = (self.seq == self.core) & ((self.shard - turn) % self.mp == self.x)
            chunks.append(((self.x + turn) % self.mp, jnp.where(mine, rows, chunk).astype(kind)))
        return assemble(chunks)

    def bits(self):
        return self.chips.bit_length() - 1

    def meet(self, values, bits):
        mp = self.mp

        def target(chip, x, core):
            for bit in bits:
                if bit == "sequence":
                    line = (x * 2 + core + mp) % (2 * mp)
                    x, core = line // 2, line % 2
                elif bit == "core":
                    core = 1 - core
                elif isinstance(bit, tuple):
                    x = x ^ (1 << bit[1])
                else:
                    chip = chip ^ (1 << bit)
            return chip, x, core

        return self.send(values, target)

    def my_bit(self, bit):
        if bit == "sequence":
            return self.seq
        if bit == "core":
            return self.core
        return (self.chip >> bit) & 1


class Scatter:
    def __init__(self, at, values, stages, last):
        bits = at.bits()
        self.at, self.order, self.axes = at, [stage for stage in stages if stage], list(range(bits))[::-1] + [last]
        self.values = values.reshape((2,) * (bits + 1) + (values.shape[0] // 2 ** (bits + 1), values.shape[1]))
        self.arrived = None

    def pieces(self):
        stage = self.order.pop(0)
        if isinstance(stage[0], tuple):
            self.sets = [tuple(stage)]
            return self.values, [self.values]
        sets = [()]
        for bit in stage:
            sets += [some + (bit,) for some in sets]
        axes = self.axes
        self.axes = [axis for axis in axes if axis not in stage]
        self.sets = sets[1:]
        size = [1 if axis in stage else 2 for axis in axes] + list(self.values.shape[-2:])
        shape = [2] * len(self.axes) + list(self.values.shape[-2:])
        parts = []
        for some in sets:
            start = [0] * len(size)
            for bit in stage:
                mine = self.at.my_bit(bit)
                start[axes.index(bit)] = 1 - mine if bit in some else mine
            parts.append(lax.dynamic_slice(self.values, start, size).reshape(shape))
        return parts[0], parts[1:]

    def prepare(self):
        self.kept, sent = self.pieces()
        self.sent = [part.astype(BF16) for part in sent]

    def start(self):
        self.arrived = [self.at.meet(part, some) for part, some in zip(self.sent, self.sets)]

    def finish(self):
        self.values = sum((part.astype(F32) for part in self.arrived), self.kept.astype(F32))
        self.arrived = None


def launch(chains, *values):
    moving = []
    for chain in chains:
        if chain.arrived is not None:
            chain.finish()
        if chain.order:
            chain.prepare()
            moving.append(chain)
    values, sents = lax.optimization_barrier((values, [chain.sent for chain in moving]))
    for chain, sent in zip(moving, sents):
        chain.sent = sent
        chain.start()
    return values[0] if len(values) == 1 else values


def settle(chains, *values):
    moving = [chain for chain in chains if chain.arrived is not None]
    values, arrivals = lax.optimization_barrier((values, [chain.arrived for chain in moving]))
    for chain, arrived in zip(moving, arrivals):
        chain.arrived = arrived
    return values[0] if len(values) == 1 else values


def per_device(
    decoder_layer_input,
    encoder_states,
    retrieved_owner,
    retrieved_block,
    self_query,
    self_attention_key,
    self_value,
    self_out,
    gain_first,
    shift_first,
    cross_query,
    cross_key,
    cross_value,
    cross_out,
    gain_second,
    shift_second,
    hidden_up,
    hidden_down,
    gain_third,
    shift_third,
    out_grad,
):
    at = Places()
    score_scale = jnp.asarray(DH**-0.5, BF16)
    seq_len, width = decoder_layer_input.shape
    shard_width = self_query.shape[1]
    chunk = seq_len // at.mp
    blocks_here = encoder_states.shape[0] // BLOCK
    chip_bits = list(range(at.bits()))
    x_bits = [("x", i) for i in range(at.mp.bit_length() - 1)]
    tie = lambda *values: lax.optimization_barrier(values)

    def even(weight):
        extra = -weight.shape[1] % LANES
        return jnp.pad(weight, ((0, 0), (0, extra))) if extra else weight

    def even_rows(weight):
        extra = -weight.shape[0] % LANES
        return jnp.pad(weight, ((0, extra), (0, 0))) if extra else weight

    def interleave(*weights):
        weights = [even(weight) for weight in weights]
        return jnp.concatenate(
            [w[:, i : i + LANES] for i in range(0, weights[0].shape[1], LANES) for w in weights], 1
        )

    def separate(values, count):
        size = values.shape[1] // count
        return [
            jnp.concatenate([values[:, (i * count + j) * LANES :][:, :LANES] for i in range(size // LANES)], 1)[
                :, :shard_width
            ]
            for j in range(count)
        ]

    store = lax.all_gather(encoder_states, "dp", axis=0, tiled=True)
    keys = store.shape[0]

    w_out, w_cross_query = at.weight(self_out), at.weight(cross_query)
    mix_first, total_first = self_forward(
        *(nn(decoder_layer_input, even(w)).astype(BF16) for w in (self_query, self_attention_key, self_value))
    )
    mix_first, w_out, w_cross_query, own_rows, next_key, next_value, owner, block = tie(
        mix_first,
        w_out,
        w_cross_query,
        decoder_layer_input,
        cross_key,
        cross_value,
        retrieved_owner,
        retrieved_block,
    )
    w_out, w_cross_query = even_rows(w_out), even(w_cross_query)
    self_mix = at.to_work(mix_first)
    own_rows = at.sequence_chunk(own_rows).astype(F32)
    names = at.sequence(owner * blocks_here + block)
    w_cross_key, w_cross_value = at.weight(next_key), at.weight(next_value)

    self_mix, own_rows, names, next_out = tie(self_mix, own_rows, names, cross_out)
    w_cross_out = at.weight(next_out)
    first_in = own_rows + at.scatter_sum(lambda rows: nn(rows, w_out), [self_mix], F32)
    first_in, w_cross_key, w_cross_value = tie(first_in, w_cross_key, w_cross_value)
    first_unit, first_scale = normalize(first_in)
    first = first_unit * gain_first + shift_first
    first_low = at.gather(first.astype(BF16))
    first_low, w_cross_out = tie(first_low, w_cross_out)
    w_store = interleave(w_cross_key, w_cross_value)
    queries = nn(first_low, w_cross_query).astype(BF16) * score_scale
    queries, store, w_store, next_up, next_down, rows_grad = tie(
        queries, store, w_store, hidden_up, hidden_down, out_grad
    )
    w_up, w_down = at.weight(next_up), at.weight(next_down)
    rows_grad = at.sequence_chunk(rows_grad)
    store_kv = nn(store, w_store).astype(BF16)
    terms = key_terms(keys, keys // BLOCK + 3 > DH)
    cross_sum, cross_mix, cross_total, barred = cross_forward(queries, names, store_kv, terms)
    cross_mix, w_up, w_down, rows_grad = tie(cross_mix, w_up, w_down, rows_grad)
    w_cross_out, rows_grad = even_rows(w_cross_out), rows_grad.astype(F32)
    second_in = first + at.scatter_sum(lambda rows: nn(rows, w_cross_out), [cross_mix], F32)
    second_unit, second_scale = normalize(second_in)
    second = second_unit * gain_second + shift_second
    second_low = at.gather(second.astype(BF16))
    hidden_pre = nn(second_low, w_up)
    bell = 0.5 + 0.5 * lax.erf(hidden_pre * 0.5**0.5)
    hidden_act = (hidden_pre * bell).astype(BF16)
    slope = bell + hidden_pre * jnp.exp(-0.5 * hidden_pre * hidden_pre) * 0.3989422804014327
    third_in = second + at.scatter_sum(lambda rows: nn(rows, w_down), [hidden_act])
    third_unit, third_scale = normalize(third_in)
    layer_out = (third_unit * gain_third + shift_third).astype(BF16)

    res3_grad, gain_third_grad, shift_third_grad = norm_backward(third_unit, third_scale, gain_third, rows_grad)
    ffn_grad = at.gather(res3_grad.astype(BF16))
    pre_grad = (slope * nt(ffn_grad, w_down)).astype(BF16)
    second_grad = res3_grad + at.scatter_sum(lambda rows: nt(rows, w_up), [pre_grad])
    res2_grad, gain_second_grad, shift_second_grad = norm_backward(
        second_unit, second_scale, gain_second, second_grad
    )
    cross_grad = at.gather(res2_grad.astype(BF16))
    mix_grad = nt(cross_grad, w_cross_out).astype(BF16)
    early = jnp.concatenate(
        [
            tn(ffn_grad, hidden_act).astype(BF16),
            tn(second_low, pre_grad).astype(BF16),
            tn(cross_grad, cross_mix).astype(BF16),
        ],
        1,
    )
    w_triple = interleave(self_query, self_attention_key, self_value)
    mix_grad, early, layer_out, w_triple, self_total, rows_in = tie(
        mix_grad, early, layer_out, w_triple, total_first, decoder_layer_input
    )
    rows_in = at.sequence(rows_in)
    early = at.sum_group(early)
    layer_arrived = at.spread(layer_out)
    w_triple = at.weight(w_triple)
    self_total = at.to_work(self_total)
    queries_grad, kv_grad = cross_backward(
        queries, barred, store_kv, terms, 0, keys, mix_grad, cross_sum, cross_total, (), True
    )
    queries_grad, kv_grad, layer_arrived, w_triple, self_total, rows_in = tie(
        queries_grad, kv_grad, layer_arrived, w_triple, self_total, rows_in
    )
    encoder = Scatter(at, kv_grad, [["core"], chip_bits[:2], chip_bits[2:]], "core")
    kept, sent = encoder.pieces()
    shape = kept.shape[:-1] + (width,)
    encoder.sent = [nt(part.reshape(-1, part.shape[-1]), w_store).astype(BF16).reshape(shape) for part in sent]
    encoder.start()
    encoder.kept = nt(kept.reshape(-1, kept.shape[-1]), w_store).reshape(shape)
    first_grad = res2_grad + at.scatter_sum(lambda rows: nt(rows, w_cross_query), [queries_grad])
    res1_grad, gain_first_grad, shift_first_grad = norm_backward(first_unit, first_scale, gain_first, first_grad)
    res1_grad = launch([encoder], res1_grad)
    self_grad = at.gather(res1_grad.astype(BF16))
    side = Scatter(
        at,
        jnp.concatenate(
            [
                tn(store, kv_grad).astype(BF16),
                tn(first_low, queries_grad).astype(BF16),
                tn(self_grad, self_mix).astype(BF16),
            ],
            1,
        ),
        [["sequence"], chip_bits[1:2], chip_bits[:1], chip_bits[2:]],
        "sequence",
    )
    self_grad = launch([side], self_grad)
    norms = jnp.stack(
        [
            gain_first_grad,
            shift_first_grad,
            gain_second_grad,
            shift_second_grad,
            gain_third_grad,
            shift_third_grad,
        ],
        0,
    )
    norms = sum((at.along(norms, by) for by in range(1, at.mp)), norms)
    norms = tn(norms.astype(BF16), jnp.eye(6, LANES, dtype=BF16)).astype(BF16)
    part, last = self_backward(rows_in, w_triple, self_grad, w_out, self_mix, self_total, norms)
    part, last, early, layer_out, layer_arrived = settle(
        [side, encoder], part, last, early, layer_out, layer_arrived
    )
    input_rows = (res1_grad + at.scatter_sum(lambda rows: rows, [part])).astype(BF16)
    last = Scatter(at, last, [chip_bits[:1], ["sequence"], chip_bits[1:]], "sequence")
    launch([last, side, encoder])
    input_arrived = at.spread(input_rows)
    early = at.from_work(early.astype(BF16))
    layer_out = at.spread_out(layer_out, layer_arrived, BF16)
    input_arrived, early = settle([last, side, encoder], input_arrived, early)
    early = early.astype(F32)
    input_arrived = launch([last, side], input_arrived)
    input_grad = at.spread_out(input_rows, input_arrived, F32)
    encoder.order += [[bit] for bit in x_bits]
    chains = [last, side, encoder]
    while any(chain.order or chain.arrived is not None for chain in chains):
        settle(chains)
        launch(chains)

    encoder_grad = encoder.values
    last_width = last.values.shape[1]
    gathered = at.from_work(jnp.concatenate([chain.values.astype(BF16) for chain in (last, side)], 1)).astype(F32)
    last, side = gathered[:, :last_width], gathered[:, last_width:]
    part_width = w_triple.shape[1] // 3
    norms = last[:, 3 * part_width :][:, :6].T
    self_query_grad, self_key_grad, self_value_grad = separate(last[:, : 3 * part_width], 3)
    cross_key_grad, cross_value_grad = separate(side[:, : 2 * part_width], 2)
    cross_query_grad = side[:, 2 * part_width : 2 * part_width + shard_width]
    self_out_grad = side[:, 3 * part_width : 3 * part_width + shard_width]
    hidden = hidden_act.shape[1]
    hidden_down_grad, hidden_up_grad = early[:, :hidden], early[:, hidden : 2 * hidden]
    cross_out_grad = early[:, 2 * hidden : 2 * hidden + shard_width]
    share = width // at.dp
    return (
        layer_out,
        input_grad,
        encoder_grad,
        self_query_grad,
        self_key_grad,
        self_value_grad,
        self_out_grad.T,
        norms[0],
        norms[1],
        cross_query_grad,
        cross_key_grad,
        cross_value_grad,
        cross_out_grad.T,
        norms[2],
        norms[3],
        hidden_up_grad,
        hidden_down_grad.T,
        norms[4],
        norms[5],
    )


def solution(mesh):
    rows, columns, parts, copied = P("dp", None), P(None, "mp"), P("mp", None), P()
    return jax.shard_map(
        per_device,
        mesh=mesh,
        in_specs=(rows,) * 4
        + (columns,) * 3
        + (parts, copied, copied)
        + (columns,) * 3
        + (parts, copied, copied)
        + (columns, parts, copied, copied, rows),
        out_specs=(rows,) * 3
        + (P("dp", "mp"),) * 3
        + (P("mp", "dp"), P("dp"), P("dp"))
        + (P("dp", "mp"),) * 3
        + (P("mp", "dp"), P("dp"), P("dp"))
        + (P("dp", "mp"), P("mp", "dp"), P("dp"), P("dp")),
        check_vma=False,
    )
```

```python
import functools

import jax
import jax.numpy as jnp
import numpy as np
from jax import lax
from jax.experimental import pallas as pl
from jax.experimental.pallas import tpu as pltpu
from jax.sharding import PartitionSpec as P

DH = 64
BLOCK = 128
LANES = 128
EPSILON = 1e-05
NEGATIVE = -1e30
VMEM_LIMIT = 56 * 1024 * 1024
BF16, F32 = jnp.bfloat16, jnp.float32


def nn(left, right):
    return lax.dot_general(left, right, (((1,), (0,)), ((), ())), preferred_element_type=F32)


def nt(left, right):
    return lax.dot_general(left, right, (((1,), (1,)), ((), ())), preferred_element_type=F32)


def tn(left, right):
    return lax.dot_general(left, right, (((0,), (0,)), ((), ())), preferred_element_type=F32)


def low_half(shape):
    return lax.broadcasted_iota(jnp.int32, shape, 1) < DH


def pick(low, head, own, other):
    return jnp.where(low, own, other) if head == 0 else jnp.where(low, other, own)


def split_three(values):
    high = values.astype(BF16)
    rest = values - high.astype(F32)
    middle = rest.astype(BF16)
    last = (rest - middle.astype(F32)).astype(BF16)
    return high.astype(F32), middle.astype(F32), last.astype(F32)


def widen(base, extra):
    return base if extra is None else jnp.concatenate([base, extra], 1)


def barred_lanes(names, blocks, period):
    shape = (names.shape[0], LANES)
    lane = lax.broadcasted_iota(jnp.int32, shape, 1) % period
    found = lane >= blocks
    for request in range(names.shape[1]):
        found = found | (names[:, request : request + 1] == lane)
    return jnp.where(found, 0.0, NEGATIVE)


def key_terms(keys, wide):
    blocks = keys // BLOCK
    free = 0 if wide else blocks
    block, lane = np.arange(keys)[:, None] // BLOCK, np.arange(LANES)[None, :]
    ones = (lane % DH >= free) & (lane % DH < free + 3)
    if wide:
        terms = np.concatenate([np.broadcast_to(ones, (keys, LANES)), block == lane], 1)
    else:
        terms = ones | (block == lane % DH)
    return jnp.asarray(terms.astype(np.float32), BF16)


def cross_forward_kernel(
    chunk, blocks, wide, q_ref, names_ref, kv_ref, terms_ref, sum_ref, mix_ref, total_ref, barred_ref, k_wide, v_wide, s_ref
):
    keys, rows = kv_ref.shape[0], q_ref.shape[0]

    @pl.when(pl.program_id(1) == 0)
    def _():
        for at in range(0, keys, chunk):
            part = slice(at, at + chunk)
            low = low_half((chunk, LANES))
            k, v = kv_ref[part, :LANES], kv_ref[part, LANES:]
            terms = terms_ref[part, :]
            for head in range(2):
                k_wide[head, part, :] = widen(
                    pick(low, head, k, terms[:, :LANES]), terms[:, LANES:] if wide else None
                )
                v_wide[head, part, :] = pick(low, head, v, jnp.ones_like(v))

    size = s_ref.shape[1]
    low = low_half((size, LANES))
    here = pl.ds(pl.multiple_of(pl.program_id(1) * rows, rows), rows)

    @pl.when(pl.program_id(0) == 0)
    def _():
        barred_ref[here, :] = barred_lanes(names_ref[...], blocks, LANES if wide else DH).astype(BF16)

    units = [(head, at) for at in range(0, rows, size) for head in range(2)]

    def begin(unit):
        head, at = units[unit]
        q = q_ref[at : at + size, :]
        barred = barred_ref[pl.ds(pl.multiple_of(pl.program_id(1) * rows + at, size), size), :]
        return widen(pick(low, head, q, jnp.zeros_like(q)), barred) if wide else pick(low, head, q, barred)

    def score(unit, q_wide, part, peak):
        scores = nt(q_wide, k_wide[units[unit][0], part, :])
        s_ref[unit % 2, :, part] = scores
        for lane in range(0, chunk, LANES):
            peak = jnp.maximum(peak, scores[:, lane : lane + LANES])
        return peak

    parts = [slice(at, at + chunk) for at in range(0, keys, chunk)]
    nothing = jnp.full((size, LANES), -jnp.inf, F32)
    peak, q_wide = nothing, begin(0)
    for part in parts:
        peak = score(0, q_wide, part, peak)
    done = []
    for unit, (head, at) in enumerate(units):
        top = jnp.max(peak, -1, keepdims=True)
        more = unit + 1 < len(units)
        peak, q_wide = nothing, begin(unit + 1) if more else None
        mixed = jnp.zeros((size, LANES), F32)
        for part in parts:
            if more:
                peak = score(unit + 1, q_wide, part, peak)
            prob = jnp.exp(s_ref[unit % 2, :, part] - top).astype(BF16)
            mixed = mixed + nn(prob, v_wide[head, part, :])
        weight = mixed[:, DH : DH + 1] if head == 0 else mixed[:, 0:1]
        done.append((mixed / weight, top + jnp.log(weight)))
        if head == 1:
            sums = jnp.where(low, done[-2][0], done[-1][0])
            sum_ref[at : at + size, :] = sums
            mix_ref[at : at + size, :] = sums.astype(BF16)
            total_ref[at : at + size, :] = jnp.where(low, done[-2][1], done[-1][1])


def cross_forward(q, names, kv, terms):
    rows, width = q.shape
    keys = kv.shape[0]
    blocks = keys // BLOCK
    wide = blocks + 3 > DH
    tile, size = (rows, min(rows, 256)) if keys <= 4096 else (64, 64)
    chunk = min(keys, 512)
    by_tile = pl.BlockSpec((tile, LANES), lambda pair, i: (i, pair))
    return pl.pallas_call(
        functools.partial(cross_forward_kernel, chunk, blocks, wide),
        grid=(width // LANES, rows // tile),
        in_specs=[
            by_tile,
            pl.BlockSpec((tile, names.shape[1]), lambda pair, i: (i, 0)),
            pl.BlockSpec((keys, 2 * LANES), lambda pair, i: (0, pair)),
            pl.BlockSpec(terms.shape, lambda pair, i: (0, 0)),
        ],
        out_specs=[by_tile] * 3 + [pl.BlockSpec((rows, LANES), lambda pair, i: (0, 0))],
        out_shape=[
            jax.ShapeDtypeStruct((rows, width), F32),
            jax.ShapeDtypeStruct((rows, width), BF16),
            jax.ShapeDtypeStruct((rows, width), F32),
            jax.ShapeDtypeStruct((rows, LANES), BF16),
        ],
        scratch_shapes=[
            pltpu.VMEM((2, keys, 2 * LANES if wide else LANES), BF16),
            pltpu.VMEM((2, keys, LANES), BF16),
            pltpu.VMEM((2, size, keys), F32),
        ],
        compiler_params=pltpu.CompilerParams(vmem_limit_bytes=VMEM_LIMIT),
        cost_estimate=pl.CostEstimate(flops=2 * rows * keys * width, bytes_accessed=8 * keys * width, transcendentals=0),
        name="cross_forward",
    )(q, names, kv, terms)


def cross_backward_kernel(blocks, wide, merge, *refs):
    q_ref, barred_ref, kv_ref, terms_ref, grad_ref, sum_ref, total_ref = refs[:7]
    refs = refs[7:]
    if merge:
        old_ref, refs = refs[0], refs[1:]
    dq_ref, dkv_ref, q_wide, q_only, g_wide, g_only, dq_sum = refs
    rows, chunk = q_ref.shape[0], kv_ref.shape[0]
    step = pl.program_id(1)
    free = 0 if wide else blocks

    @pl.when(step == 0)
    def _():
        size = min(rows, 256)
        low = low_half((size, LANES))
        lane = lax.broadcasted_iota(jnp.int32, (size, LANES), 1) % DH
        zero = jnp.zeros((size, LANES), F32)
        for at in range(0, rows, size):
            part = slice(at, at + size)
            q, grad = q_ref[part, :].astype(F32), grad_ref[part, :].astype(F32)
            total = total_ref[part, :]
            high, middle, last = split_three(jnp.where(low, total[:, DH : DH + 1], total[:, 0:1]))
            barred = barred_ref[part, :].astype(F32)
            extra = zero if wide else barred
            extra = jnp.where(lane == free, -high, extra)
            extra = jnp.where(lane == free + 1, -middle, extra)
            extra = jnp.where(lane == free + 2, -last, extra)
            inner = grad * sum_ref[part, :]
            inner_0 = jnp.sum(jnp.where(low, inner, zero), -1, keepdims=True)
            inner_1 = jnp.sum(jnp.where(low, zero, inner), -1, keepdims=True)
            high, middle, last = split_three(jnp.where(low, inner_1, inner_0))
            less = jnp.where(lane == 0, -high, jnp.where(lane == 1, -middle, jnp.where(lane == 2, -last, zero)))
            for head in range(2):
                q_wide[head, part, :] = widen(pick(low, head, q, extra), barred if wide else None).astype(BF16)
                q_only[head, part, :] = pick(low, head, q, zero).astype(BF16)
                g_wide[head, part, :] = pick(low, head, grad, less).astype(BF16)
                g_only[head, part, :] = pick(low, head, grad, zero).astype(BF16)
        dq_sum[...] = jnp.zeros_like(dq_sum)

    low = low_half((chunk, LANES))
    k, v = kv_ref[:, :LANES], kv_ref[:, LANES:]
    terms, own_terms = terms_ref[:, :LANES], terms_ref[:, LANES:] if wide else None
    dk = dv = None
    for head in range(2):
        prob = jnp.exp(nt(widen(pick(low, head, k, terms), own_terms), q_wide[head]))
        prob_grad = nt(pick(low, head, v, jnp.ones_like(v)), g_wide[head])
        score_grad = (prob * prob_grad).astype(BF16)
        dv_head, dk_head = nn(prob.astype(BF16), g_only[head]), nn(score_grad, q_only[head])
        dv = dv_head if dv is None else dv + dv_head
        dk = dk_head if dk is None else dk + dk_head
        dq_sum[...] += tn(pick(low, head, k, jnp.zeros_like(k)), score_grad)
    dkv_ref[:, :LANES] = dk.astype(dkv_ref.dtype)
    dkv_ref[:, LANES:] = dv.astype(dkv_ref.dtype)

    @pl.when(step == pl.num_programs(1) - 1)
    def _():
        dq = dq_sum[...].T * DH**-0.5
        if merge:
            dq = dq + old_ref[...]
        dq_ref[...] = dq.astype(dq_ref.dtype)


def cross_backward(q, barred, kv, terms, start, keys, grad, cross_sum, total, old, final):
    rows, width = q.shape
    blocks = kv.shape[0] // BLOCK
    wide = blocks + 3 > DH
    chunk = min(keys, 512 if wide else 2048)
    by_pair = pl.BlockSpec((rows, LANES), lambda pair, i: (0, pair))
    return pl.pallas_call(
        functools.partial(cross_backward_kernel, blocks, wide, bool(old)),
        grid=(width // LANES, keys // chunk),
        in_specs=[
            by_pair,
            pl.BlockSpec((rows, LANES), lambda pair, i: (0, 0)),
            pl.BlockSpec((chunk, 2 * LANES), lambda pair, i: (i + start // chunk, pair)),
            pl.BlockSpec((chunk, terms.shape[1]), lambda pair, i: (i + start // chunk, 0)),
        ]
        + [by_pair] * (3 + len(old)),
        out_specs=[by_pair, pl.BlockSpec((chunk, 2 * LANES), lambda pair, i: (i, pair))],
        out_shape=[
            jax.ShapeDtypeStruct((rows, width), BF16 if final else F32),
            jax.ShapeDtypeStruct((keys, 2 * width), BF16),
        ],
        scratch_shapes=[pltpu.VMEM((2, rows, 2 * LANES if wide else LANES), BF16)]
        + [pltpu.VMEM((2, rows, LANES), BF16)] * 3
        + [pltpu.VMEM((LANES, rows), F32)],
        compiler_params=pltpu.CompilerParams(vmem_limit_bytes=VMEM_LIMIT),
        cost_estimate=pl.CostEstimate(flops=2 * rows * keys * width, bytes_accessed=8 * keys * width, transcendentals=0),
        name="cross_backward",
    )(q, barred, kv, terms, grad, cross_sum, total, *old)


def self_forward_kernel(tile, q_ref, k_ref, v_ref, mix_ref, total_ref):
    rows = q_ref.shape[0]
    low_all = low_half((rows, LANES))
    low = low_half((tile, LANES))
    k, v = k_ref[...], v_ref[...]
    zero = jnp.zeros_like(k)
    keys = [pick(low_all, head, k, zero) for head in range(2)]
    values = [pick(low_all, head, v, jnp.ones_like(v)) for head in range(2)]
    ahead = lax.broadcasted_iota(jnp.int32, (tile, tile), 1) > lax.broadcasted_iota(jnp.int32, (tile, tile), 0)
    for at in range(0, rows, tile):
        q = q_ref[at : at + tile, :] * jnp.asarray(DH**-0.5, BF16)
        sums, totals = [], []
        for head in range(2):
            edge = jnp.where(ahead, NEGATIVE, nt(q, keys[head][at : at + tile]))
            top = jnp.max(edge, -1, keepdims=True)
            if at:
                before = nt(q, keys[head][:at])
                top = jnp.maximum(top, jnp.max(before, -1, keepdims=True))
            mixed = nn(jnp.exp(edge - top).astype(BF16), values[head][at : at + tile])
            if at:
                mixed = mixed + nn(jnp.exp(before - top).astype(BF16), values[head][:at])
            weight = mixed[:, DH : DH + 1] if head == 0 else mixed[:, 0:1]
            sums.append(mixed / weight)
            totals.append(top + jnp.log(weight))
        mix_ref[at : at + tile, :] = jnp.where(low, sums[0], sums[1]).astype(BF16)
        columns = jnp.where(low, totals[0], totals[1]).T
        total_ref[0, 0:1, at : at + tile] = columns[0:1]
        total_ref[0, 1:2, at : at + tile] = columns[DH : DH + 1]


def self_forward(q, k, v):
    rows, width = q.shape
    return pl.pallas_call(
        functools.partial(self_forward_kernel, min(rows, 512)),
        grid=(width // LANES,),
        in_specs=[pl.BlockSpec((rows, LANES), lambda pair: (0, pair))] * 3,
        out_specs=[
            pl.BlockSpec((rows, LANES), lambda pair: (0, pair)),
            pl.BlockSpec((1, 2, rows), lambda pair: (pair, 0, 0)),
        ],
        out_shape=[
            jax.ShapeDtypeStruct((rows, width), BF16),
            jax.ShapeDtypeStruct((width // LANES, 2, rows), F32),
        ],
        compiler_params=pltpu.CompilerParams(vmem_limit_bytes=VMEM_LIMIT),
        cost_estimate=pl.CostEstimate(flops=2 * rows * rows * width, bytes_accessed=8 * rows * width, transcendentals=0),
        name="self_forward",
    )(q, k, v)


def self_backward_kernel(
    tile, rows_ref, w_ref, self_grad_ref, w_out_ref, mix_ref, total_ref, norms_ref, part_ref, last_ref, out_ref, qkv_ref, grad_ref
):
    rows = rows_ref.shape[0]
    tiles = rows // tile
    pair = pl.program_id(0)
    for at in range(0, rows, tile):
        part = slice(at, at + tile)
        qkv_ref[part, :] = nn(rows_ref[part, :], w_ref[...]).astype(BF16)
        grad_ref[part, :] = nt(self_grad_ref[part, :], w_out_ref[...]).astype(BF16)
    low_all = low_half((rows, LANES))
    low = low_half((tile, LANES))
    q, grad = qkv_ref[:, :LANES] * jnp.asarray(DH**-0.5, BF16), grad_ref[...]
    zero = jnp.zeros_like(q)
    q_only = [pick(low_all, head, q, zero) for head in range(2)]
    g_only = [pick(low_all, head, grad, zero) for head in range(2)]
    inner = grad.astype(F32) * mix_ref[...].astype(F32)
    mine = lax.broadcasted_iota(jnp.int32, (8, LANES), 1) < DH
    ones = lax.broadcasted_iota(jnp.int32, (8, LANES), 0) == jnp.where(mine, 0, 1)
    inners = lax.dot_general(
        ones.astype(F32), inner, (((1,), (1,)), ((), ())), precision=lax.Precision.HIGHEST, preferred_element_type=F32
    )
    behind = lax.broadcasted_iota(jnp.int32, (tile, tile), 0) > lax.broadcasted_iota(jnp.int32, (tile, tile), 1)
    dq = [None] * tiles
    for i in range(tiles):
        part = slice(i * tile, (i + 1) * tile)
        k, v = qkv_ref[part, LANES : 2 * LANES], qkv_ref[part, 2 * LANES :]
        dk = dv = None
        for head in range(2):
            k_only = pick(low, head, k, jnp.zeros_like(k))
            v_only = pick(low, head, v, jnp.zeros_like(v))
            for j in range(i, tiles):
                at = slice(j * tile, (j + 1) * tile)
                scores = nt(k_only, q[at]) - total_ref[0, head : head + 1, at]
                if i == j:
                    scores = jnp.where(behind, NEGATIVE, scores)
                prob = jnp.exp(scores)
                prob_grad = nt(v_only, grad[at])
                score_grad = (prob * (prob_grad - inners[head : head + 1, at])).astype(BF16)
                dv_part = nn(prob.astype(BF16), g_only[head][at])
                dk_part = nn(score_grad, q_only[head][at])
                dq_part = tn(score_grad, k_only)
                dv = dv_part if dv is None else dv + dv_part
                dk = dk_part if dk is None else dk + dk_part
                dq[j] = dq_part if dq[j] is None else dq[j] + dq_part
        out_ref[part, LANES : 2 * LANES] = dk.astype(BF16)
        out_ref[part, 2 * LANES :] = dv.astype(BF16)
    for i in range(tiles):
        out_ref[i * tile : (i + 1) * tile, :LANES] = (dq[i] * DH**-0.5).astype(BF16)
    size = 3 * LANES
    for i in range(tiles):
        part = slice(i * tile, (i + 1) * tile)
        rows_part = nt(out_ref[part, :], w_ref[...])

        @pl.when(pair == 0)
        def _():
            part_ref[part, :] = rows_part

        @pl.when(pair > 0)
        def _():
            part_ref[part, :] += rows_part

    last_ref[:, pl.ds(pl.multiple_of(pair * size, size), size)] = tn(rows_ref[...], out_ref[...]).astype(BF16)
    last_ref[:, last_ref.shape[1] - LANES :] = norms_ref[...]


def self_backward(rows_in, w_triple, self_grad, w_out, mix, total, norms):
    rows, width = rows_in.shape
    size = 3 * LANES
    by_pair = pl.BlockSpec((rows, LANES), lambda pair: (0, pair))
    whole = lambda array: pl.BlockSpec(array.shape, lambda pair: (0, 0))
    last = jax.ShapeDtypeStruct((width, w_triple.shape[1] + LANES), BF16)
    return pl.pallas_call(
        functools.partial(self_backward_kernel, min(rows, 512)),
        grid=(w_triple.shape[1] // size,),
        in_specs=[
            whole(rows_in),
            pl.BlockSpec((width, size), lambda pair: (0, pair)),
            whole(self_grad),
            pl.BlockSpec((LANES, width), lambda pair: (pair, 0)),
            by_pair,
            pl.BlockSpec((1, 2, rows), lambda pair: (pair, 0, 0)),
            whole(norms),
        ],
        out_specs=[whole(rows_in), whole(last)],
        out_shape=[jax.ShapeDtypeStruct((rows, width), F32), last],
        scratch_shapes=[pltpu.VMEM((rows, size), BF16)] * 2 + [pltpu.VMEM((rows, LANES), BF16)],
        compiler_params=pltpu.CompilerParams(vmem_limit_bytes=VMEM_LIMIT),
        cost_estimate=pl.CostEstimate(flops=rows * rows * LANES, bytes_accessed=rows * width, transcendentals=0),
        name="self_backward",
    )(rows_in, w_triple, self_grad, w_out, mix, total, norms)


def join_kernel(*refs):
    at = 0
    for ref in refs[:-1]:
        refs[-1][:, at : at + ref.shape[1]] = ref[...]
        at += ref.shape[1]


def join(*arrays):
    rows, width = arrays[0].shape[0], sum(array.shape[1] for array in arrays)
    return pl.pallas_call(
        join_kernel,
        out_shape=jax.ShapeDtypeStruct((rows, width), arrays[0].dtype),
        compiler_params=pltpu.CompilerParams(vmem_limit_bytes=VMEM_LIMIT),
        cost_estimate=pl.CostEstimate(flops=rows * width, bytes_accessed=2 * rows * width, transcendentals=0),
        name="join",
    )(*arrays)


def normalize(values):
    center = values - jnp.mean(values, -1, keepdims=True)
    scale = lax.rsqrt(jnp.mean(center * center, -1, keepdims=True) + EPSILON)
    return center * scale, scale


def norm_backward(unit, scale, gain, upstream):
    weighted = upstream * gain
    grad = weighted - jnp.mean(weighted, -1, keepdims=True) - unit * jnp.mean(weighted * unit, -1, keepdims=True)
    return grad * scale, jnp.sum(upstream * unit, 0), jnp.sum(upstream, 0)


def chunk_of(rows, index, size):
    return lax.dynamic_slice_in_dim(rows, index * size, size, 0)


def assemble(chunks):
    size, width = chunks[0][1].shape
    result = jnp.zeros((size * len(chunks), width), chunks[0][1].dtype)
    for index, rows in chunks:
        result = lax.dynamic_update_slice_in_dim(result, rows, index * size, 0)
    return result


class Places:
    def __init__(self):
        self.mp, self.dp = lax.axis_size("mp"), lax.axis_size("dp")
        self.chips = self.dp // 2
        self.x, self.d = lax.axis_index("mp"), lax.axis_index("dp")
        self.core, self.chip = self.d % 2, self.d // 2
        self.line = self.x * 2 + self.core
        self.shard, self.seq = self.line % self.mp, self.line // self.mp

    def send(self, values, target):
        pairs = []
        for chip in range(self.chips):
            for x in range(self.mp):
                for core in range(2):
                    to_chip, to_x, to_core = target(chip, x, core)
                    pair = ((chip * 2 + core) * self.mp + x, (to_chip * 2 + to_core) * self.mp + to_x)
                    if pair[0] != pair[1]:
                        pairs.append(pair)
        return lax.ppermute(values, ("dp", "mp"), pairs)

    def weight(self, values):
        def target(chip, x, core):
            line = x if core else self.mp + x
            return chip, line // 2, line % 2

        return self.send(values, target)

    def to_work(self, values):
        arrived = self.send(values, lambda chip, x, core: (chip, (core * self.mp + x) // 2, (core * self.mp + x) % 2))
        return jnp.where((self.shard == self.x) & (self.seq == self.core), values, arrived)

    def from_work(self, values):
        mp = self.mp
        arrived = self.send(values, lambda chip, x, core: (chip, (x * 2 + core) % mp, (x * 2 + core) // mp))
        return jnp.where((self.shard == self.x) & (self.seq == self.core), values, arrived)

    def to_partner(self, values):
        def target(chip, x, core):
            return chip, x, 1 - core if (x * 2 + 1 - core) // self.mp == core else core

        return self.send(values, target)

    def sequence(self, values):
        return jnp.where(self.core == self.seq, values, self.to_partner(values))

    def sequence_chunk(self, values):
        size = values.shape[0] // self.mp
        partner = (self.x * 2 + 1 - self.core) % self.mp
        arrived = self.to_partner(chunk_of(values, partner, size))
        return jnp.where(self.core == self.seq, chunk_of(values, self.shard, size), arrived)

    def sum_group(self, grads):
        groups = [
            [
                (chip * 2 + line % 2) * self.mp + line // 2
                for chip in range(self.chips)
                for line in (shard, self.mp + shard)
            ]
            for shard in range(self.mp)
        ]
        return lax.psum_scatter(grads, ("dp", "mp"), scatter_dimension=0, axis_index_groups=groups, tiled=True)

    def along(self, values, shift):
        def target(chip, x, core):
            line = x * 2 + core
            line = line // self.mp * self.mp + (line + shift) % self.mp
            return chip, line // 2, line % 2

        return self.send(values, target)

    def scatter_parts(self, product, lefts, kind=BF16):
        size = lefts[0].shape[0] // self.mp

        def part(by):
            return product(*(chunk_of(left, (self.shard + by) % self.mp, size) for left in lefts))

        return [self.along(part(by).astype(kind), by) for by in range(1, self.mp)], part(0)

    def scatter_sum(self, product, lefts, kind=BF16):
        arrived, own = self.scatter_parts(product, lefts, kind)
        return sum((rows.astype(F32) for rows in arrived), own)

    def gather(self, rows):
        chunks = [(self.shard, rows)]
        chunks += [((self.shard + by) % self.mp, self.along(rows, -by)) for by in range(1, self.mp)]
        return assemble(chunks)

    def spread(self, rows):
        mp = self.mp
        arrived = []
        for turn in range(mp):

            def target(chip, x, core, turn=turn):
                line = x * 2 + core
                return chip, (line % mp - turn) % mp, line // mp

            arrived.append(self.send(rows, target))
        return arrived

    def spread_out(self, rows, arrived, kind):
        chunks = []
        for turn, chunk in enumerate(arrived):
            mine = (self.seq == self.core) & ((self.shard - turn) % self.mp == self.x)
            chunks.append(((self.x + turn) % self.mp, jnp.where(mine, rows, chunk).astype(kind)))
        return assemble(chunks)

    def bits(self):
        return self.chips.bit_length() - 1

    def meet(self, values, bits):
        mp = self.mp

        def target(chip, x, core):
            for bit in bits:
                if bit == "sequence":
                    line = (x * 2 + core + mp) % (2 * mp)
                    x, core = line // 2, line % 2
                elif bit == "core":
                    core = 1 - core
                elif isinstance(bit, tuple):
                    x = x ^ (1 << bit[1])
                else:
                    chip = chip ^ (1 << bit)
            return chip, x, core

        return self.send(values, target)

    def my_bit(self, bit):
        if bit == "sequence":
            return self.seq
        if bit == "core":
            return self.core
        return (self.chip >> bit) & 1


class Scatter:
    def __init__(self, at, values, stages, last):
        bits = at.bits()
        self.at, self.order, self.axes = at, [stage for stage in stages if stage], list(range(bits))[::-1] + [last]
        self.values = values.reshape((2,) * (bits + 1) + (values.shape[0] // 2 ** (bits + 1), values.shape[1]))
        self.arrived = None

    def pieces(self):
        stage = self.order.pop(0)
        if isinstance(stage[0], tuple):
            self.sets = [tuple(stage)]
            return self.values, [self.values]
        sets = [()]
        for bit in stage:
            sets += [some + (bit,) for some in sets]
        axes = self.axes
        self.axes = [axis for axis in axes if axis not in stage]
        self.sets = sets[1:]
        size = [1 if axis in stage else 2 for axis in axes] + list(self.values.shape[-2:])
        shape = [2] * len(self.axes) + list(self.values.shape[-2:])
        parts = []
        for some in sets:
            start = [0] * len(size)
            for bit in stage:
                mine = self.at.my_bit(bit)
                start[axes.index(bit)] = 1 - mine if bit in some else mine
            parts.append(lax.dynamic_slice(self.values, start, size).reshape(shape))
        return parts[0], parts[1:]

    def prepare(self):
        self.kept, sent = self.pieces()
        self.sent = [part.astype(BF16) for part in sent]

    def start(self):
        self.arrived = [self.at.meet(part, some) for part, some in zip(self.sent, self.sets)]

    def finish(self):
        self.values = sum((part.astype(F32) for part in self.arrived), self.kept.astype(F32))
        self.arrived = None


def launch(chains, *values):
    moving = []
    for chain in chains:
        if chain.arrived is not None:
            chain.finish()
        if chain.order:
            chain.prepare()
            moving.append(chain)
    values, sents = lax.optimization_barrier((values, [chain.sent for chain in moving]))
    for chain, sent in zip(moving, sents):
        chain.sent = sent
        chain.start()
    return values[0] if len(values) == 1 else values


def settle(chains, *values):
    moving = [chain for chain in chains if chain.arrived is not None]
    values, arrivals = lax.optimization_barrier((values, [chain.arrived for chain in moving]))
    for chain, arrived in zip(moving, arrivals):
        chain.arrived = arrived
    return values[0] if len(values) == 1 else values


def per_device(
    decoder_layer_input,
    encoder_states,
    retrieved_owner,
    retrieved_block,
    self_query,
    self_attention_key,
    self_value,
    self_out,
    gain_first,
    shift_first,
    cross_query,
    cross_key,
    cross_value,
    cross_out,
    gain_second,
    shift_second,
    hidden_up,
    hidden_down,
    gain_third,
    shift_third,
    out_grad,
):
    at = Places()
    score_scale = jnp.asarray(DH**-0.5, BF16)
    seq_len, width = decoder_layer_input.shape
    shard_width = self_query.shape[1]
    chunk = seq_len // at.mp
    blocks_here = encoder_states.shape[0] // BLOCK
    chip_bits = list(range(at.bits()))
    x_bits = [("x", i) for i in range(at.mp.bit_length() - 1)]
    tie = lambda *values: lax.optimization_barrier(values)

    def even(weight):
        extra = -weight.shape[1] % LANES
        return jnp.pad(weight, ((0, 0), (0, extra))) if extra else weight

    def even_rows(weight):
        extra = -weight.shape[0] % LANES
        return jnp.pad(weight, ((0, extra), (0, 0))) if extra else weight

    def interleave(*weights):
        weights = [even(weight) for weight in weights]
        return jnp.concatenate(
            [w[:, i : i + LANES] for i in range(0, weights[0].shape[1], LANES) for w in weights], 1
        )

    def separate(values, count):
        size = values.shape[1] // count
        return [
            jnp.concatenate([values[:, (i * count + j) * LANES :][:, :LANES] for i in range(size // LANES)], 1)[
                :, :shard_width
            ]
            for j in range(count)
        ]

    store = lax.all_gather(encoder_states, "dp", axis=0, tiled=True)
    keys = store.shape[0]

    w_out, w_cross_query = at.weight(self_out), at.weight(cross_query)
    mix_first, total_first = self_forward(
        *(nn(decoder_layer_input, even(w)).astype(BF16) for w in (self_query, self_attention_key, self_value))
    )
    mix_first, w_out, w_cross_query, own_rows, next_key, next_value, owner, block = tie(
        mix_first,
        w_out,
        w_cross_query,
        decoder_layer_input,
        cross_key,
        cross_value,
        retrieved_owner,
        retrieved_block,
    )
    w_out, w_cross_query = even_rows(w_out), even(w_cross_query)
    self_mix = at.to_work(mix_first)
    own_rows = at.sequence_chunk(own_rows).astype(F32)
    names = at.sequence(owner * blocks_here + block)
    w_cross_key, w_cross_value = at.weight(next_key), at.weight(next_value)

    self_mix, own_rows, names, next_out = tie(self_mix, own_rows, names, cross_out)
    w_cross_out = at.weight(next_out)
    first_in = own_rows + at.scatter_sum(lambda rows: nn(rows, w_out), [self_mix], F32)
    first_in, w_cross_key, w_cross_value = tie(first_in, w_cross_key, w_cross_value)
    first_unit, first_scale = normalize(first_in)
    first = first_unit * gain_first + shift_first
    first_low = at.gather(first.astype(BF16))
    first_low, w_cross_out = tie(first_low, w_cross_out)
    w_store = interleave(w_cross_key, w_cross_value)
    queries = nn(first_low, w_cross_query).astype(BF16) * score_scale
    queries, store, w_store, next_up, next_down, rows_grad = tie(
        queries, store, w_store, hidden_up, hidden_down, out_grad
    )
    w_up, w_down = at.weight(next_up), at.weight(next_down)
    rows_grad = at.sequence_chunk(rows_grad)
    store_kv = nn(store, w_store).astype(BF16)
    terms = key_terms(keys, keys // BLOCK + 3 > DH)
    cross_sum, cross_mix, cross_total, barred = cross_forward(queries, names, store_kv, terms)
    cross_mix, w_up, w_down, rows_grad = tie(cross_mix, w_up, w_down, rows_grad)
    w_cross_out, rows_grad = even_rows(w_cross_out), rows_grad.astype(F32)
    second_in = first + at.scatter_sum(lambda rows: nn(rows, w_cross_out), [cross_mix], F32)
    second_unit, second_scale = normalize(second_in)
    second = second_unit * gain_second + shift_second
    second_low = at.gather(second.astype(BF16))
    hidden_pre = nn(second_low, w_up)
    bell = 0.5 + 0.5 * lax.erf(hidden_pre * 0.5**0.5)
    hidden_act = (hidden_pre * bell).astype(BF16)
    slope = bell + hidden_pre * jnp.exp(-0.5 * hidden_pre * hidden_pre) * 0.3989422804014327
    third_in = second + at.scatter_sum(lambda rows: nn(rows, w_down), [hidden_act])
    third_unit, third_scale = normalize(third_in)
    layer_out = (third_unit * gain_third + shift_third).astype(BF16)

    res3_grad, gain_third_grad, shift_third_grad = norm_backward(third_unit, third_scale, gain_third, rows_grad)
    ffn_grad = at.gather(res3_grad.astype(BF16))
    pre_grad = (slope * nt(ffn_grad, w_down)).astype(BF16)
    second_grad = res3_grad + at.scatter_sum(lambda rows: nt(rows, w_up), [pre_grad])
    res2_grad, gain_second_grad, shift_second_grad = norm_backward(
        second_unit, second_scale, gain_second, second_grad
    )
    cross_grad = at.gather(res2_grad.astype(BF16))
    mix_grad = nt(cross_grad, w_cross_out).astype(BF16)
    early = jnp.concatenate(
        [
            tn(ffn_grad, hidden_act).astype(BF16),
            tn(second_low, pre_grad).astype(BF16),
            tn(cross_grad, cross_mix).astype(BF16),
        ],
        1,
    )
    w_triple = interleave(self_query, self_attention_key, self_value)
    mix_grad, early, layer_out, w_triple, self_total, rows_in = tie(
        mix_grad, early, layer_out, w_triple, total_first, decoder_layer_input
    )
    rows_in = at.sequence(rows_in)
    early = at.sum_group(early)
    layer_arrived = at.spread(layer_out)
    w_triple = at.weight(w_triple)
    self_total = at.to_work(self_total)
    queries_grad, kv_grad = cross_backward(
        queries, barred, store_kv, terms, 0, keys, mix_grad, cross_sum, cross_total, (), True
    )
    queries_grad, kv_grad, layer_arrived, w_triple, self_total, rows_in = tie(
        queries_grad, kv_grad, layer_arrived, w_triple, self_total, rows_in
    )
    encoder = Scatter(at, kv_grad, [["core"], chip_bits[:2], chip_bits[2:]], "core")
    kept, sent = encoder.pieces()
    shape = kept.shape[:-1] + (width,)
    encoder.sent = [nt(part.reshape(-1, part.shape[-1]), w_store).astype(BF16).reshape(shape) for part in sent]
    encoder.start()
    encoder.kept = nt(kept.reshape(-1, kept.shape[-1]), w_store).reshape(shape)
    first_grad = res2_grad + at.scatter_sum(lambda rows: nt(rows, w_cross_query), [queries_grad])
    res1_grad, gain_first_grad, shift_first_grad = norm_backward(first_unit, first_scale, gain_first, first_grad)
    res1_grad = launch([encoder], res1_grad)
    self_grad = at.gather(res1_grad.astype(BF16))
    side = Scatter(
        at,
        join(
            tn(store, kv_grad).astype(BF16),
            tn(first_low, queries_grad).astype(BF16),
            tn(self_grad, self_mix).astype(BF16),
        ),
        [["sequence"], chip_bits[1:2], chip_bits[:1], chip_bits[2:]],
        "sequence",
    )
    self_grad = launch([side], self_grad)
    norms = jnp.stack(
        [
            gain_first_grad,
            shift_first_grad,
            gain_second_grad,
            shift_second_grad,
            gain_third_grad,
            shift_third_grad,
        ],
        0,
    )
    norms = sum((at.along(norms, by) for by in range(1, at.mp)), norms)
    norms = tn(norms.astype(BF16), jnp.eye(6, LANES, dtype=BF16)).astype(BF16)
    part, last = self_backward(rows_in, w_triple, self_grad, w_out, self_mix, self_total, norms)
    part, last, early, layer_out, layer_arrived = settle(
        [side, encoder], part, last, early, layer_out, layer_arrived
    )
    input_rows = (res1_grad + at.scatter_sum(lambda rows: rows, [part])).astype(BF16)
    last = Scatter(at, last, [chip_bits[:1], ["sequence"], chip_bits[1:]], "sequence")
    launch([last, side, encoder])
    input_arrived = at.spread(input_rows)
    early = at.from_work(early.astype(BF16))
    layer_out = at.spread_out(layer_out, layer_arrived, BF16)
    input_arrived, early = settle([last, side, encoder], input_arrived, early)
    early = early.astype(F32)
    input_arrived = launch([last, side], input_arrived)
    input_grad = at.spread_out(input_rows, input_arrived, F32)
    encoder.order += [[bit] for bit in x_bits]
    chains = [last, side, encoder]
    while any(chain.order or chain.arrived is not None for chain in chains):
        settle(chains)
        launch(chains)

    encoder_grad = encoder.values
    last_width = last.values.shape[1]
    gathered = at.from_work(jnp.concatenate([chain.values.astype(BF16) for chain in (last, side)], 1)).astype(F32)
    last, side = gathered[:, :last_width], gathered[:, last_width:]
    part_width = w_triple.shape[1] // 3
    norms = last[:, 3 * part_width :][:, :6].T
    self_query_grad, self_key_grad, self_value_grad = separate(last[:, : 3 * part_width], 3)
    cross_key_grad, cross_value_grad = separate(side[:, : 2 * part_width], 2)
    cross_query_grad = side[:, 2 * part_width : 2 * part_width + shard_width]
    self_out_grad = side[:, 3 * part_width : 3 * part_width + shard_width]
    hidden = hidden_act.shape[1]
    hidden_down_grad, hidden_up_grad = early[:, :hidden], early[:, hidden : 2 * hidden]
    cross_out_grad = early[:, 2 * hidden : 2 * hidden + shard_width]
    share = width // at.dp
    return (
        layer_out,
        input_grad,
        encoder_grad,
        self_query_grad,
        self_key_grad,
        self_value_grad,
        self_out_grad.T,
        norms[0],
        norms[1],
        cross_query_grad,
        cross_key_grad,
        cross_value_grad,
        cross_out_grad.T,
        norms[2],
        norms[3],
        hidden_up_grad,
        hidden_down_grad.T,
        norms[4],
        norms[5],
    )


def solution(mesh):
    rows, columns, parts, copied = P("dp", None), P(None, "mp"), P("mp", None), P()
    return jax.shard_map(
        per_device,
        mesh=mesh,
        in_specs=(rows,) * 4
        + (columns,) * 3
        + (parts, copied, copied)
        + (columns,) * 3
        + (parts, copied, copied)
        + (columns, parts, copied, copied, rows),
        out_specs=(rows,) * 3
        + (P("dp", "mp"),) * 3
        + (P("mp", "dp"), P("dp"), P("dp"))
        + (P("dp", "mp"),) * 3
        + (P("mp", "dp"), P("dp"), P("dp"))
        + (P("dp", "mp"), P("mp", "dp"), P("dp"), P("dp")),
        check_vma=False,
    )
```
